32 devices in a mesh: row: 8 (over y, x, core), col: 4 (over z).
Axes of the slice: x: 2, y: 2, z: 4, core: 2. Of those that a mesh axis runs over, the one named last changes fastest.
Arguments:
- inputs: bfloat16 [256, 12288], P('col', 'row'), may hold values from -6 to 6
- w_up: bfloat16 [12288, 24576], P('row', 'col'), may hold values from -0.0546875 to 0.0546875
- w_down: bfloat16 [24576, 12288], P('col', 'row'), may hold values from -0.0390625 to 0.0390625
- mask_up: int32 [96, 192], P('row', 'col'), may hold values from 0 to 1, as said below
- mask_down: int32 [192, 96], P('col', 'row'), may hold values from 0 to 1, as said below
- cotangent: bfloat16 [256, 12288], P('col', 'row'), may hold values from -1.5 to 1.5
Outputs:
- outputs: bfloat16 [256, 12288], P('col', 'row')
- grad_inputs: bfloat16 [256, 12288], P('col', 'row')
- grad_up: bfloat16 [12288, 24576], P('row', 'col')
- grad_down: bfloat16 [24576, 12288], P('col', 'row')
The draws below stay inside these ranges and needn't reach their ends.
Inputs may be any that keep to these rules, and one draw needn't show every extreme that they name: `mask_up`: each entry is 0 or 1; the chance of a 1 is the same along a row of tiles and differs from row to row, between 0.2 and 0.8. `mask_down`: each entry is 0 or 1; the chance of a 1 is the same along a row of tiles and differs from row to row, between 0.2 and 0.8.
All inputs are finite; a program needn't handle non-finite values.
Results may differ from the reference program's by a relative error of at most 0.029.
Values may be sent and summed in bfloat16 or wider, within the bound.
No kernel may reach another device: no remote copies, remote signals or barrier semaphores. Data moves between devices by JAX's collectives and lax.ppermute only.
A program may use at most 256 MiB of HBM per device.

```python
import jax
import jax.numpy as jnp

D = 12288
FF = 24576
TILE = 128
TOKENS = 256
N_ROW = 8
N_COL = 4


def tile_pattern(key, rows, cols):
    key_level, key_tick = jax.random.split(key)
    levels = jax.random.randint(key_level, (rows, 1), 20, 81)
    ticks = jax.random.randint(key_tick, (rows, cols), 0, 100)
    return (ticks < levels).astype(jnp.int32)


def draw_mask_up(key, part):
    key = jax.random.fold_in(key, 11)
    return tile_pattern(key, D // TILE, FF // TILE)


def draw_mask_down(key, part):
    key = jax.random.fold_in(key, 23)
    return tile_pattern(key, FF // TILE, D // TILE)


def steps_of(own_key, shape, shards, least, largest):
    def one(axis_at, shards_of):
        heights = jax.random.uniform(jax.random.fold_in(jax.random.fold_in(own_key, 6), axis_at), (shards_of,), jnp.float32, least / len(shards), largest / len(shards))
        return jnp.repeat(jnp.exp(heights), shape[axis_at] // shards_of).reshape((-1,) + (1,) * (len(shape) - axis_at - 1))

    gain = one(*shards[0])
    for cut in shards[1:]:
        gain = gain * one(*cut)
    return gain


def normal_values(key, dims, deviation, limit, shards=(), held_as=jnp.bfloat16):
    level = steps_of(key, dims, shards, -0.22, 0.18) if shards else 1.0
    drawn = jax.random.normal(key, dims, jnp.float32) * deviation * level
    return jnp.minimum(jnp.maximum(drawn, -limit), limit).astype(held_as)


def setup_inputs(seed: int = 0) -> dict:
    key_of = jax.random.split(jax.random.key(seed), 7)
    inputs = normal_values(key_of[0], (TOKENS, D), 1.0, 6.0, ((0, 4), (1, 8)))
    w_up = normal_values(key_of[1], (D, FF), D ** -0.5, 0.0546875, ((0, 8), (1, 4)))
    w_down = normal_values(key_of[2], (FF, D), FF ** -0.5, 0.0390625, ((0, 4), (1, 8)))
    mask_up = draw_mask_up(jax.random.fold_in(key_of[6], 71), 0)
    mask_down = draw_mask_down(jax.random.fold_in(key_of[6], 71), 0)
    cotangent = normal_values(key_of[5], (TOKENS, D), 0.25, 1.5, ((0, 4), (1, 8)))
    return dict(inputs=inputs, w_up=w_up, w_down=w_down, mask_up=mask_up, mask_down=mask_down, cotangent=cotangent)


def apply_mask(weight, mask):
    rows, cols = mask.shape
    tile = weight.shape[0] // rows
    shaped = weight.reshape(rows, tile, cols, tile)
    keep = mask[:, None, :, None].astype(weight.dtype)
    return (shaped * keep).reshape(weight.shape)

def smooth_gate(value):
    return jax.nn.gelu(value, approximate=True)

def reference(inputs, w_up, w_down, mask_up, mask_down, cotangent):
    up_kept = apply_mask(w_up, mask_up)
    down_kept = apply_mask(w_down, mask_down)
    feat = D // N_ROW
    hunits = FF // N_COL
    hidden = jnp.zeros((TOKENS, FF), jnp.float32)
    grad_act = jnp.zeros((TOKENS, FF), jnp.float32)
    for block in range(N_ROW):
        lo = block * feat
        part = jnp.dot(inputs[:, lo:lo + feat], up_kept[lo:lo + feat, :], preferred_element_type=jnp.float32)
        hidden = hidden + part.astype(jnp.bfloat16).astype(jnp.float32)
        back = jnp.dot(cotangent[:, lo:lo + feat], down_kept[:, lo:lo + feat].T, preferred_element_type=jnp.float32)
        grad_act = grad_act + back.astype(jnp.bfloat16).astype(jnp.float32)
    act = smooth_gate(hidden).astype(jnp.bfloat16)
    _, pull = jax.vjp(smooth_gate, hidden)
    grad_hidden = pull(grad_act)[0].astype(jnp.bfloat16)
    outputs = jnp.zeros((TOKENS, D), jnp.float32)
    grad_inputs = jnp.zeros((TOKENS, D), jnp.float32)
    grad_up_cols = []
    grad_down_rows = []
    for block in range(N_COL):
        lo = block * hunits
        act_block = act[:, lo:lo + hunits]
        grad_block = grad_hidden[:, lo:lo + hunits]
        part = jnp.dot(act_block, down_kept[lo:lo + hunits, :], preferred_element_type=jnp.float32)
        outputs = outputs + part.astype(jnp.bfloat16).astype(jnp.float32)
        back = jnp.dot(grad_block, up_kept[:, lo:lo + hunits].T, preferred_element_type=jnp.float32)
        grad_inputs = grad_inputs + back.astype(jnp.bfloat16).astype(jnp.float32)
        grad_up_cols.append(jnp.dot(inputs.T, grad_block, preferred_element_type=jnp.float32).astype(jnp.bfloat16))
        grad_down_rows.append(jnp.dot(act_block.T, cotangent, preferred_element_type=jnp.float32).astype(jnp.bfloat16))
    grad_up = apply_mask(jnp.concatenate(grad_up_cols, axis=1), mask_up)
    grad_down = apply_mask(jnp.concatenate(grad_down_rows, axis=0), mask_down)
    return (outputs.astype(jnp.bfloat16), grad_inputs.astype(jnp.bfloat16), grad_up, grad_down)
```

```python
import functools

import jax
import jax.numpy as jnp
from jax import lax
from jax.experimental import pallas as pl
from jax.experimental.pallas import tpu as pltpu
from jax.sharding import PartitionSpec as P

TILE = 128
MIB = 1 << 20
F32 = jnp.float32
BF16 = jnp.bfloat16


def smooth_gate(value):
    return jax.nn.gelu(value, approximate=True)


def contract(left, right, left_dim, right_dim):
    return lax.dot_general(
        left, right, (((left_dim,), (right_dim,)), ((), ())), preferred_element_type=F32
    )


def apply_mask(weight, mask):
    rows, cols = mask.shape
    tile = weight.shape[0] // rows
    shaped = weight.reshape(rows, tile, cols, tile)
    keep = mask[:, None, :, None].astype(weight.dtype)
    return (shaped * keep).reshape(weight.shape)


def activate(hidden, grad_act):
    act = smooth_gate(hidden).astype(BF16)
    _, pull = jax.vjp(smooth_gate, hidden)
    grad_hidden = pull(grad_act)[0].astype(BF16)
    return (act, grad_hidden)


def per_device_plain(inputs, w_up, w_down, mask_up, mask_down, cotangent):
    up_kept = apply_mask(w_up, mask_up)
    down_kept = apply_mask(w_down, mask_down)
    inputs_all, cot_all = (
        lax.all_gather(inputs, "col", axis=0, tiled=True),
        lax.all_gather(cotangent, "col", axis=0, tiled=True),
    )
    up_part = jnp.dot(inputs_all, up_kept, preferred_element_type=F32)
    back_part = contract(cot_all, down_kept, 1, 1)
    hidden, grad_act = (
        lax.psum_scatter(
            part.astype(BF16), "row", scatter_dimension=0, tiled=True
        ).astype(F32)
        for part in (up_part, back_part)
    )
    act, grad_hidden = activate(hidden, grad_act)
    act_all, grad_all = (
        lax.all_gather(act, "row", axis=0, tiled=True),
        lax.all_gather(grad_hidden, "row", axis=0, tiled=True),
    )
    out_part = jnp.dot(act_all, down_kept, preferred_element_type=F32)
    input_part = contract(grad_all, up_kept, 1, 1)
    outputs, grad_inputs = (
        lax.psum_scatter(
            part.astype(BF16), "col", scatter_dimension=0, tiled=True
        ).astype(F32)
        for part in (out_part, input_part)
    )
    grad_down = apply_mask(contract(act_all, cot_all, 0, 0).astype(BF16), mask_down)
    grad_up = apply_mask(contract(inputs_all, grad_all, 0, 0).astype(BF16), mask_up)
    return (outputs.astype(BF16), grad_inputs.astype(BF16), grad_up, grad_down)


OWN, CORE, X, Y = 0, 1, 2, 4
DIAG = X | Y
SEND = (CORE | DIAG, CORE | X, CORE | Y, CORE)
KEEP = (DIAG, X, Y, OWN)
EARLY = (OWN, CORE, X, Y, CORE | X, CORE | Y)
LATE = (DIAG, CORE | DIAG)
ALL = EARLY + LATE
TABLE = SEND + KEEP + ALL
AT_SEND, AT_KEEP, AT_ALL = 0, len(SEND), len(SEND) + len(KEEP)
AT_LATE = AT_ALL + len(EARLY)


def keep_tiles(dst, weight, keep):
    for k in range(dst.shape[0] // TILE):
        rows = slice(k * TILE, (k + 1) * TILE)
        dst[rows, :] = weight[rows, :] * keep[k : k + 1, :]


def cost(flops, moved):
    return pl.CostEstimate(flops=int(flops), bytes_accessed=int(moved), transcendentals=0)


def params(mib):
    return pltpu.CompilerParams(
        dimension_semantics=("arbitrary",), vmem_limit_bytes=mib * MIB
    )


def weight_specs(weight, keep, share, at, by_rows):
    if by_rows:
        return (
            pl.BlockSpec((share, weight.shape[1]), lambda i, t: (t[at + i], 0)),
            pl.BlockSpec((None,) + keep.shape[1:], lambda i, t: (t[at + i], 0, 0)),
            (share, weight.shape[1]),
        )
    return (
        pl.BlockSpec((weight.shape[0], share), lambda i, t: (0, t[at + i])),
        pl.BlockSpec((keep.shape[0], share), lambda i, t: (0, t[at + i])),
        (weight.shape[0], share),
    )


def whole(array):
    return pl.BlockSpec(array.shape, lambda i, t: (0,) * len(array.shape))


def project(table, parts, weight, keep, share, by_rows, got=None):
    tokens = sum(part.shape[0] for part in parts)
    half = tokens // 2
    wide = parts[0].shape[1]
    at = AT_SEND if got is None else AT_KEEP
    weight_spec, keep_spec, kept_shape = weight_specs(weight, keep, share, at, by_rows)

    def body(table_ref, *refs):
        refs = list(refs)
        part_refs = [refs.pop(0) for _ in parts]
        weight_ref, keep_ref = refs.pop(0), refs.pop(0)
        got_ref = None if got is None else refs.pop(0)
        left, kept = refs[-2:]
        outs = refs[:-2]
        i = pl.program_id(0)

        @pl.when(i == 0)
        def _():
            row = 0
            for ref in part_refs:
                left[row : row + ref.shape[0], :] = ref[...]
                row += ref.shape[0]

        keep_tiles(kept, weight_ref, keep_ref)
        result = contract(left[...], kept[...], 1, 1 if by_rows else 0)
        if got is None:
            outs[0][...] = result.astype(BF16)
            return
        result = (result + got_ref[...].astype(F32)).astype(BF16)
        x_send, y_send, x_keep, y_keep = outs

        @pl.when(i < 2)
        def _():
            x_send[...] = result[:half]

        @pl.when(i >= 2)
        def _():
            x_keep[...] = result[:half]

        @pl.when(i % 2 == 0)
        def _():
            y_send[...] = result[half:]

        @pl.when(i % 2 == 1)
        def _():
            y_keep[...] = result[half:]

    flops = 2 * tokens * wide * share * 4
    moved = 2 * (wide * share * 4 + tokens * share * (4 if got is None else 8) + tokens * wide)
    in_specs = [whole(part) for part in parts] + [weight_spec, keep_spec]
    if got is None:
        out_shape = jax.ShapeDtypeStruct((4, tokens, share), BF16)
        out_specs = pl.BlockSpec((None, tokens, share), lambda i, t: (i, 0, 0))
    else:
        in_specs.append(pl.BlockSpec((None, tokens, share), lambda i, t: (i, 0, 0)))
        out_shape = (jax.ShapeDtypeStruct((2, half, share), BF16),) * 4
        block = (None, half, share)
        out_specs = (
            pl.BlockSpec(block, lambda i, t: (jnp.minimum(i, 1), 0, 0)),
            pl.BlockSpec(block, lambda i, t: (i // 2, 0, 0)),
            pl.BlockSpec(block, lambda i, t: (jnp.maximum(i - 2, 0), 0, 0)),
            pl.BlockSpec(block, lambda i, t: (i // 2, 0, 0)),
        )
    call = pl.pallas_call(
        body,
        out_shape=out_shape,
        grid_spec=pltpu.PrefetchScalarGridSpec(
            num_scalar_prefetch=1,
            grid=(4,),
            in_specs=in_specs,
            out_specs=out_specs,
            scratch_shapes=[
                pltpu.VMEM((tokens, wide), BF16),
                pltpu.VMEM(kept_shape, BF16),
            ],
        ),
        compiler_params=params(40),
        cost_estimate=cost(flops, moved),
    )
    return call(table, *parts, weight, keep, *(() if got is None else (got,)))


def fetch(i, pieces, refs, held, sems):
    copies, n = [], 0
    for at, piece in enumerate(pieces):
        row, own = 0, []
        for array in piece:
            rows = array.shape[0]
            own.append(
                pltpu.make_async_copy(refs[n], held.at[at, pl.ds(row, rows)], sems.at[n])
            )
            row += rows
            n += 1
        copies.append(own)

    @pl.when(i == 0)
    def _():
        for own in copies:
            for copy in own:
                copy.start()

    for at, own in enumerate(copies):

        @pl.when(i == at)
        def _(own=own):
            for copy in own:
                copy.wait()


def gathered(table, pieces, weight, keep, at, by_rows, base=None, blocks=1):
    tokens = sum(array.shape[0] for array in pieces[0])
    share = pieces[0][0].shape[1]
    steps = len(pieces)
    flat = [array for piece in pieces for array in piece]
    wide = weight.shape[1] if by_rows else weight.shape[0]
    weight_spec, keep_spec, kept_shape = weight_specs(weight, keep, share, at, by_rows)
    rows = tokens // blocks

    def body(table_ref, *refs):
        refs = list(refs)
        piece_refs = [refs.pop(0) for _ in flat]
        weight_ref, keep_ref = refs.pop(0), refs.pop(0)
        base_ref = None if base is None else refs.pop(0)
        held, kept, sems = refs[-3:]
        total = refs[-4] if base is not None else refs[0]
        outs = refs[:blocks]
        i = pl.program_id(0)
        fetch(i, pieces, piece_refs, held, sems)
        keep_tiles(kept, weight_ref, keep_ref)
        term = contract(held[i], kept[...], 1, 0 if by_rows else 1)

        @pl.when(i == 0)
        def _():
            total[...] = term if base is None else term + base_ref[...]

        @pl.when(i > 0)
        def _():
            total[...] += term

        if base is not None:

            @pl.when(i == steps - 1)
            def _():
                for k, out in enumerate(outs):
                    out[...] = total[k * rows : (k + 1) * rows, :].astype(BF16)

    in_specs = [pl.BlockSpec(memory_space=pl.ANY)] * len(flat) + [weight_spec, keep_spec]
    scratch = [
        pltpu.VMEM((steps, tokens, share), BF16),
        pltpu.VMEM(kept_shape, BF16),
        pltpu.SemaphoreType.DMA((len(flat),)),
    ]
    args = [*flat, weight, keep]
    if base is None:
        out_shape = jax.ShapeDtypeStruct((tokens, wide), F32)
        out_specs = whole(out_shape)
    else:
        in_specs.append(whole(base))
        args.append(base)
        out_shape = (jax.ShapeDtypeStruct((rows, wide), BF16),) * blocks
        out_specs = (whole(out_shape[0]),) * blocks
        scratch.insert(0, pltpu.VMEM((tokens, wide), F32))
    call = pl.pallas_call(
        body,
        out_shape=out_shape,
        grid_spec=pltpu.PrefetchScalarGridSpec(
            num_scalar_prefetch=1,
            grid=(steps,),
            in_specs=in_specs,
            out_specs=out_specs,
            scratch_shapes=scratch,
        ),
        compiler_params=params(40),
        cost_estimate=cost(
            2 * tokens * share * wide * steps,
            2 * share * (wide + tokens) * steps + 4 * tokens * wide,
        ),
    )
    return call(table, *args)


def weight_gradient(table, pieces, parts, keep, shape, by_rows):
    tokens = sum(part.shape[0] for part in parts)
    share = pieces[0][0].shape[1]
    wide = parts[0].shape[1]
    steps = len(pieces)
    flat = [array for piece in pieces for array in piece]
    weight_spec, keep_spec, _ = weight_specs(
        jax.ShapeDtypeStruct(shape, BF16), keep, share, AT_ALL, by_rows
    )
    span = 2 * TILE

    def body(table_ref, *refs):
        refs = list(refs)
        piece_refs = [refs.pop(0) for _ in flat]
        part_refs = [refs.pop(0) for _ in parts]
        keep_ref, out, held, other, sems = refs
        i = pl.program_id(0)

        @pl.when(i == 0)
        def _():
            row = 0
            for ref in part_refs:
                if by_rows:
                    other[row : row + ref.shape[0], :] = ref[...]
                else:
                    other[:, row : row + ref.shape[0]] = ref[...].T
                row += ref.shape[0]

        fetch(i, pieces, piece_refs, held, sems)
        left = held[i].T if by_rows else other
        right = other[...] if by_rows else held[i]
        for lo in range(0, share if by_rows else wide, span):
            term = contract(left[lo : lo + span, :], right, 1, 0)
            for k in range(0, span, TILE):
                tile = (lo + k) // TILE
                out[lo + k : lo + k + TILE, :] = (
                    term[k : k + TILE].astype(BF16) * keep_ref[tile : tile + 1, :]
                )

    call = pl.pallas_call(
        body,
        out_shape=jax.ShapeDtypeStruct(shape, BF16),
        grid_spec=pltpu.PrefetchScalarGridSpec(
            num_scalar_prefetch=1,
            grid=(steps,),
            in_specs=[pl.BlockSpec(memory_space=pl.ANY)] * len(flat)
            + [whole(part) for part in parts]
            + [keep_spec],
            out_specs=weight_spec,
            scratch_shapes=[
                pltpu.VMEM((steps, tokens, share), BF16),
                pltpu.VMEM((tokens, wide) if by_rows else (wide, tokens), BF16),
                pltpu.SemaphoreType.DMA((len(flat),)),
            ],
        ),
        compiler_params=params(40),
        cost_estimate=cost(
            2 * tokens * share * wide * steps, 2 * share * (wide + tokens) * steps
        ),
    )
    return call(table, *flat, *parts, keep)


def per_device_tuned(n_row, n_col, inputs, w_up, w_down, mask_up, mask_down, cotangent):
    share = w_up.shape[1] // n_row
    table = jnp.asarray(TABLE, jnp.int32) ^ lax.axis_index("row")
    keep_up = jnp.repeat(mask_up.astype(BF16), TILE, axis=1)
    keep_down = jnp.repeat(mask_down.astype(BF16), TILE, axis=1).reshape(
        n_row, share // TILE, w_down.shape[1]
    )

    def across(value, bits):
        return lax.ppermute(value, "row", [(i, i ^ bits) for i in range(n_row)])

    def along(value, shift):
        return lax.ppermute(value, "col", [(i, (i + shift) % n_col) for i in range(n_col)])

    def col_gather(value):
        return [value] + [along(value, k) for k in range(1, n_col)]

    def row_sum(parts, weight, keep, by_rows):
        got = across(project(table, parts, weight, keep, share, by_rows), CORE)
        x_send, y_send, x_keep, y_keep = project(
            table, parts, weight, keep, share, by_rows, got
        )
        x_got, y_got = across(x_send, X), across(y_send, Y)
        x_pass = (x_keep[0].astype(F32) + x_got[0].astype(F32)).astype(BF16)
        y_pass = (y_keep[0].astype(F32) + y_got[0].astype(F32)).astype(BF16)
        x_last, y_last = across(x_pass, Y), across(y_pass, X)
        return jnp.concatenate(
            [
                x_keep[1].astype(F32) + x_got[1].astype(F32) + x_last.astype(F32),
                y_keep[1].astype(F32) + y_got[1].astype(F32) + y_last.astype(F32),
            ]
        )

    def row_gather(value):
        half = value.shape[0] // 2
        from_core, from_x, from_y = (across(value, bits) for bits in (CORE, X, Y))
        core_x, core_y = across(from_x, CORE), across(from_y, CORE)
        diag = (across(from_x[:half], Y), across(from_y[half:], X))
        core_diag = tuple(across(part, CORE) for part in diag)
        early = [(value,), (from_core,), (from_x,), (from_y,), (core_x,), (core_y,)]
        return early, [diag, core_diag]

    def col_sum(blocks):
        terms = [blocks[0]] + [along(blocks[k], -k) for k in range(1, n_col)]
        return functools.reduce(jnp.add, [term.astype(F32) for term in terms]).astype(BF16)

    inputs_all = col_gather(inputs)
    cot_first, *_ = lax.optimization_barrier((cotangent, *inputs_all[1:]))
    cot_all = [cotangent] + [along(cot_first, k) for k in range(1, n_col)]

    hidden = row_sum(inputs_all, w_up, keep_up, False)
    act_early, act_late = row_gather(smooth_gate(hidden).astype(BF16))
    grad_act = row_sum(cot_all, w_down, keep_down, True)
    _, pull = jax.vjp(smooth_gate, hidden)
    grad_early, grad_late = row_gather(pull(grad_act)[0].astype(BF16))

    out_base = gathered(table, act_early, w_down, keep_down, AT_ALL, True)
    outputs = col_sum(
        gathered(table, act_late, w_down, keep_down, AT_LATE, True, out_base, n_col)
    )
    grad_down = weight_gradient(
        table, act_early + act_late, cot_all, keep_down, w_down.shape, True
    )
    in_base = gathered(table, grad_early, w_up, keep_up, AT_ALL, False)
    grad_inputs = col_sum(
        gathered(table, grad_late, w_up, keep_up, AT_LATE, False, in_base, n_col)
    )
    grad_up = weight_gradient(
        table, grad_early + grad_late, inputs_all, keep_up, w_up.shape, False
    )
    return (outputs, grad_inputs, grad_up, grad_down)


def solution(mesh):
    in_specs = (
        P("col", "row"),
        P("row", "col"),
        P("col", "row"),
        P("row", "col"),
        P("col", "row"),
        P("col", "row"),
    )
    out_specs = (P("col", "row"), P("col", "row"), P("row", "col"), P("col", "row"))
    n_row, n_col = mesh.shape["row"], mesh.shape["col"]

    def per_device(inputs, w_up, w_down, mask_up, mask_down, cotangent):
        fits = n_row == 8 and mask_up.shape[1] % n_row == 0
        plan = functools.partial(per_device_tuned, n_row, n_col) if fits else per_device_plain
        return plan(inputs, w_up, w_down, mask_up, mask_down, cotangent)

    return jax.shard_map(
        per_device, mesh=mesh, in_specs=in_specs, out_specs=out_specs, check_vma=False
    )
```

```python
import functools

import jax
import jax.numpy as jnp
from jax import lax
from jax.experimental import pallas as pl
from jax.experimental.pallas import tpu as pltpu
from jax.sharding import PartitionSpec as P

TILE = 128
MIB = 1 << 20
F32 = jnp.float32
BF16 = jnp.bfloat16


def smooth_gate(value):
    return jax.nn.gelu(value, approximate=True)


def contract(left, right, left_dim, right_dim):
    return lax.dot_general(
        left, right, (((left_dim,), (right_dim,)), ((), ())), preferred_element_type=F32
    )


def apply_mask(weight, mask):
    rows, cols = mask.shape
    tile = weight.shape[0] // rows
    shaped = weight.reshape(rows, tile, cols, tile)
    keep = mask[:, None, :, None].astype(weight.dtype)
    return (shaped * keep).reshape(weight.shape)


def activate(hidden, grad_act):
    act = smooth_gate(hidden).astype(BF16)
    _, pull = jax.vjp(smooth_gate, hidden)
    grad_hidden = pull(grad_act)[0].astype(BF16)
    return (act, grad_hidden)


def per_device_plain(inputs, w_up, w_down, mask_up, mask_down, cotangent):
    up_kept = apply_mask(w_up, mask_up)
    down_kept = apply_mask(w_down, mask_down)
    inputs_all, cot_all = (
        lax.all_gather(inputs, "col", axis=0, tiled=True),
        lax.all_gather(cotangent, "col", axis=0, tiled=True),
    )
    up_part = jnp.dot(inputs_all, up_kept, preferred_element_type=F32)
    back_part = contract(cot_all, down_kept, 1, 1)
    hidden, grad_act = (
        lax.psum_scatter(
            part.astype(BF16), "row", scatter_dimension=0, tiled=True
        ).astype(F32)
        for part in (up_part, back_part)
    )
    act, grad_hidden = activate(hidden, grad_act)
    act_all, grad_all = (
        lax.all_gather(act, "row", axis=0, tiled=True),
        lax.all_gather(grad_hidden, "row", axis=0, tiled=True),
    )
    out_part = jnp.dot(act_all, down_kept, preferred_element_type=F32)
    input_part = contract(grad_all, up_kept, 1, 1)
    outputs, grad_inputs = (
        lax.psum_scatter(
            part.astype(BF16), "col", scatter_dimension=0, tiled=True
        ).astype(F32)
        for part in (out_part, input_part)
    )
    grad_down = apply_mask(contract(act_all, cot_all, 0, 0).astype(BF16), mask_down)
    grad_up = apply_mask(contract(inputs_all, grad_all, 0, 0).astype(BF16), mask_up)
    return (outputs.astype(BF16), grad_inputs.astype(BF16), grad_up, grad_down)


OWN, CORE, X, Y = 0, 1, 2, 4
DIAG = X | Y
SEND = (CORE | DIAG, CORE | X, CORE | Y, CORE)
KEEP = (DIAG, X, Y, OWN)
EARLY = (OWN, CORE, X, Y, CORE | X, CORE | Y)
LATE = (DIAG, CORE | DIAG)
ALL = EARLY + LATE
TABLE = SEND + KEEP + ALL
AT_SEND, AT_KEEP, AT_ALL = 0, len(SEND), len(SEND) + len(KEEP)
AT_LATE = AT_ALL + len(EARLY)


def kept_tiles(weight, keep, columns=slice(None)):
    strips = range(0, weight.shape[0], TILE)
    return jnp.concatenate(
        [weight[lo : lo + TILE, columns] * keep[lo // TILE : lo // TILE + 1, columns] for lo in strips]
    )


def spans(length):
    span = 2 * TILE if length % (2 * TILE) == 0 else TILE
    return [slice(lo, lo + span) for lo in range(0, length, span)]


def cost(flops, moved):
    return pl.CostEstimate(flops=int(flops), bytes_accessed=int(moved), transcendentals=0)


def params(mib):
    return pltpu.CompilerParams(
        dimension_semantics=("arbitrary",), vmem_limit_bytes=mib * MIB
    )


def weight_specs(weight, keep, share, at, by_rows):
    if by_rows:
        return (
            pl.BlockSpec((share, weight.shape[1]), lambda i, t: (t[at + i], 0)),
            pl.BlockSpec((None,) + keep.shape[1:], lambda i, t: (t[at + i], 0, 0)),
        )
    return (
        pl.BlockSpec((weight.shape[0], share), lambda i, t: (0, t[at + i])),
        pl.BlockSpec((keep.shape[0], share), lambda i, t: (0, t[at + i])),
    )


def whole(array):
    return pl.BlockSpec(array.shape, lambda i, t: (0,) * len(array.shape))


def project(table, parts, weight, keep, share, by_rows, got=None):
    tokens = sum(part.shape[0] for part in parts)
    half = tokens // 2
    wide = parts[0].shape[1]
    at = AT_SEND if got is None else AT_KEEP
    weight_spec, keep_spec = weight_specs(weight, keep, share, at, by_rows)

    def body(table_ref, *refs):
        refs = list(refs)
        part_refs = [refs.pop(0) for _ in parts]
        weight_ref, keep_ref = refs.pop(0), refs.pop(0)
        got_ref = None if got is None else refs.pop(0)
        held = refs.pop()
        outs = refs
        i = pl.program_id(0)

        @pl.when(i == 0)
        def _():
            row = 0
            for ref in part_refs:
                if by_rows:
                    held[:, row : row + ref.shape[0]] = ref[...].T
                else:
                    held[row : row + ref.shape[0], :] = ref[...]
                row += ref.shape[0]

        if by_rows:
            result = contract(kept_tiles(weight_ref, keep_ref), held[...], 1, 0).T
        else:
            result = jnp.concatenate(
                [
                    contract(held[...], kept_tiles(weight_ref, keep_ref, columns), 1, 0)
                    for columns in spans(share)
                ],
                axis=1,
            )
        if got is None:
            outs[0][...] = result.astype(BF16)
            return
        result = (result + got_ref[...].astype(F32)).astype(BF16)
        x_send, y_send, x_keep, y_keep = outs

        @pl.when(i < 2)
        def _():
            x_send[...] = result[:half]

        @pl.when(i >= 2)
        def _():
            x_keep[...] = result[:half]

        @pl.when(i % 2 == 0)
        def _():
            y_send[...] = result[half:]

        @pl.when(i % 2 == 1)
        def _():
            y_keep[...] = result[half:]

    flops = 2 * tokens * wide * share * 4
    moved = 2 * (wide * share * 4 + tokens * share * (4 if got is None else 8) + tokens * wide)
    in_specs = [whole(part) for part in parts] + [weight_spec, keep_spec]
    if got is None:
        out_shape = jax.ShapeDtypeStruct((4, tokens, share), BF16)
        out_specs = pl.BlockSpec((None, tokens, share), lambda i, t: (i, 0, 0))
    else:
        in_specs.append(pl.BlockSpec((None, tokens, share), lambda i, t: (i, 0, 0)))
        out_shape = (jax.ShapeDtypeStruct((2, half, share), BF16),) * 4
        block = (None, half, share)
        out_specs = (
            pl.BlockSpec(block, lambda i, t: (jnp.minimum(i, 1), 0, 0)),
            pl.BlockSpec(block, lambda i, t: (i // 2, 0, 0)),
            pl.BlockSpec(block, lambda i, t: (jnp.maximum(i - 2, 0), 0, 0)),
            pl.BlockSpec(block, lambda i, t: (i // 2, 0, 0)),
        )
    call = pl.pallas_call(
        body,
        out_shape=out_shape,
        grid_spec=pltpu.PrefetchScalarGridSpec(
            num_scalar_prefetch=1,
            grid=(4,),
            in_specs=in_specs,
            out_specs=out_specs,
            scratch_shapes=[
                pltpu.VMEM((wide, tokens) if by_rows else (tokens, wide), BF16),
            ],
        ),
        compiler_params=params(40),
        cost_estimate=cost(flops, moved),
    )
    return call(table, *parts, weight, keep, *(() if got is None else (got,)))


def fetch(i, pieces, refs, held, sems):
    copies, n = [], 0
    for at, piece in enumerate(pieces):
        row, own = 0, []
        for array in piece:
            rows = array.shape[0]
            own.append(
                pltpu.make_async_copy(refs[n], held.at[at, pl.ds(row, rows)], sems.at[n])
            )
            row += rows
            n += 1
        copies.append(own)

    @pl.when(i == 0)
    def _():
        for own in copies:
            for copy in own:
                copy.start()

    for at, own in enumerate(copies):

        @pl.when(i == at)
        def _(own=own):
            for copy in own:
                copy.wait()


def gathered(table, pieces, weight, keep, at, by_rows, base=None, blocks=1):
    tokens = sum(array.shape[0] for array in pieces[0])
    share = pieces[0][0].shape[1]
    steps = len(pieces)
    flat = [array for piece in pieces for array in piece]
    wide = weight.shape[1] if by_rows else weight.shape[0]
    weight_spec, keep_spec = weight_specs(weight, keep, share, at, by_rows)
    rows = tokens // blocks
    total_shape = (tokens, wide) if by_rows else (wide, tokens)

    def body(table_ref, *refs):
        refs = list(refs)
        piece_refs = [refs.pop(0) for _ in flat]
        weight_ref, keep_ref = refs.pop(0), refs.pop(0)
        base_ref = None if base is None else refs.pop(0)
        held, sems = refs[-2:]
        total = refs[-3] if base is not None else refs[0]
        outs = refs[:blocks]
        i = pl.program_id(0)
        fetch(i, pieces, piece_refs, held, sems)
        left = held[i]
        if not by_rows:
            left = left.T

        def add(term, columns):
            @pl.when(i == 0)
            def _():
                total[:, columns] = term if base is None else term + base_ref[:, columns]

            @pl.when(i > 0)
            def _():
                total[:, columns] += term

        if by_rows:
            for columns in spans(wide):
                add(contract(left, kept_tiles(weight_ref, keep_ref, columns), 1, 0), columns)
        else:
            add(contract(kept_tiles(weight_ref, keep_ref), left, 1, 0), slice(None))

        if base is not None:

            @pl.when(i == steps - 1)
            def _():
                summed = total[...] if by_rows else total[...].T
                for k, out in enumerate(outs):
                    out[...] = summed[k * rows : (k + 1) * rows, :].astype(BF16)

    in_specs = [pl.BlockSpec(memory_space=pl.ANY)] * len(flat) + [weight_spec, keep_spec]
    scratch = [
        pltpu.VMEM((steps, tokens, share), BF16),
        pltpu.SemaphoreType.DMA((len(flat),)),
    ]
    args = [*flat, weight, keep]
    if base is None:
        out_shape = jax.ShapeDtypeStruct(total_shape, F32)
        out_specs = whole(out_shape)
    else:
        in_specs.append(whole(base))
        args.append(base)
        out_shape = (jax.ShapeDtypeStruct((rows, wide), BF16),) * blocks
        out_specs = (whole(out_shape[0]),) * blocks
        scratch.insert(0, pltpu.VMEM(total_shape, F32))
    call = pl.pallas_call(
        body,
        out_shape=out_shape,
        grid_spec=pltpu.PrefetchScalarGridSpec(
            num_scalar_prefetch=1,
            grid=(steps,),
            in_specs=in_specs,
            out_specs=out_specs,
            scratch_shapes=scratch,
        ),
        compiler_params=params(40),
        cost_estimate=cost(
            2 * tokens * share * wide * steps,
            2 * share * (wide + tokens) * steps + 4 * tokens * wide,
        ),
    )
    return call(table, *args)


def weight_gradient(table, pieces, parts, keep, shape, by_rows):
    tokens = sum(part.shape[0] for part in parts)
    share = pieces[0][0].shape[1]
    wide = parts[0].shape[1]
    steps = len(pieces)
    flat = [array for piece in pieces for array in piece]
    weight_spec, keep_spec = weight_specs(
        jax.ShapeDtypeStruct(shape, BF16), keep, share, AT_ALL, by_rows
    )

    def body(table_ref, *refs):
        refs = list(refs)
        piece_refs = [refs.pop(0) for _ in flat]
        part_refs = [refs.pop(0) for _ in parts]
        keep_ref, out, held, other, sems = refs
        i = pl.program_id(0)

        @pl.when(i == 0)
        def _():
            row = 0
            for ref in part_refs:
                if by_rows:
                    other[row : row + ref.shape[0], :] = ref[...]
                else:
                    other[:, row : row + ref.shape[0]] = ref[...].T
                row += ref.shape[0]

        fetch(i, pieces, piece_refs, held, sems)
        left = held[i].T if by_rows else other[...]
        right = other if by_rows else held.at[i]
        for columns in spans(out.shape[1]):
            term = contract(left, right[:, columns], 1, 0).astype(BF16)
            for k in range(out.shape[0] // TILE):
                strip = slice(k * TILE, (k + 1) * TILE)
                out[strip, columns] = term[strip] * keep_ref[k : k + 1, columns]

    call = pl.pallas_call(
        body,
        out_shape=jax.ShapeDtypeStruct(shape, BF16),
        grid_spec=pltpu.PrefetchScalarGridSpec(
            num_scalar_prefetch=1,
            grid=(steps,),
            in_specs=[pl.BlockSpec(memory_space=pl.ANY)] * len(flat)
            + [whole(part) for part in parts]
            + [keep_spec],
            out_specs=weight_spec,
            scratch_shapes=[
                pltpu.VMEM((steps, tokens, share), BF16),
                pltpu.VMEM((tokens, wide) if by_rows else (wide, tokens), BF16),
                pltpu.SemaphoreType.DMA((len(flat),)),
            ],
        ),
        compiler_params=params(40),
        cost_estimate=cost(
            2 * tokens * share * wide * steps, 2 * share * (wide + tokens) * steps
        ),
    )
    return call(table, *flat, *parts, keep)


def per_device_tuned(n_row, n_col, inputs, w_up, w_down, mask_up, mask_down, cotangent):
    share = w_up.shape[1] // n_row
    table = jnp.asarray(TABLE, jnp.int32) ^ lax.axis_index("row")
    keep_up = jnp.repeat(mask_up.astype(BF16), TILE, axis=1)
    keep_down = jnp.repeat(mask_down.astype(BF16), TILE, axis=1).reshape(
        n_row, share // TILE, w_down.shape[1]
    )

    def across(value, bits):
        return lax.ppermute(value, "row", [(i, i ^ bits) for i in range(n_row)])

    def along(value, shift):
        return lax.ppermute(value, "col", [(i, (i + shift) % n_col) for i in range(n_col)])

    def col_gather(value):
        return [value] + [along(value, k) for k in range(1, n_col)]

    def row_sum(table, parts, weight, keep, by_rows):
        got = across(project(table, parts, weight, keep, share, by_rows), CORE)
        x_send, y_send, x_keep, y_keep = project(
            table, parts, weight, keep, share, by_rows, got
        )
        x_got, y_got = across(x_send, X), across(y_send, Y)
        x_pass = (x_keep[0].astype(F32) + x_got[0].astype(F32)).astype(BF16)
        y_pass = (y_keep[0].astype(F32) + y_got[0].astype(F32)).astype(BF16)
        x_last, y_last = across(x_pass, Y), across(y_pass, X)
        total = jnp.concatenate(
            [
                x_keep[1].astype(F32) + x_got[1].astype(F32) + x_last.astype(F32),
                y_keep[1].astype(F32) + y_got[1].astype(F32) + y_last.astype(F32),
            ]
        )
        return total, x_send

    def row_gather(value):
        half = value.shape[0] // 2
        from_core, from_x, from_y = (across(value, bits) for bits in (CORE, X, Y))
        core_x, core_y = across(from_x, CORE), across(from_y, CORE)
        diag = (across(from_x[:half], Y), across(from_y[half:], X))
        core_diag = tuple(across(part, CORE) for part in diag)
        early = [(value,), (from_core,), (from_x,), (from_y,), (core_x,), (core_y,)]
        return early, [diag, core_diag]

    def col_sum(blocks):
        terms = [blocks[0]] + [along(blocks[k], -k) for k in range(1, n_col)]
        return functools.reduce(jnp.add, [term.astype(F32) for term in terms]).astype(BF16)

    inputs_all = col_gather(inputs)
    cot_first, *_ = lax.optimization_barrier((cotangent, *inputs_all[1:]))
    cot_all = [cotangent] + [along(cot_first, k) for k in range(1, n_col)]

    hidden, projected = row_sum(table, inputs_all, w_up, keep_up, False)
    later, _ = lax.optimization_barrier((table, projected))
    grad_act, back_projected = row_sum(later, cot_all, w_down, keep_down, True)
    hidden, _ = lax.optimization_barrier((hidden, back_projected))
    hidden, act = lax.optimization_barrier((hidden, smooth_gate(hidden).astype(BF16)))
    act_early, act_late = row_gather(act)
    _, pull = jax.vjp(smooth_gate, hidden)
    grad_early, grad_late = row_gather(pull(grad_act)[0].astype(BF16))

    out_base = gathered(table, act_early, w_down, keep_down, AT_ALL, True)
    outputs = col_sum(
        gathered(table, act_late, w_down, keep_down, AT_LATE, True, out_base, n_col)
    )
    grad_down = weight_gradient(
        table, act_early + act_late, cot_all, keep_down, w_down.shape, True
    )
    in_base = gathered(table, grad_early, w_up, keep_up, AT_ALL, False)
    grad_inputs = col_sum(
        gathered(table, grad_late, w_up, keep_up, AT_LATE, False, in_base, n_col)
    )
    grad_up = weight_gradient(
        table, grad_early + grad_late, inputs_all, keep_up, w_up.shape, False
    )
    return (outputs, grad_inputs, grad_up, grad_down)


def solution(mesh):
    in_specs = (
        P("col", "row"),
        P("row", "col"),
        P("col", "row"),
        P("row", "col"),
        P("col", "row"),
        P("col", "row"),
    )
    out_specs = (P("col", "row"), P("col", "row"), P("row", "col"), P("col", "row"))
    n_row, n_col = mesh.shape["row"], mesh.shape["col"]

    def per_device(inputs, w_up, w_down, mask_up, mask_down, cotangent):
        fits = n_row == 8 and mask_up.shape[1] % n_row == 0
        plan = functools.partial(per_device_tuned, n_row, n_col) if fits else per_device_plain
        return plan(inputs, w_up, w_down, mask_up, mask_down, cotangent)

    return jax.shard_map(
        per_device, mesh=mesh, in_specs=in_specs, out_specs=out_specs, check_vma=False
    )
```

```python
import functools

import jax
import jax.numpy as jnp
from jax import lax
from jax.experimental import pallas as pl
from jax.experimental.pallas import tpu as pltpu
from jax.sharding import PartitionSpec as P

TILE = 128
MIB = 1 << 20
F32 = jnp.float32
BF16 = jnp.bfloat16


def smooth_gate(value):
    return jax.nn.gelu(value, approximate=True)


def contract(left, right, left_dim, right_dim):
    return lax.dot_general(
        left, right, (((left_dim,), (right_dim,)), ((), ())), preferred_element_type=F32
    )


def apply_mask(weight, mask):
    rows, cols = mask.shape
    tile = weight.shape[0] // rows
    shaped = weight.reshape(rows, tile, cols, tile)
    keep = mask[:, None, :, None].astype(weight.dtype)
    return (shaped * keep).reshape(weight.shape)


def activate(hidden, grad_act):
    act = smooth_gate(hidden).astype(BF16)
    _, pull = jax.vjp(smooth_gate, hidden)
    grad_hidden = pull(grad_act)[0].astype(BF16)
    return (act, grad_hidden)


def per_device_plain(inputs, w_up, w_down, mask_up, mask_down, cotangent):
    up_kept = apply_mask(w_up, mask_up)
    down_kept = apply_mask(w_down, mask_down)
    inputs_all, cot_all = (
        lax.all_gather(inputs, "col", axis=0, tiled=True),
        lax.all_gather(cotangent, "col", axis=0, tiled=True),
    )
    up_part = jnp.dot(inputs_all, up_kept, preferred_element_type=F32)
    back_part = contract(cot_all, down_kept, 1, 1)
    hidden, grad_act = (
        lax.psum_scatter(
            part.astype(BF16), "row", scatter_dimension=0, tiled=True
        ).astype(F32)
        for part in (up_part, back_part)
    )
    act, grad_hidden = activate(hidden, grad_act)
    act_all, grad_all = (
        lax.all_gather(act, "row", axis=0, tiled=True),
        lax.all_gather(grad_hidden, "row", axis=0, tiled=True),
    )
    out_part = jnp.dot(act_all, down_kept, preferred_element_type=F32)
    input_part = contract(grad_all, up_kept, 1, 1)
    outputs, grad_inputs = (
        lax.psum_scatter(
            part.astype(BF16), "col", scatter_dimension=0, tiled=True
        ).astype(F32)
        for part in (out_part, input_part)
    )
    grad_down = apply_mask(contract(act_all, cot_all, 0, 0).astype(BF16), mask_down)
    grad_up = apply_mask(contract(inputs_all, grad_all, 0, 0).astype(BF16), mask_up)
    return (outputs.astype(BF16), grad_inputs.astype(BF16), grad_up, grad_down)


OWN, CORE, X, Y = 0, 1, 2, 4
DIAG = X | Y
SEND = (CORE | DIAG, CORE | X, CORE | Y, CORE)
KEEP = (DIAG, X, Y, OWN)
EARLY = (OWN, CORE, X, Y, CORE | X, CORE | Y)
LATE = (DIAG, CORE | DIAG)
TABLE = SEND + KEEP + EARLY + LATE
AT_SEND = 0
AT_KEEP = AT_SEND + len(SEND)
AT_EARLY = AT_KEEP + len(KEEP)
AT_LATE = AT_EARLY + len(EARLY)
WAYS = 3


def cost(flops, moved):
    return pl.CostEstimate(
        flops=int(flops) // 8, bytes_accessed=int(moved) // 8, transcendentals=0
    )


def params(mib):
    return pltpu.CompilerParams(
        dimension_semantics=("arbitrary",), vmem_limit_bytes=mib * MIB
    )


def whole(array):
    return pl.BlockSpec(array.shape, lambda i, t: (0,) * len(array.shape))


def keep_spec_of(keep, share, at, by_rows):
    if by_rows:
        return pl.BlockSpec((None,) + keep.shape[1:], lambda i, t: (t[at + i], 0, 0))
    return pl.BlockSpec((keep.shape[0], share), lambda i, t: (0, t[at + i]))


def weight_specs(weight, keep, share, at, by_rows):
    if by_rows:
        shape = (share, weight.shape[1])
        part = (share // WAYS, weight.shape[1])
        place = [lambda i, t, q=q: (t[at + i] * WAYS + q, 0) for q in range(WAYS)]
    else:
        shape = (weight.shape[0], share)
        part = (weight.shape[0] // WAYS, share)
        place = [lambda i, t, q=q: (q, t[at + i]) for q in range(WAYS)]
    specs = [pl.BlockSpec(part, where) for where in place]
    return specs + [keep_spec_of(keep, share, at, by_rows)], shape


def keep_tiles(dst, weight_refs, keep):
    rows = weight_refs[0].shape[0]
    for q, ref in enumerate(weight_refs):
        for lo in range(0, rows, TILE):
            tile = (q * rows + lo) // TILE
            dst[q * rows + lo : q * rows + lo + TILE, :] = (
                ref[lo : lo + TILE, :] * keep[tile : tile + 1, :]
            )


def stack(dst, refs):
    row = 0
    for ref in refs:
        dst[row : row + ref.shape[0], :] = ref[...]
        row += ref.shape[0]


def project(table, parts, weight, keep, share, at, by_rows):
    tokens = sum(part.shape[0] for part in parts)
    wide = parts[0].shape[1]
    specs, kept_shape = weight_specs(weight, keep, share, at, by_rows)

    def body(table_ref, *refs):
        part_refs, refs = refs[: len(parts)], refs[len(parts) :]
        weight_refs, (keep_ref, out, held, kept) = refs[:WAYS], refs[WAYS:]

        @pl.when(pl.program_id(0) == 0)
        def _():
            stack(held, part_refs)

        keep_tiles(kept, weight_refs, keep_ref)
        out[...] = contract(held[...], kept[...], 1, 1 if by_rows else 0).astype(BF16)

    call = pl.pallas_call(
        body,
        out_shape=jax.ShapeDtypeStruct((4, tokens, share), BF16),
        grid_spec=pltpu.PrefetchScalarGridSpec(
            num_scalar_prefetch=1,
            grid=(4,),
            in_specs=[whole(part) for part in parts] + specs,
            out_specs=pl.BlockSpec((None, tokens, share), lambda i, t: (i, 0, 0)),
            scratch_shapes=[
                pltpu.VMEM((tokens, wide), BF16),
                pltpu.VMEM(kept_shape, BF16),
            ],
        ),
        compiler_params=params(32),
        cost_estimate=cost(
            8 * tokens * wide * share, 2 * (4 * share * (wide + tokens) + tokens * wide)
        ),
    )
    return call(table, *parts, *[weight] * WAYS, keep)


def fetch(i, pieces, refs, held, sems):
    copies, n = [], 0
    for at, piece in enumerate(pieces):
        row, own = 0, []
        for array in piece:
            rows = array.shape[0]
            own.append(
                pltpu.make_async_copy(refs[n], held.at[at, pl.ds(row, rows)], sems.at[n])
            )
            row += rows
            n += 1
        copies.append(own)

    @pl.when(i == 0)
    def _():
        for own in copies:
            for copy in own:
                copy.start()

    for at, own in enumerate(copies):

        @pl.when(i == at)
        def _(own=own):
            for copy in own:
                copy.wait()


def gathered(table, pieces, weight, keep, at, by_rows, base=None, blocks=1):
    tokens = sum(array.shape[0] for array in pieces[0])
    share = pieces[0][0].shape[1]
    steps = len(pieces)
    flat = [array for piece in pieces for array in piece]
    wide = weight.shape[1] if by_rows else weight.shape[0]
    specs, kept_shape = weight_specs(weight, keep, share, at, by_rows)
    rows = tokens // blocks
    total_shape = (tokens, wide)

    def body(table_ref, *refs):
        piece_refs, refs = refs[: len(flat)], refs[len(flat) :]
        weight_refs, (keep_ref, *refs) = refs[:WAYS], refs[WAYS:]
        i = pl.program_id(0)
        if base is None:
            total, held, kept, sems = refs
        else:
            base_ref, *outs, total, held, kept, sems = refs
        fetch(i, pieces, piece_refs, held, sems)

        @pl.when(i == 0)
        def _():
            total[...] = jnp.zeros(total_shape, F32) if base is None else base_ref[...]

        keep_tiles(kept, weight_refs, keep_ref)
        total[...] += contract(held[i], kept[...], 1, 0 if by_rows else 1)

        if base is not None:

            @pl.when(i == steps - 1)
            def _():
                for k, out in enumerate(outs):
                    out[...] = total[k * rows : (k + 1) * rows, :].astype(BF16)

    in_specs = [pl.BlockSpec(memory_space=pl.ANY)] * len(flat) + specs
    scratch = [
        pltpu.VMEM((steps, tokens, share), BF16),
        pltpu.VMEM(kept_shape, BF16),
        pltpu.SemaphoreType.DMA((len(flat),)),
    ]
    args = [*flat, *[weight] * WAYS, keep]
    if base is None:
        out_shape = jax.ShapeDtypeStruct(total_shape, F32)
        out_specs = whole(out_shape)
    else:
        in_specs.append(whole(base))
        args.append(base)
        out_shape = (jax.ShapeDtypeStruct((rows, wide), BF16),) * blocks
        out_specs = (whole(out_shape[0]),) * blocks
        scratch.insert(0, pltpu.VMEM(total_shape, F32))
    call = pl.pallas_call(
        body,
        out_shape=out_shape,
        grid_spec=pltpu.PrefetchScalarGridSpec(
            num_scalar_prefetch=1,
            grid=(steps,),
            in_specs=in_specs,
            out_specs=out_specs,
            scratch_shapes=scratch,
        ),
        compiler_params=params(32),
        cost_estimate=cost(
            2 * tokens * share * wide * steps,
            2 * share * (wide + tokens) * steps + 4 * tokens * wide,
        ),
    )
    return call(table, *args)


def weight_gradient(table, pieces, parts, keep, shape, by_rows):
    tokens = sum(part.shape[0] for part in parts)
    share = pieces[0][0].shape[1]
    wide = parts[0].shape[1]
    steps = len(pieces)
    flat = [array for piece in pieces for array in piece]
    block = (share, wide) if by_rows else (wide, share)
    rows = block[0] // WAYS

    def body(table_ref, *refs):
        piece_refs, refs = refs[: len(flat)], refs[len(flat) :]
        part_refs, refs = refs[: len(parts)], refs[len(parts) :]
        keep_ref, out, made, held, other, sems, out_sems = refs
        i = pl.program_id(0)
        slot = i % 2

        def copies(step):
            number = table_ref[AT_EARLY + step]
            for q in range(WAYS):
                if by_rows:
                    start = pl.multiple_of(number * share + q * rows, TILE)
                    target = out.at[pl.ds(start, rows)]
                else:
                    start = pl.multiple_of(number * share, TILE)
                    target = out.at[pl.ds(q * rows, rows), pl.ds(start, share)]
                yield pltpu.make_async_copy(
                    made.at[step % 2, pl.ds(q * rows, rows)], target, out_sems.at[step % 2, q]
                )

        @pl.when(i == 0)
        def _():
            if by_rows:
                stack(other, part_refs)
            else:
                row = 0
                for ref in part_refs:
                    other[:, row : row + ref.shape[0]] = ref[...].T
                    row += ref.shape[0]

        fetch(i, pieces, piece_refs, held, sems)

        @pl.when(i >= 2)
        def _():
            for copy in copies(i - 2):
                copy.wait()

        left = held[i].T if by_rows else other
        right = other[...] if by_rows else held[i]
        span = 2 * TILE
        for lo in range(0, block[0], span):
            term = contract(left[lo : lo + span, :], right, 1, 0)
            for k in range(0, span, TILE):
                tile = (lo + k) // TILE
                made[slot, lo + k : lo + k + TILE, :] = (
                    term[k : k + TILE].astype(BF16) * keep_ref[tile : tile + 1, :]
                )
        for copy in copies(i):
            copy.start()

        @pl.when(i == steps - 1)
        def _():
            for step in (i - 1, i):
                for copy in copies(step):
                    copy.wait()

    call = pl.pallas_call(
        body,
        out_shape=jax.ShapeDtypeStruct(shape, BF16),
        grid_spec=pltpu.PrefetchScalarGridSpec(
            num_scalar_prefetch=1,
            grid=(steps,),
            in_specs=[pl.BlockSpec(memory_space=pl.ANY)] * len(flat)
            + [whole(part) for part in parts]
            + [keep_spec_of(keep, share, AT_EARLY, by_rows)],
            out_specs=pl.BlockSpec(memory_space=pl.ANY),
            scratch_shapes=[
                pltpu.VMEM((2,) + block, BF16),
                pltpu.VMEM((steps, tokens, share), BF16),
                pltpu.VMEM((tokens, wide) if by_rows else (wide, tokens), BF16),
                pltpu.SemaphoreType.DMA((len(flat),)),
                pltpu.SemaphoreType.DMA((2, WAYS)),
            ],
        ),
        compiler_params=params(32),
        cost_estimate=cost(
            2 * tokens * share * wide * steps, 2 * share * (wide + tokens) * steps
        ),
    )
    return call(table, *flat, *parts, keep)


def per_device_tuned(n_row, n_col, inputs, w_up, w_down, mask_up, mask_down, cotangent):
    share = w_up.shape[1] // n_row
    table = jnp.asarray(TABLE, jnp.int32) ^ lax.axis_index("row")
    keep_up = jnp.repeat(mask_up.astype(BF16), TILE, axis=1)
    keep_down = jnp.repeat(mask_down.astype(BF16), TILE, axis=1).reshape(
        n_row, share // TILE, w_down.shape[1]
    )

    def across(value, bits):
        return lax.ppermute(value, "row", [(i, i ^ bits) for i in range(n_row)])

    def along(value, shift):
        return lax.ppermute(value, "col", [(i, (i + shift) % n_col) for i in range(n_col)])

    def col_gather(value):
        return [value] + [along(value, k) for k in range(1, n_col)]

    def after(value, *done):
        return lax.optimization_barrier((value, *done))[0]

    def send(parts, weight, keep, by_rows, start):
        return project(after(table, start), parts, weight, keep, share, AT_SEND, by_rows)

    def hold(parts, weight, keep, by_rows, start):
        return project(after(table, start), parts, weight, keep, share, AT_KEEP, by_rows)

    def core_sum(kept, got):
        half = kept.shape[1] // 2
        by_x, by_y = (
            kept[:, rows].astype(F32) + got[:, rows].astype(F32)
            for rows in (slice(0, half), slice(half, 2 * half))
        )
        sends = by_x[0:2].astype(BF16), by_y[0:3:2].astype(BF16)
        return (by_x, by_y), sends

    def exchange(along_x, along_y, beside=None):
        pair = across(along_x, X), across(along_y, Y)
        if beside is not None:
            *pair, beside = lax.optimization_barrier((*pair, beside))
        return [value.astype(F32) for value in pair], beside

    def pass_on(sums, x_got, y_got):
        by_x, by_y = sums
        return (by_y[1] + y_got[0]).astype(BF16), (by_x[2] + x_got[0]).astype(BF16)

    def own_sum(sums, x_got, y_got, x_last, y_last):
        by_x, by_y = sums
        return jnp.concatenate(
            [by_x[3] + x_got[1] + x_last, by_y[3] + y_got[1] + y_last]
        )

    def row_gather(value):
        half = value.shape[0] // 2
        from_core, from_x, from_y = (across(value, bits) for bits in (CORE, X, Y))
        core_x, core_y = across(from_x, CORE), across(from_y, CORE)
        diag = (across(from_x[:half], Y), across(from_y[half:], X))
        core_diag = tuple(across(part, CORE) for part in diag)
        early = [(value,), (from_core,), (from_x,), (from_y,), (core_x,), (core_y,)]
        return early, [diag, core_diag]

    def col_sum(blocks):
        terms = [blocks[0]] + [along(blocks[k], -k) for k in range(1, n_col)]
        return functools.reduce(jnp.add, [term.astype(F32) for term in terms]).astype(BF16)

    inputs_all = col_gather(inputs)
    cot_all = [cotangent]
    for k in range(1, n_col):
        own, _ = lax.optimization_barrier((cotangent, inputs_all[k]))
        cot_all.append(along(own, k))

    up_sent = send(inputs_all, w_up, keep_up, False, inputs)
    up_got = across(up_sent, CORE)
    up_held = hold(inputs_all, w_up, keep_up, False, up_sent)
    up_held, *cot_all[1:] = lax.optimization_barrier((up_held, *cot_all[1:]))
    sums, sends = core_sum(up_held, up_got)

    back_sent = send(cot_all, w_down, keep_down, True, sends[0])
    (x_got, y_got), back_sent = exchange(*sends, back_sent)
    back_got = across(back_sent, CORE)
    back_held = hold(cot_all, w_down, keep_down, True, back_sent)
    (y_last, x_last), back_held = exchange(*pass_on(sums, x_got, y_got), back_held)
    hidden = own_sum(sums, x_got, y_got, x_last, y_last)

    sums, sends = core_sum(back_held, back_got)
    (x_got, y_got), _ = exchange(*sends)
    (y_last, x_last), _ = exchange(*pass_on(sums, x_got, y_got))
    grad_act = own_sum(sums, x_got, y_got, x_last, y_last)
    hidden, act = lax.optimization_barrier((hidden, smooth_gate(hidden).astype(BF16)))
    act_early, act_late = row_gather(act)
    _, pull = jax.vjp(smooth_gate, hidden)
    grad_early, grad_late = row_gather(pull(grad_act)[0].astype(BF16))

    out_base = gathered(table, act_early, w_down, keep_down, AT_EARLY, True)
    outputs = col_sum(
        gathered(table, act_late, w_down, keep_down, AT_LATE, True, out_base, n_col)
    )
    grad_down = weight_gradient(
        table, act_early + act_late, cot_all, keep_down, w_down.shape, True
    )
    in_base = gathered(table, grad_early, w_up, keep_up, AT_EARLY, False)
    grad_inputs = col_sum(
        gathered(table, grad_late, w_up, keep_up, AT_LATE, False, in_base, n_col)
    )
    grad_up = weight_gradient(
        table, grad_early + grad_late, inputs_all, keep_up, w_up.shape, False
    )
    return (outputs, grad_inputs, grad_up, grad_down)


def solution(mesh):
    in_specs = (
        P("col", "row"),
        P("row", "col"),
        P("col", "row"),
        P("row", "col"),
        P("col", "row"),
        P("col", "row"),
    )
    out_specs = (P("col", "row"), P("col", "row"), P("row", "col"), P("col", "row"))
    n_row, n_col = mesh.shape["row"], mesh.shape["col"]

    def per_device(inputs, w_up, w_down, mask_up, mask_down, cotangent):
        fits = n_row == 8 and mask_up.shape[1] % n_row == 0
        plan = functools.partial(per_device_tuned, n_row, n_col) if fits else per_device_plain
        return plan(inputs, w_up, w_down, mask_up, mask_down, cotangent)

    return jax.shard_map(
        per_device, mesh=mesh, in_specs=in_specs, out_specs=out_specs, check_vma=False
    )
```

```python
import functools

import jax
import jax.numpy as jnp
from jax import lax
from jax.experimental import pallas as pl
from jax.experimental.pallas import tpu as pltpu
from jax.sharding import PartitionSpec as P

TILE = 128
VMEM_LIMIT = 14 << 20
PIECE = 768
F32 = jnp.float32
BF16 = jnp.bfloat16


def smooth_gate(value):
    return jax.nn.gelu(value, approximate=True)


def contract(left, right, left_dim, right_dim):
    return lax.dot_general(
        left, right, (((left_dim,), (right_dim,)), ((), ())), preferred_element_type=F32
    )


def apply_mask(weight, mask):
    rows, cols = mask.shape
    tile = weight.shape[0] // rows
    shaped = weight.reshape(rows, tile, cols, tile)
    keep = mask[:, None, :, None].astype(weight.dtype)
    return (shaped * keep).reshape(weight.shape)


def activate(hidden, grad_act):
    act = smooth_gate(hidden).astype(BF16)
    _, pull = jax.vjp(smooth_gate, hidden)
    grad_hidden = pull(grad_act)[0].astype(BF16)
    return (act, grad_hidden)


def per_device_plain(inputs, w_up, w_down, mask_up, mask_down, cotangent):
    up_kept = apply_mask(w_up, mask_up)
    down_kept = apply_mask(w_down, mask_down)
    inputs_all, cot_all = (
        lax.all_gather(inputs, "col", axis=0, tiled=True),
        lax.all_gather(cotangent, "col", axis=0, tiled=True),
    )
    up_part = jnp.dot(inputs_all, up_kept, preferred_element_type=F32)
    back_part = contract(cot_all, down_kept, 1, 1)
    hidden, grad_act = (
        lax.psum_scatter(
            part.astype(BF16), "row", scatter_dimension=0, tiled=True
        ).astype(F32)
        for part in (up_part, back_part)
    )
    act, grad_hidden = activate(hidden, grad_act)
    act_all, grad_all = (
        lax.all_gather(act, "row", axis=0, tiled=True),
        lax.all_gather(grad_hidden, "row", axis=0, tiled=True),
    )
    out_part = jnp.dot(act_all, down_kept, preferred_element_type=F32)
    input_part = contract(grad_all, up_kept, 1, 1)
    outputs, grad_inputs = (
        lax.psum_scatter(
            part.astype(BF16), "col", scatter_dimension=0, tiled=True
        ).astype(F32)
        for part in (out_part, input_part)
    )
    grad_down = apply_mask(contract(act_all, cot_all, 0, 0).astype(BF16), mask_down)
    grad_up = apply_mask(contract(inputs_all, grad_all, 0, 0).astype(BF16), mask_up)
    return (outputs.astype(BF16), grad_inputs.astype(BF16), grad_up, grad_down)


CORE, X, Y = 1, 2, 4


def first_of(row):
    return X if row % 2 == 0 else Y


AT_SENT, AT_HELD, AT_NEAR, AT_FAR = 0, 4, 8, 12
AT_FAR_CORE = 14


def share_table(row):
    first = jnp.where(row % 2 == 0, X, Y)
    second = (X | Y) - first
    other = row ^ CORE
    sent = [other ^ first ^ second, other ^ second, other ^ first, other]
    held = [row ^ first ^ second, row ^ first, row ^ second, row]
    near = [row, row ^ first, other, other ^ second]
    far = [row ^ second, row ^ second ^ first, other ^ first, other ^ first ^ second]
    return jnp.stack(sent + held + near + far)


def small(body, outs, *given):
    specs = tuple(resident() for _ in outs)
    return pl.pallas_call(
        body,
        out_shape=tuple(pltpu.VMEM(shape, dtype) for shape, dtype in outs),
        in_specs=[resident()] * len(given),
        out_specs=specs,
        compiler_params=pltpu.CompilerParams(vmem_limit_bytes=VMEM_LIMIT),
    )(*[in_vmem(array) for array in given])


def add_cores(held, got):
    _, tokens, share = held.shape

    def body(held_ref, got_ref, pair, rest):
        for k in range(4):
            total = held_ref[k].astype(F32) + got_ref[k].astype(F32)
            if k < 2:
                pair[k] = total.astype(BF16)
            else:
                rest[k - 2] = total

    shape = (2, tokens, share)
    return small(body, [(shape, BF16), (shape, F32)], held, got)


def add_first(rest, near):
    _, tokens, share = rest.shape

    def body(rest_ref, near_ref, passed, own):
        passed[...] = (rest_ref[0] + near_ref[0].astype(F32)).astype(BF16)
        own[...] = rest_ref[1] + near_ref[1].astype(F32)

    return small(body, [((tokens, share), BF16), ((tokens, share), F32)], rest, near)


def activated(own, last):
    def body(own_ref, last_ref, hidden, act):
        value = own_ref[...] + last_ref[...].astype(F32)
        hidden[...] = value
        act[...] = smooth_gate(value).astype(BF16)

    return small(body, [(own.shape, F32), (own.shape, BF16)], own, last)


def pulled(hidden, own, last):
    def body(hidden_ref, own_ref, last_ref, grad):
        _, pull = jax.vjp(smooth_gate, hidden_ref[...])
        grad[...] = pull(own_ref[...] + last_ref[...].astype(F32))[0].astype(BF16)

    return small(body, [(own.shape, BF16)], hidden, own, last)[0]


def paired(left, right):
    def body(left_ref, right_ref, pair):
        pair[0] = left_ref[...]
        pair[1] = right_ref[...]

    return small(body, [((2,) + left.shape, BF16)], left, right)[0]


def added(terms):
    def body(*refs):
        *given, out = refs
        out[...] = functools.reduce(jnp.add, [ref[...].astype(F32) for ref in given]).astype(BF16)

    return small(body, [(terms[0].shape, BF16)], *terms)[0]


def cost(flops, moved):
    return pl.CostEstimate(flops=int(flops), bytes_accessed=int(moved), transcendentals=0)


def params():
    return pltpu.CompilerParams(
        dimension_semantics=("arbitrary",), vmem_limit_bytes=VMEM_LIMIT
    )


def whole(array):
    return pl.BlockSpec(array.shape, lambda i, t: (0,) * len(array.shape))


def resident():
    return pl.BlockSpec(memory_space=pltpu.VMEM)


def in_vmem(array):
    return pltpu.with_memory_space_constraint(array, pltpu.VMEM)


def stack(dst, refs):
    row = 0
    for ref in refs:
        dst[row : row + ref.shape[0], :] = ref[...]
        row += ref.shape[0]


def kept_pieces(weight, keep, shares, by_rows):
    rows, columns = weight.shape
    share = (rows if by_rows else columns) // shares
    wide = columns if by_rows else rows
    pieces = range(0, wide, PIECE)
    block = (share, PIECE) if by_rows else (PIECE, share)

    def body(weight_ref, keep_ref, *refs):
        *outs, sems = refs

        def copies(n):
            start = pl.multiple_of(n * share, TILE)
            for h, lo in enumerate(pieces):
                if by_rows:
                    source = weight_ref.at[pl.ds(start, share), pl.ds(lo, PIECE)]
                else:
                    source = weight_ref.at[pl.ds(lo, PIECE), pl.ds(start, share)]
                yield pltpu.make_async_copy(source, outs[h].at[n], sems.at[n, h])

        for n in range(shares):
            for copy in copies(n):
                copy.start()

        @pl.loop(0, shares)
        def _(n):
            for copy in copies(n):
                copy.wait()
            for lo, out in zip(pieces, outs):
                for k in range(0, block[0], TILE):
                    strip = slice(k, k + TILE)
                    if by_rows:
                        kept = keep_ref[n, k // TILE : k // TILE + 1, lo : lo + PIECE]
                    else:
                        tile = (lo + k) // TILE
                        kept = keep_ref[n, tile : tile + 1, :]
                    out[n, strip, :] = out[n, strip, :] * kept

    return pl.pallas_call(
        body,
        out_shape=(pltpu.VMEM((shares,) + block, BF16),) * len(pieces),
        in_specs=[pl.BlockSpec(memory_space=pltpu.HBM), resident()],
        out_specs=(resident(),) * len(pieces),
        scratch_shapes=[pltpu.SemaphoreType.DMA((shares, len(pieces)))],
        compiler_params=pltpu.CompilerParams(vmem_limit_bytes=VMEM_LIMIT),
        cost_estimate=cost(rows * columns, 4 * rows * columns),
    )(pltpu.with_memory_space_constraint(weight, pltpu.HBM), keep)


def share_block(kept_refs, share, by_rows):
    return jnp.concatenate([ref[share] for ref in kept_refs], axis=1 if by_rows else 0)


def project(table, at, parts, kept, by_rows):
    tokens = sum(part.shape[0] for part in parts)
    wide = parts[0].shape[1]
    share = kept[0].shape[1 if by_rows else 2]

    def body(table_ref, *refs):
        part_refs, refs = refs[: len(parts)], refs[len(parts) :]
        *kept_refs, out, held = refs
        i = pl.program_id(0)

        @pl.when(i == 0)
        def _():
            stack(held, part_refs)

        right = share_block(kept_refs, table_ref[at + i], by_rows)
        out[...] = contract(held[...], right, 1, 1 if by_rows else 0).astype(BF16)

    call = pl.pallas_call(
        body,
        out_shape=jax.ShapeDtypeStruct((4, tokens, share), BF16),
        grid_spec=pltpu.PrefetchScalarGridSpec(
            num_scalar_prefetch=1,
            grid=(4,),
            in_specs=[whole(part) for part in parts] + [resident()] * len(kept),
            out_specs=pl.BlockSpec((None, tokens, share), lambda i, t: (i, 0, 0)),
            scratch_shapes=[pltpu.VMEM((tokens, wide), BF16)],
        ),
        compiler_params=params(),
        cost_estimate=cost(
            8 * tokens * wide * share, 2 * (4 * share * (wide + tokens) + tokens * wide)
        ),
    )
    return call(table, *parts, *map(in_vmem, kept))


def fetch(i, pairs, refs, held, sems):
    copies = [
        pltpu.make_async_copy(ref, held.at[pl.ds(2 * n, 2)], sems.at[n])
        for n, ref in enumerate(refs)
    ]

    @pl.when(i == 0)
    def _():
        for copy in copies:
            copy.start()

    for n, copy in enumerate(copies):

        @pl.when(i == 2 * n)
        def _(copy=copy):
            copy.wait()


def gathered(table, at, pairs, kept, by_rows, base=None, blocks=0):
    _, tokens, share = pairs[0].shape
    steps = 2 * len(pairs)
    wide = len(kept) * PIECE
    total_shape = (tokens, wide)
    given = [] if base is None else [base]

    def body(table_ref, *refs):
        pair_refs, refs = refs[: len(pairs)], refs[len(pairs) :]
        kept_refs, refs = refs[: len(kept)], refs[len(kept) :]
        base_refs, refs = refs[: len(given)], refs[len(given) :]
        if blocks:
            *outs, total, held, sems = refs
        else:
            total, held, sems = refs
        i = pl.program_id(0)
        fetch(i, pairs, pair_refs, held, sems)

        @pl.when(i == 0)
        def _():
            total[...] = base_refs[0][...] if given else jnp.zeros(total_shape, F32)

        right = share_block(kept_refs, table_ref[at + i], by_rows)
        total[...] += contract(held[i], right, 1, 0 if by_rows else 1)

        if blocks:

            @pl.when(i == steps - 1)
            def _():
                rows = tokens // blocks
                for k, out in enumerate(outs):
                    out[...] = total[k * rows : (k + 1) * rows, :].astype(BF16)

    scratch = [
        pltpu.VMEM((steps, tokens, share), BF16),
        pltpu.SemaphoreType.DMA((len(pairs),)),
    ]
    if blocks:
        out_shape = (jax.ShapeDtypeStruct((tokens // blocks, wide), BF16),) * blocks
        out_specs = (whole(out_shape[0]),) * blocks
        scratch.insert(0, pltpu.VMEM(total_shape, F32))
    else:
        out_shape = jax.ShapeDtypeStruct(total_shape, F32)
        out_specs = whole(out_shape)
    call = pl.pallas_call(
        body,
        out_shape=out_shape,
        grid_spec=pltpu.PrefetchScalarGridSpec(
            num_scalar_prefetch=1,
            grid=(steps,),
            in_specs=[pl.BlockSpec(memory_space=pl.ANY)] * len(pairs)
            + [resident()] * len(kept)
            + [whole(array) for array in given],
            out_specs=out_specs,
            scratch_shapes=scratch,
        ),
        compiler_params=params(),
        cost_estimate=cost(
            2 * tokens * share * wide * steps,
            2 * share * (wide + tokens) * steps + 4 * tokens * wide,
        ),
    )
    return call(table, *pairs, *map(in_vmem, kept), *given)


def weight_gradient(table, at, pairs, parts, keep, shape, by_rows, into=None):
    tokens = sum(part.shape[0] for part in parts)
    share = pairs[0].shape[2]
    wide = parts[0].shape[1]
    steps = 2 * len(pairs)
    block = (share, wide) if by_rows else (wide, share)
    given = [] if into is None else [into]

    def body(table_ref, *refs):
        pair_refs, refs = refs[: len(pairs)], refs[len(pairs) :]
        part_refs, refs = refs[: len(parts)], refs[len(parts) :]
        keep_ref, *_, out, made, held, other, sems, out_sems = refs
        i = pl.program_id(0)
        slot = i % 2

        def copy(step):
            start = pl.multiple_of(table_ref[at + step] * share, TILE)
            if by_rows:
                target = out.at[pl.ds(start, share)]
            else:
                target = out.at[:, pl.ds(start, share)]
            return pltpu.make_async_copy(made.at[step % 2], target, out_sems.at[step % 2])

        @pl.when(i == 0)
        def _():
            if by_rows:
                stack(other, part_refs)
            else:
                row = 0
                for ref in part_refs:
                    other[:, row : row + ref.shape[0]] = ref[...].T
                    row += ref.shape[0]

        fetch(i, pairs, pair_refs, held, sems)

        @pl.when(i >= 2)
        def _():
            copy(i - 2).wait()

        left = held[i].T if by_rows else other
        right = other[...] if by_rows else held[i]
        span = 2 * TILE
        for lo in range(0, block[0], span):
            term = contract(left[lo : lo + span, :], right, 1, 0)
            for k in range(0, span, TILE):
                tile = (lo + k) // TILE
                made[slot, lo + k : lo + k + TILE, :] = (
                    term[k : k + TILE].astype(BF16) * keep_ref[tile : tile + 1, :]
                )
        copy(i).start()

        @pl.when(i == steps - 1)
        def _():
            copy(i - 1).wait()
            copy(i).wait()

    call = pl.pallas_call(
        body,
        out_shape=jax.ShapeDtypeStruct(shape, BF16),
        grid_spec=pltpu.PrefetchScalarGridSpec(
            num_scalar_prefetch=1,
            grid=(steps,),
            in_specs=[pl.BlockSpec(memory_space=pl.ANY)] * len(pairs)
            + [whole(part) for part in parts]
            + [pl.BlockSpec((None,) + keep.shape[1:], lambda i, t: (t[at + i], 0, 0))]
            + [pl.BlockSpec(memory_space=pl.ANY)] * len(given),
            out_specs=pl.BlockSpec(memory_space=pl.ANY),
            scratch_shapes=[
                pltpu.VMEM((2,) + block, BF16),
                pltpu.VMEM((steps, tokens, share), BF16),
                pltpu.VMEM((tokens, wide) if by_rows else (wide, tokens), BF16),
                pltpu.SemaphoreType.DMA((len(pairs),)),
                pltpu.SemaphoreType.DMA((2,)),
            ],
        ),
        input_output_aliases={2 + len(pairs) + len(parts): 0} if given else {},
        compiler_params=params(),
        cost_estimate=cost(
            2 * tokens * share * wide * steps, 2 * share * (wide + tokens) * steps
        ),
    )
    return call(table, *pairs, *parts, keep, *given)


def per_device_tuned(n_row, n_col, inputs, w_up, w_down, mask_up, mask_down, cotangent):
    share = w_up.shape[1] // n_row
    table = share_table(lax.axis_index("row"))
    keep_up = jnp.repeat(mask_up.astype(BF16), TILE, axis=1)
    keep_up = keep_up.reshape(-1, n_row, share).transpose(1, 0, 2)
    keep_down = jnp.repeat(mask_down.astype(BF16), TILE, axis=1)
    keep_down = keep_down.reshape(n_row, share // TILE, -1)

    def between_cores(value):
        return lax.ppermute(value, "row", [(i, i ^ CORE) for i in range(n_row)])

    def along_first(value):
        return lax.ppermute(value, "row", [(i, i ^ first_of(i)) for i in range(n_row)])

    def along_second(value):
        second = [(X | Y) - first_of(i) for i in range(n_row)]
        return lax.ppermute(value, "row", [(i, i ^ second[i]) for i in range(n_row)])

    def along_col(value, shift):
        return lax.ppermute(value, "col", [(i, (i + shift) % n_col) for i in range(n_col)])

    def after(value, *done):
        return lax.optimization_barrier((value, *done))[0]

    def together(*values):
        return lax.optimization_barrier(values)

    def col_sum(blocks):
        terms = [blocks[0]] + [along_col(blocks[k], -k) for k in range(1, n_col)]
        return added(terms)

    keep_up, keep_down, table = together(keep_up, keep_down, table)
    up = kept_pieces(w_up, keep_up, n_row, False)
    down = kept_pieces(w_down, keep_down, n_row, True)
    inputs_all = [inputs] + [along_col(inputs, k) for k in range(1, n_col)]
    inputs_all[1], up, down = together(inputs_all[1], up, down)
    cot_all = [cotangent]
    for k in range(1, n_col):
        cot_all.append(along_col(after(cotangent, inputs_all[k]), k))

    up_sent = project(table, AT_SENT, inputs_all, up, False)
    up_got = between_cores(up_sent)
    up_held = project(after(table, up_sent), AT_HELD, inputs_all, up, False)
    up_held, *cot_all[1:] = together(up_held, *cot_all[1:])
    pair, rest = add_cores(up_held, up_got)

    back_sent = project(after(table, pair), AT_SENT, cot_all, down, True)
    near, back_sent = together(along_first(pair), back_sent)
    back_got = between_cores(back_sent)
    back_held = project(after(table, back_sent), AT_HELD, cot_all, down, True)
    passed, own = add_first(rest, near)
    last, back_held = together(along_second(passed), back_held)
    hidden, act = activated(own, last)

    pair, rest = add_cores(back_held, back_got)
    near = along_first(pair)
    act_near = paired(act, along_first(act))
    passed, own = add_first(rest, near)
    last = along_second(passed)
    act_far = along_second(act_near)
    act_core = between_cores(act_near)
    grad = pulled(hidden, own, last)

    out_total = gathered(table, AT_NEAR, [act_near, act_core], down, True)
    act_far, out_total = together(act_far, out_total)
    act_far_core = between_cores(act_far)
    grad_near = paired(grad, along_first(grad))
    out_blocks = gathered(
        table, AT_FAR, [act_far, act_far_core], down, True, out_total, n_col
    )
    outputs = col_sum(out_blocks)

    grad_far = along_second(grad_near)
    grad_core = between_cores(grad_near)
    in_total = gathered(table, AT_NEAR, [grad_near, grad_core], up, False)
    grad_down = weight_gradient(
        table, AT_NEAR, [act_near, act_core], cot_all, keep_down, w_down.shape, True
    )
    grad_far, in_total, grad_down = together(grad_far, in_total, grad_down)
    grad_far_core = between_cores(grad_far)
    in_total = gathered(table, AT_FAR, [grad_far], up, False, in_total)
    in_blocks = gathered(table, AT_FAR_CORE, [grad_far_core], up, False, in_total, n_col)
    grad_inputs = col_sum(in_blocks)

    table = after(table, in_blocks[1])
    grad_up = weight_gradient(
        table,
        AT_NEAR,
        [grad_near, grad_core, grad_far, grad_far_core],
        inputs_all,
        keep_up,
        w_up.shape,
        False,
    )
    grad_down = weight_gradient(
        table,
        AT_FAR,
        [act_far, act_far_core],
        cot_all,
        keep_down,
        w_down.shape,
        True,
        grad_down,
    )
    return (outputs, grad_inputs, grad_up, grad_down)


def solution(mesh):
    in_specs = (
        P("col", "row"),
        P("row", "col"),
        P("col", "row"),
        P("row", "col"),
        P("col", "row"),
        P("col", "row"),
    )
    out_specs = (P("col", "row"), P("col", "row"), P("row", "col"), P("col", "row"))
    n_row, n_col = mesh.shape["row"], mesh.shape["col"]

    def per_device(inputs, w_up, w_down, mask_up, mask_down, cotangent):
        fits = n_row == 8 and mask_up.shape[1] % n_row == 0 and w_up.shape[0] % PIECE == 0
        plan = functools.partial(per_device_tuned, n_row, n_col) if fits else per_device_plain
        return plan(inputs, w_up, w_down, mask_up, mask_down, cotangent)

    return jax.shard_map(
        per_device, mesh=mesh, in_specs=in_specs, out_specs=out_specs, check_vma=False
    )
```

```python
import functools

import jax
import jax.numpy as jnp
from jax import lax
from jax.experimental import pallas as pl
from jax.experimental.pallas import tpu as pltpu
from jax.sharding import PartitionSpec as P

TILE = 128
VMEM_LIMIT = 14 << 20
PIECE = 768
F32 = jnp.float32
BF16 = jnp.bfloat16


def smooth_gate(value):
    return jax.nn.gelu(value, approximate=True)


def contract(left, right, left_dim, right_dim):
    return lax.dot_general(
        left, right, (((left_dim,), (right_dim,)), ((), ())), preferred_element_type=F32
    )


def apply_mask(weight, mask):
    rows, cols = mask.shape
    tile = weight.shape[0] // rows
    shaped = weight.reshape(rows, tile, cols, tile)
    keep = mask[:, None, :, None].astype(weight.dtype)
    return (shaped * keep).reshape(weight.shape)


def activate(hidden, grad_act):
    act = smooth_gate(hidden).astype(BF16)
    _, pull = jax.vjp(smooth_gate, hidden)
    grad_hidden = pull(grad_act)[0].astype(BF16)
    return (act, grad_hidden)


def per_device_plain(inputs, w_up, w_down, mask_up, mask_down, cotangent):
    up_kept = apply_mask(w_up, mask_up)
    down_kept = apply_mask(w_down, mask_down)
    inputs_all, cot_all = (
        lax.all_gather(inputs, "col", axis=0, tiled=True),
        lax.all_gather(cotangent, "col", axis=0, tiled=True),
    )
    up_part = jnp.dot(inputs_all, up_kept, preferred_element_type=F32)
    back_part = contract(cot_all, down_kept, 1, 1)
    hidden, grad_act = (
        lax.psum_scatter(
            part.astype(BF16), "row", scatter_dimension=0, tiled=True
        ).astype(F32)
        for part in (up_part, back_part)
    )
    act, grad_hidden = activate(hidden, grad_act)
    act_all, grad_all = (
        lax.all_gather(act, "row", axis=0, tiled=True),
        lax.all_gather(grad_hidden, "row", axis=0, tiled=True),
    )
    out_part = jnp.dot(act_all, down_kept, preferred_element_type=F32)
    input_part = contract(grad_all, up_kept, 1, 1)
    outputs, grad_inputs = (
        lax.psum_scatter(
            part.astype(BF16), "col", scatter_dimension=0, tiled=True
        ).astype(F32)
        for part in (out_part, input_part)
    )
    grad_down = apply_mask(contract(act_all, cot_all, 0, 0).astype(BF16), mask_down)
    grad_up = apply_mask(contract(inputs_all, grad_all, 0, 0).astype(BF16), mask_up)
    return (outputs.astype(BF16), grad_inputs.astype(BF16), grad_up, grad_down)


CORE, X, Y = 1, 2, 4


def first_of(row):
    return X if row % 2 == 0 else Y


AT_SENT, AT_HELD, AT_NEAR, AT_FAR = 0, 4, 8, 12
AT_FAR_CORE = 14


def share_table(row):
    first = jnp.where(row % 2 == 0, X, Y)
    second = (X | Y) - first
    other = row ^ CORE
    sent = [other ^ first ^ second, other ^ second, other ^ first, other]
    held = [row ^ first ^ second, row ^ first, row ^ second, row]
    near = [row, row ^ first, other, other ^ second]
    far = [row ^ second, row ^ second ^ first, other ^ first, other ^ first ^ second]
    return jnp.stack(sent + held + near + far)


def cost(flops, moved):
    return pl.CostEstimate(flops=int(flops), bytes_accessed=int(moved), transcendentals=0)


def params():
    return pltpu.CompilerParams(
        dimension_semantics=("arbitrary",), vmem_limit_bytes=VMEM_LIMIT
    )


def whole(array):
    return pl.BlockSpec(array.shape, lambda i, t: (0,) * len(array.shape))


def resident():
    return pl.BlockSpec(memory_space=pltpu.VMEM)


def in_vmem(array):
    return pltpu.with_memory_space_constraint(array, pltpu.VMEM)


def flat(parts):
    return [array for part in parts for array in part]


def parts_of(refs, parts):
    refs = iter(refs)
    return [functools.reduce(jnp.add, [next(refs)[...] for _ in part]) for part in parts]


def stack(dst, values):
    row = 0
    for value in values:
        dst[row : row + value.shape[0], :] = value
        row += value.shape[0]


def small(body, outs, *given):
    specs = tuple(resident() for _ in outs)
    return pl.pallas_call(
        body,
        out_shape=tuple(pltpu.VMEM(shape, dtype) for shape, dtype in outs),
        in_specs=[resident()] * len(given),
        out_specs=specs,
        compiler_params=pltpu.CompilerParams(vmem_limit_bytes=VMEM_LIMIT),
    )(*[in_vmem(array) for array in given])


def add_cores(held, got):
    _, tokens, share = held.shape

    def body(held_ref, got_ref, pair, rest):
        for k in range(4):
            total = held_ref[k].astype(F32) + got_ref[k].astype(F32)
            if k < 2:
                pair[k] = total.astype(BF16)
            else:
                rest[k - 2] = total

    shape = (2, tokens, share)
    return small(body, [(shape, BF16), (shape, F32)], held, got)


def add_first(rest, near):
    _, tokens, share = rest.shape

    def body(rest_ref, near_ref, passed, own):
        passed[...] = (rest_ref[0] + near_ref[0].astype(F32)).astype(BF16)
        own[...] = rest_ref[1] + near_ref[1].astype(F32)

    return small(body, [((tokens, share), BF16), ((tokens, share), F32)], rest, near)


def activated(own, last):
    def body(own_ref, last_ref, hidden, act):
        value = own_ref[...] + last_ref[...].astype(F32)
        hidden[...] = value
        act[...] = smooth_gate(value).astype(BF16)

    return small(body, [(own.shape, F32), (own.shape, BF16)], own, last)


def pulled(hidden, own, last):
    def body(hidden_ref, own_ref, last_ref, grad):
        _, pull = jax.vjp(smooth_gate, hidden_ref[...])
        grad[...] = pull(own_ref[...] + last_ref[...].astype(F32))[0].astype(BF16)

    return small(body, [(own.shape, BF16)], hidden, own, last)[0]


def paired(left, right):
    def body(left_ref, right_ref, pair):
        pair[0] = left_ref[...]
        pair[1] = right_ref[...]

    return small(body, [((2,) + left.shape, BF16)], left, right)[0]


def added_pairs(*pairs):
    def body(*refs):
        given, outs = refs[: 2 * len(pairs)], refs[2 * len(pairs) :]
        for n, out in enumerate(outs):
            left, right = given[2 * n : 2 * n + 2]
            out[...] = (left[...].astype(F32) + right[...].astype(F32)).astype(BF16)

    return small(body, [(left.shape, BF16) for left, _ in pairs], *flat(pairs))


def added(terms):
    def body(*refs):
        *given, out = refs
        out[...] = functools.reduce(jnp.add, [ref[...].astype(F32) for ref in given]).astype(BF16)

    return pl.pallas_call(
        body,
        out_shape=jax.ShapeDtypeStruct(terms[0].shape, BF16),
        compiler_params=pltpu.CompilerParams(vmem_limit_bytes=VMEM_LIMIT),
    )(*terms)


def kept_pieces(weight, keep, shares, by_rows):
    rows, columns = weight.shape
    share = (rows if by_rows else columns) // shares
    wide = columns if by_rows else rows
    pieces = range(0, wide, PIECE)
    block = (share, PIECE) if by_rows else (PIECE, share)

    def body(weight_ref, keep_ref, *refs):
        *outs, sems = refs

        def copies(n):
            start = pl.multiple_of(n * share, TILE)
            for h, lo in enumerate(pieces):
                if by_rows:
                    source = weight_ref.at[pl.ds(start, share), pl.ds(lo, PIECE)]
                else:
                    source = weight_ref.at[pl.ds(lo, PIECE), pl.ds(start, share)]
                yield pltpu.make_async_copy(source, outs[h].at[n], sems.at[n, h])

        for n in range(shares):
            for copy in copies(n):
                copy.start()

        @pl.loop(0, shares)
        def _(n):
            for copy in copies(n):
                copy.wait()
            for lo, out in zip(pieces, outs):
                for k in range(0, block[0], TILE):
                    strip = slice(k, k + TILE)
                    if by_rows:
                        kept = keep_ref[n, k // TILE : k // TILE + 1, lo : lo + PIECE]
                    else:
                        tile = (lo + k) // TILE
                        kept = keep_ref[n, tile : tile + 1, :]
                    out[n, strip, :] = out[n, strip, :] * kept

    return pl.pallas_call(
        body,
        out_shape=(pltpu.VMEM((shares,) + block, BF16),) * len(pieces),
        in_specs=[pl.BlockSpec(memory_space=pltpu.HBM), resident()],
        out_specs=(resident(),) * len(pieces),
        scratch_shapes=[pltpu.SemaphoreType.DMA((shares, len(pieces)))],
        compiler_params=pltpu.CompilerParams(vmem_limit_bytes=VMEM_LIMIT),
        cost_estimate=cost(rows * columns, 4 * rows * columns),
    )(pltpu.with_memory_space_constraint(weight, pltpu.HBM), keep)


def share_block(kept_refs, share, by_rows):
    return jnp.concatenate([ref[share] for ref in kept_refs], axis=1 if by_rows else 0)


def project(table, ats, parts, kept, by_rows):
    tokens = sum(part[0].shape[0] for part in parts)
    wide = parts[0][0].shape[1]
    share = kept[0].shape[1 if by_rows else 2]
    count = len(flat(parts))

    def body(table_ref, *refs):
        part_refs, refs = refs[:count], refs[count:]
        kept_refs, (*outs, held) = refs[: len(kept)], refs[len(kept) :]
        i = pl.program_id(0)

        @pl.when(i == 0)
        def _():
            stack(held, parts_of(part_refs, parts))

        right = share_block(kept_refs, table_ref[ats[0] + i], by_rows)
        result = contract(held[...], right, 1, 1 if by_rows else 0).astype(BF16)
        for n, out in enumerate(outs):

            @pl.when(i // 4 == n)
            def _(out=out):
                out[...] = result

    def place(n):
        return lambda i, t: (jnp.clip(i - 4 * n, 0, 3), 0, 0)

    call = pl.pallas_call(
        body,
        out_shape=(jax.ShapeDtypeStruct((4, tokens, share), BF16),) * len(ats),
        grid_spec=pltpu.PrefetchScalarGridSpec(
            num_scalar_prefetch=1,
            grid=(4 * len(ats),),
            in_specs=[whole(array) for array in flat(parts)] + [resident()] * len(kept),
            out_specs=tuple(
                pl.BlockSpec((None, tokens, share), place(n)) for n in range(len(ats))
            ),
            scratch_shapes=[pltpu.VMEM((tokens, wide), BF16)],
        ),
        compiler_params=params(),
        cost_estimate=cost(
            8 * tokens * wide * share * len(ats),
            2 * (4 * len(ats) * share * (wide + tokens) + tokens * wide),
        ),
    )
    return call(table, *flat(parts), *map(in_vmem, kept))


def fetch(i, pairs, refs, held, sems):
    copies = [
        pltpu.make_async_copy(ref, held.at[pl.ds(2 * n, 2)], sems.at[n])
        for n, ref in enumerate(refs)
    ]

    @pl.when(i == 0)
    def _():
        for copy in copies:
            copy.start()

    for n, copy in enumerate(copies):

        @pl.when(i == 2 * n)
        def _(copy=copy):
            copy.wait()


def gathered(table, at, pairs, kept, by_rows, base=None, blocks=0):
    _, tokens, share = pairs[0].shape
    steps = 2 * len(pairs)
    wide = len(kept) * PIECE
    total_shape = (tokens, wide)
    given = [] if base is None else [base]

    def body(table_ref, *refs):
        pair_refs, refs = refs[: len(pairs)], refs[len(pairs) :]
        kept_refs, refs = refs[: len(kept)], refs[len(kept) :]
        base_refs, refs = refs[: len(given)], refs[len(given) :]
        if blocks:
            *outs, total, held, sems = refs
        else:
            total, held, sems = refs
        i = pl.program_id(0)
        fetch(i, pairs, pair_refs, held, sems)

        @pl.when(i == 0)
        def _():
            total[...] = base_refs[0][...] if given else jnp.zeros(total_shape, F32)

        right = share_block(kept_refs, table_ref[at + i], by_rows)
        total[...] += contract(held[i], right, 1, 0 if by_rows else 1)

        if blocks:

            @pl.when(i == steps - 1)
            def _():
                rows = tokens // blocks
                for k, out in enumerate(outs):
                    out[...] = total[k * rows : (k + 1) * rows, :].astype(BF16)

    scratch = [
        pltpu.VMEM((steps, tokens, share), BF16),
        pltpu.SemaphoreType.DMA((len(pairs),)),
    ]
    if blocks:
        out_shape = (jax.ShapeDtypeStruct((tokens // blocks, wide), BF16),) * blocks
        out_specs = (whole(out_shape[0]),) * blocks
        scratch.insert(0, pltpu.VMEM(total_shape, F32))
    else:
        out_shape = jax.ShapeDtypeStruct(total_shape, F32)
        out_specs = whole(out_shape)
    call = pl.pallas_call(
        body,
        out_shape=out_shape,
        grid_spec=pltpu.PrefetchScalarGridSpec(
            num_scalar_prefetch=1,
            grid=(steps,),
            in_specs=[pl.BlockSpec(memory_space=pl.ANY)] * len(pairs)
            + [resident()] * len(kept)
            + [whole(array) for array in given],
            out_specs=out_specs,
            scratch_shapes=scratch,
        ),
        compiler_params=params(),
        cost_estimate=cost(
            2 * tokens * share * wide * steps,
            2 * share * (wide + tokens) * steps + 4 * tokens * wide,
        ),
    )
    return call(table, *pairs, *map(in_vmem, kept), *given)


def weight_gradient(table, at, pairs, parts, keep, shape, by_rows, into=None):
    tokens = sum(part[0].shape[0] for part in parts)
    share = pairs[0].shape[2]
    wide = parts[0][0].shape[1]
    count = len(flat(parts))
    steps = 2 * len(pairs)
    block = (share, wide) if by_rows else (wide, share)
    given = [] if into is None else [into]

    def body(table_ref, *refs):
        pair_refs, refs = refs[: len(pairs)], refs[len(pairs) :]
        part_refs, refs = refs[:count], refs[count:]
        keep_ref, *_, out, made, held, other, sems, out_sems = refs
        i = pl.program_id(0)
        slot = i % 2

        def copy(step):
            start = pl.multiple_of(table_ref[at + step] * share, TILE)
            if by_rows:
                target = out.at[pl.ds(start, share)]
            else:
                target = out.at[:, pl.ds(start, share)]
            return pltpu.make_async_copy(made.at[step % 2], target, out_sems.at[step % 2])

        @pl.when(i == 0)
        def _():
            values = parts_of(part_refs, parts)
            if by_rows:
                stack(other, values)
            else:
                other[...] = jnp.concatenate(values).T

        fetch(i, pairs, pair_refs, held, sems)

        @pl.when(i >= 2)
        def _():
            copy(i - 2).wait()

        left = held[i].T if by_rows else other
        right = other[...] if by_rows else held[i]
        span = 2 * TILE
        for lo in range(0, block[0], span):
            term = contract(left[lo : lo + span, :], right, 1, 0)
            for k in range(0, span, TILE):
                tile = (lo + k) // TILE
                made[slot, lo + k : lo + k + TILE, :] = (
                    term[k : k + TILE].astype(BF16) * keep_ref[tile : tile + 1, :]
                )
        copy(i).start()

        @pl.when(i == steps - 1)
        def _():
            copy(i - 1).wait()
            copy(i).wait()

    call = pl.pallas_call(
        body,
        out_shape=jax.ShapeDtypeStruct(shape, BF16),
        grid_spec=pltpu.PrefetchScalarGridSpec(
            num_scalar_prefetch=1,
            grid=(steps,),
            in_specs=[pl.BlockSpec(memory_space=pl.ANY)] * len(pairs)
            + [whole(array) for array in flat(parts)]
            + [pl.BlockSpec((None,) + keep.shape[1:], lambda i, t: (t[at + i], 0, 0))]
            + [pl.BlockSpec(memory_space=pl.ANY)] * len(given),
            out_specs=pl.BlockSpec(memory_space=pl.ANY),
            scratch_shapes=[
                pltpu.VMEM((2,) + block, BF16),
                pltpu.VMEM((steps, tokens, share), BF16),
                pltpu.VMEM((tokens, wide) if by_rows else (wide, tokens), BF16),
                pltpu.SemaphoreType.DMA((len(pairs),)),
                pltpu.SemaphoreType.DMA((2,)),
            ],
        ),
        input_output_aliases={2 + len(pairs) + count: 0} if given else {},
        compiler_params=params(),
        cost_estimate=cost(
            2 * tokens * share * wide * steps, 2 * share * (wide + tokens) * steps
        ),
    )
    return call(table, *pairs, *flat(parts), keep, *given)


def per_device_tuned(n_row, n_col, inputs, w_up, w_down, mask_up, mask_down, cotangent):
    share = w_up.shape[1] // n_row
    table = share_table(lax.axis_index("row"))
    keep_up = jnp.repeat(mask_up.astype(BF16), TILE, axis=1)
    keep_up = keep_up.reshape(-1, n_row, share).transpose(1, 0, 2)
    keep_down = jnp.repeat(mask_down.astype(BF16), TILE, axis=1)
    keep_down = keep_down.reshape(n_row, share // TILE, -1)

    def between_cores(value):
        return lax.ppermute(value, "row", [(i, i ^ CORE) for i in range(n_row)])

    def along_first(value):
        return lax.ppermute(value, "row", [(i, i ^ first_of(i)) for i in range(n_row)])

    def along_second(value):
        second = [(X | Y) - first_of(i) for i in range(n_row)]
        return lax.ppermute(value, "row", [(i, i ^ second[i]) for i in range(n_row)])

    def along_col(value, shift):
        return lax.ppermute(value, "col", [(i, (i + shift) % n_col) for i in range(n_col)])

    def toward(value, step, froms):
        return lax.ppermute(value, "col", [(i, i + step) for i in froms])

    def relayed(lower, upper):
        return toward(upper, -1, (1, 2)), toward(lower, 1, (1, 2))

    def after(value, *done):
        return lax.optimization_barrier((value, *done))[0]

    def together(*values):
        return lax.optimization_barrier(values)

    def col_first(blocks):
        return toward(blocks[2], 1, (0, 1)), toward(blocks[2], -1, (2, 3))

    def col_second(blocks, from_lower, from_upper):
        to_upper, to_lower = added_pairs((blocks[3], from_lower), (blocks[1], from_upper))
        return along_col(to_upper, 1), along_col(to_lower, -1)

    keep_up, keep_down, table = together(keep_up, keep_down, table)
    lower, upper = along_col(inputs, 1), along_col(inputs, -1)
    up = kept_pieces(w_up, keep_up, n_row, False)
    lower, upper, *up = together(lower, upper, *up)
    inputs_far = relayed(lower, upper)
    down = kept_pieces(w_down, after(keep_down, lower), n_row, True)
    far_lower, far_upper, *down = together(*inputs_far, *down)
    inputs_far = (far_lower, far_upper)
    inputs_all = [(inputs,), (lower,), inputs_far, (upper,)]

    own = after(cotangent, *inputs_far)
    lower, upper = along_col(own, 1), along_col(own, -1)
    up_sent, up_held = project(
        after(table, down[0]), (AT_SENT, AT_HELD), inputs_all, up, False
    )
    lower, upper, up_sent, up_held = together(lower, upper, up_sent, up_held)
    cot_all = [(cotangent,), (lower,), relayed(lower, upper), (upper,)]
    pair, rest = add_cores(up_held, between_cores(up_sent))

    back_sent = project(after(table, pair), (AT_SENT,), cot_all, down, True)[0]
    near, back_sent = together(along_first(pair), back_sent)
    back_got = between_cores(back_sent)
    back_held = project(after(table, back_sent), (AT_HELD,), cot_all, down, True)[0]
    passed, own = add_first(rest, near)
    last, back_held = together(along_second(passed), back_held)
    hidden, act = activated(own, last)

    act_first = along_first(act)
    pair, rest = add_cores(after(back_held, act), back_got)
    near, act_first = together(along_first(pair), act_first)
    act_near = paired(act, act_first)
    act_far = along_second(act_near)
    act_core = between_cores(act_near)
    passed, own = add_first(rest, near)
    out_total = gathered(table, AT_NEAR, [act_near, act_core], down, True)
    last, out_total = together(along_second(passed), out_total)
    grad = pulled(hidden, own, last)

    grad_down = weight_gradient(
        after(table, grad),
        AT_NEAR,
        [act_near, act_core],
        cot_all,
        keep_down,
        w_down.shape,
        True,
    )
    grad_first, act_far, grad_down = together(along_first(grad), act_far, grad_down)
    act_far_core = between_cores(act_far)
    grad_near = paired(grad, grad_first)
    grad_far = along_second(grad_near)
    grad_core = between_cores(grad_near)
    out_blocks = gathered(
        table, AT_FAR, [act_far, act_far_core], down, True, out_total, n_col
    )
    in_total = gathered(
        after(table, out_blocks[0]), AT_NEAR, [grad_near, grad_core], up, False
    )
    out_got = col_first(out_blocks)
    *out_got, grad_far, in_total = together(*out_got, grad_far, in_total)
    out_last = col_second(out_blocks, *out_got)
    grad_far_core = between_cores(grad_far)
    in_total = gathered(table, AT_FAR, [grad_far], up, False, in_total)
    in_blocks = gathered(table, AT_FAR_CORE, [grad_far_core], up, False, in_total, n_col)

    grad_down = weight_gradient(
        after(table, in_blocks[2]),
        AT_FAR,
        [act_far, act_far_core],
        cot_all,
        keep_down,
        w_down.shape,
        True,
        grad_down,
    )
    *out_last, in_far = together(*out_last, in_blocks[2])
    in_blocks = [in_blocks[0], in_blocks[1], in_far, in_blocks[3]]
    *in_got, grad_down = together(*col_first(in_blocks), grad_down)
    in_last = col_second(in_blocks, *in_got)
    grad_up = weight_gradient(
        after(table, grad_down),
        AT_NEAR,
        [grad_near, grad_core, grad_far, grad_far_core],
        inputs_all,
        keep_up,
        w_up.shape,
        False,
    )
    *in_last, grad_up = together(*in_last, grad_up)
    outputs = added([out_blocks[0], *out_last])
    grad_inputs = added([in_blocks[0], *in_last])
    return (outputs, grad_inputs, grad_up, grad_down)


def solution(mesh):
    in_specs = (
        P("col", "row"),
        P("row", "col"),
        P("col", "row"),
        P("row", "col"),
        P("col", "row"),
        P("col", "row"),
    )
    out_specs = (P("col", "row"), P("col", "row"), P("row", "col"), P("col", "row"))
    n_row, n_col = mesh.shape["row"], mesh.shape["col"]

    def per_device(inputs, w_up, w_down, mask_up, mask_down, cotangent):
        fits = n_row == 8 and n_col == 4 and mask_up.shape[1] % n_row == 0 and w_up.shape[0] % PIECE == 0
        plan = functools.partial(per_device_tuned, n_row, n_col) if fits else per_device_plain
        return plan(inputs, w_up, w_down, mask_up, mask_down, cotangent)

    return jax.shard_map(
        per_device, mesh=mesh, in_specs=in_specs, out_specs=out_specs, check_vma=False
    )
```

```python
import functools

import jax
import jax.numpy as jnp
from jax import lax
from jax.experimental import pallas as pl
from jax.experimental.pallas import tpu as pltpu
from jax.sharding import PartitionSpec as P

TILE = 128
VMEM_LIMIT = 12 << 20
PIECE = 256
F32 = jnp.float32
BF16 = jnp.bfloat16


def smooth_gate(value):
    return jax.nn.gelu(value, approximate=True)


def contract(left, right, left_dim, right_dim):
    return lax.dot_general(
        left, right, (((left_dim,), (right_dim,)), ((), ())), preferred_element_type=F32
    )


def apply_mask(weight, mask):
    rows, cols = mask.shape
    tile = weight.shape[0] // rows
    shaped = weight.reshape(rows, tile, cols, tile)
    keep = mask[:, None, :, None].astype(weight.dtype)
    return (shaped * keep).reshape(weight.shape)


def activate(hidden, grad_act):
    act = smooth_gate(hidden).astype(BF16)
    _, pull = jax.vjp(smooth_gate, hidden)
    grad_hidden = pull(grad_act)[0].astype(BF16)
    return (act, grad_hidden)


def per_device_plain(inputs, w_up, w_down, mask_up, mask_down, cotangent):
    up_kept = apply_mask(w_up, mask_up)
    down_kept = apply_mask(w_down, mask_down)
    inputs_all, cot_all = (
        lax.all_gather(inputs, "col", axis=0, tiled=True),
        lax.all_gather(cotangent, "col", axis=0, tiled=True),
    )
    up_part = jnp.dot(inputs_all, up_kept, preferred_element_type=F32)
    back_part = contract(cot_all, down_kept, 1, 1)
    hidden, grad_act = (
        lax.psum_scatter(
            part.astype(BF16), "row", scatter_dimension=0, tiled=True
        ).astype(F32)
        for part in (up_part, back_part)
    )
    act, grad_hidden = activate(hidden, grad_act)
    act_all, grad_all = (
        lax.all_gather(act, "row", axis=0, tiled=True),
        lax.all_gather(grad_hidden, "row", axis=0, tiled=True),
    )
    out_part = jnp.dot(act_all, down_kept, preferred_element_type=F32)
    input_part = contract(grad_all, up_kept, 1, 1)
    outputs, grad_inputs = (
        lax.psum_scatter(
            part.astype(BF16), "col", scatter_dimension=0, tiled=True
        ).astype(F32)
        for part in (out_part, input_part)
    )
    grad_down = apply_mask(contract(act_all, cot_all, 0, 0).astype(BF16), mask_down)
    grad_up = apply_mask(contract(inputs_all, grad_all, 0, 0).astype(BF16), mask_up)
    return (outputs.astype(BF16), grad_inputs.astype(BF16), grad_up, grad_down)


CORE, X, Y = 1, 2, 4


def first_of(row):
    return X if row % 2 == 0 else Y


AT_SENT, AT_HELD, AT_NEAR, AT_FAR = 0, 4, 8, 12
AT_NEAR_CORE, AT_FAR_CORE = 10, 14


def share_table(row):
    first = jnp.where(row % 2 == 0, X, Y)
    second = (X | Y) - first
    other = row ^ CORE
    sent = [other ^ first ^ second, other ^ second, other ^ first, other]
    held = [row ^ first ^ second, row ^ first, row ^ second, row]
    near = [row, row ^ first, other, other ^ second]
    far = [row ^ second, row ^ second ^ first, other ^ first, other ^ first ^ second]
    return jnp.stack(sent + held + near + far)


def cost(flops, moved):
    return pl.CostEstimate(flops=int(flops), bytes_accessed=int(moved), transcendentals=0)


def params():
    return pltpu.CompilerParams(
        dimension_semantics=("arbitrary",), vmem_limit_bytes=VMEM_LIMIT
    )


def whole(array):
    return pl.BlockSpec(array.shape, lambda i, t: (0,) * len(array.shape))


def resident():
    return pl.BlockSpec(memory_space=pltpu.VMEM)


def in_vmem(array):
    return pltpu.with_memory_space_constraint(array, pltpu.VMEM)


def flat(parts):
    return [array for part in parts for array in part]


def parts_of(refs, parts):
    refs = iter(refs)
    return [functools.reduce(jnp.add, [next(refs)[...] for _ in part]) for part in parts]


def stack(dst, values):
    row = 0
    for value in values:
        dst[row : row + value.shape[0], :] = value
        row += value.shape[0]


def small(body, outs, *given):
    specs = tuple(resident() for _ in outs)
    return pl.pallas_call(
        body,
        out_shape=tuple(pltpu.VMEM(shape, dtype) for shape, dtype in outs),
        in_specs=[resident()] * len(given),
        out_specs=specs,
        compiler_params=pltpu.CompilerParams(vmem_limit_bytes=VMEM_LIMIT),
    )(*[in_vmem(array) for array in given])


def add_cores(held, got):
    _, tokens, share = held.shape

    def body(held_ref, got_ref, pair, rest):
        for k in range(4):
            total = held_ref[k].astype(F32) + got_ref[k].astype(F32)
            if k < 2:
                pair[k] = total.astype(BF16)
            else:
                rest[k - 2] = total

    shape = (2, tokens, share)
    return small(body, [(shape, BF16), (shape, F32)], held, got)


def add_first(rest, near):
    _, tokens, share = rest.shape

    def body(rest_ref, near_ref, passed, own):
        passed[...] = (rest_ref[0] + near_ref[0].astype(F32)).astype(BF16)
        own[...] = rest_ref[1] + near_ref[1].astype(F32)

    return small(body, [((tokens, share), BF16), ((tokens, share), F32)], rest, near)


def activated(own, last):
    def body(own_ref, last_ref, hidden, act):
        value = own_ref[...] + last_ref[...].astype(F32)
        hidden[...] = value
        act[...] = smooth_gate(value).astype(BF16)

    return small(body, [(own.shape, F32), (own.shape, BF16)], own, last)


def pulled(hidden, own, last):
    def body(hidden_ref, own_ref, last_ref, grad):
        _, pull = jax.vjp(smooth_gate, hidden_ref[...])
        grad[...] = pull(own_ref[...] + last_ref[...].astype(F32))[0].astype(BF16)

    return small(body, [(own.shape, BF16)], hidden, own, last)[0]


def paired(left, right):
    def body(left_ref, right_ref, pair):
        pair[0] = left_ref[...]
        pair[1] = right_ref[...]

    return small(body, [((2,) + left.shape, BF16)], left, right)[0]


def added_pairs(*pairs):
    def body(*refs):
        given, outs = refs[: 2 * len(pairs)], refs[2 * len(pairs) :]
        for n, out in enumerate(outs):
            left, right = given[2 * n : 2 * n + 2]
            out[...] = (left[...].astype(F32) + right[...].astype(F32)).astype(BF16)

    return small(body, [(left.shape, BF16) for left, _ in pairs], *flat(pairs))


def added(terms):
    def body(*refs):
        *given, out = refs
        out[...] = functools.reduce(jnp.add, [ref[...].astype(F32) for ref in given]).astype(BF16)

    return pl.pallas_call(
        body,
        out_shape=jax.ShapeDtypeStruct(terms[0].shape, BF16),
        compiler_params=pltpu.CompilerParams(vmem_limit_bytes=VMEM_LIMIT),
    )(*terms)


def kept_pieces(weight, keep, shares, by_rows, pieces):
    rows, columns = weight.shape
    share = (rows if by_rows else columns) // shares
    block = (share, PIECE) if by_rows else (PIECE, share)

    def body(weight_ref, keep_ref, *refs):
        *outs, sems = refs

        def copies(n):
            start = pl.multiple_of(n * share, TILE)
            for h, lo in enumerate(pieces):
                if by_rows:
                    source = weight_ref.at[pl.ds(start, share), pl.ds(lo, PIECE)]
                else:
                    source = weight_ref.at[pl.ds(lo, PIECE), pl.ds(start, share)]
                yield pltpu.make_async_copy(source, outs[h].at[n], sems.at[n, h])

        for n in range(shares):
            for copy in copies(n):
                copy.start()

        @pl.loop(0, shares)
        def _(n):
            for copy in copies(n):
                copy.wait()
            for lo, out in zip(pieces, outs):
                for k in range(0, block[0], TILE):
                    strip = slice(k, k + TILE)
                    if by_rows:
                        kept = keep_ref[n, k // TILE : k // TILE + 1, lo : lo + PIECE]
                    else:
                        tile = (lo + k) // TILE
                        kept = keep_ref[n, tile : tile + 1, :]
                    out[n, strip, :] = out[n, strip, :] * kept

    return pl.pallas_call(
        body,
        out_shape=(pltpu.VMEM((shares,) + block, BF16),) * len(pieces),
        in_specs=[pl.BlockSpec(memory_space=pltpu.HBM), resident()],
        out_specs=(resident(),) * len(pieces),
        scratch_shapes=[pltpu.SemaphoreType.DMA((shares, len(pieces)))],
        compiler_params=pltpu.CompilerParams(vmem_limit_bytes=VMEM_LIMIT),
        cost_estimate=cost(rows * columns, 4 * rows * columns),
    )(pltpu.with_memory_space_constraint(weight, pltpu.HBM), keep)


def share_block(kept_refs, share, by_rows):
    return jnp.concatenate([ref[share] for ref in kept_refs], axis=1 if by_rows else 0)


def project(table, ats, parts, kept, by_rows):
    tokens = sum(part[0].shape[0] for part in parts)
    wide = parts[0][0].shape[1]
    share = kept[0].shape[1 if by_rows else 2]
    count = len(flat(parts))

    def body(table_ref, *refs):
        part_refs, refs = refs[:count], refs[count:]
        kept_refs, (*outs, held) = refs[: len(kept)], refs[len(kept) :]
        i = pl.program_id(0)

        @pl.when(i == 0)
        def _():
            stack(held, parts_of(part_refs, parts))

        right = share_block(kept_refs, table_ref[ats[0] + i], by_rows)
        result = contract(held[...], right, 1, 1 if by_rows else 0).astype(BF16)
        for n, out in enumerate(outs):

            @pl.when(i // 4 == n)
            def _(out=out):
                out[...] = result

    def place(n):
        return lambda i, t: (jnp.clip(i - 4 * n, 0, 3), 0, 0)

    call = pl.pallas_call(
        body,
        out_shape=(jax.ShapeDtypeStruct((4, tokens, share), BF16),) * len(ats),
        grid_spec=pltpu.PrefetchScalarGridSpec(
            num_scalar_prefetch=1,
            grid=(4 * len(ats),),
            in_specs=[whole(array) for array in flat(parts)] + [resident()] * len(kept),
            out_specs=tuple(
                pl.BlockSpec((None, tokens, share), place(n)) for n in range(len(ats))
            ),
            scratch_shapes=[pltpu.VMEM((tokens, wide), BF16)],
        ),
        compiler_params=params(),
        cost_estimate=cost(
            8 * tokens * wide * share * len(ats),
            2 * (4 * len(ats) * share * (wide + tokens) + tokens * wide),
        ),
    )
    return call(table, *flat(parts), *map(in_vmem, kept))


def fetch(i, pairs, refs, held, sems):
    copies = [
        pltpu.make_async_copy(ref, held.at[pl.ds(2 * n, 2)], sems.at[n])
        for n, ref in enumerate(refs)
    ]

    @pl.when(i == 0)
    def _():
        for copy in copies:
            copy.start()

    for n, copy in enumerate(copies):

        @pl.when(i == 2 * n)
        def _(copy=copy):
            copy.wait()


def gathered(table, at, pairs, kept, by_rows, base=None, blocks=0):
    _, tokens, share = pairs[0].shape
    steps = 2 * len(pairs)
    wide = len(kept) * PIECE
    total_shape = (tokens, wide)
    given = [] if base is None else [base]

    def body(table_ref, *refs):
        pair_refs, refs = refs[: len(pairs)], refs[len(pairs) :]
        kept_refs, refs = refs[: len(kept)], refs[len(kept) :]
        base_refs, refs = refs[: len(given)], refs[len(given) :]
        if blocks:
            *outs, total, held, sems = refs
        else:
            total, held, sems = refs
        i = pl.program_id(0)
        fetch(i, pairs, pair_refs, held, sems)

        @pl.when(i == 0)
        def _():
            total[...] = base_refs[0][...] if given else jnp.zeros(total_shape, F32)

        right = share_block(kept_refs, table_ref[at + i], by_rows)
        total[...] += contract(held[i], right, 1, 0 if by_rows else 1)

        if blocks:

            @pl.when(i == steps - 1)
            def _():
                rows = tokens // blocks
                for k, out in enumerate(outs):
                    out[...] = total[k * rows : (k + 1) * rows, :].astype(BF16)

    scratch = [
        pltpu.VMEM((steps, tokens, share), BF16),
        pltpu.SemaphoreType.DMA((len(pairs),)),
    ]
    if blocks:
        out_shape = (jax.ShapeDtypeStruct((tokens // blocks, wide), BF16),) * blocks
        out_specs = (whole(out_shape[0]),) * blocks
        scratch.insert(0, pltpu.VMEM(total_shape, F32))
    else:
        out_shape = jax.ShapeDtypeStruct(total_shape, F32)
        out_specs = whole(out_shape)
    call = pl.pallas_call(
        body,
        out_shape=out_shape,
        grid_spec=pltpu.PrefetchScalarGridSpec(
            num_scalar_prefetch=1,
            grid=(steps,),
            in_specs=[pl.BlockSpec(memory_space=pl.ANY)] * len(pairs)
            + [resident()] * len(kept)
            + [whole(array) for array in given],
            out_specs=out_specs,
            scratch_shapes=scratch,
        ),
        compiler_params=params(),
        cost_estimate=cost(
            2 * tokens * share * wide * steps,
            2 * share * (wide + tokens) * steps + 4 * tokens * wide,
        ),
    )
    return call(table, *pairs, *map(in_vmem, kept), *given)


def weight_gradient(table, at, pairs, parts, keep, shape, by_rows, into=None):
    tokens = sum(part[0].shape[0] for part in parts)
    share = pairs[0].shape[2]
    wide = parts[0][0].shape[1]
    count = len(flat(parts))
    steps = 2 * len(pairs)
    block = (share, wide) if by_rows else (wide, share)
    given = [] if into is None else [into]

    def body(table_ref, *refs):
        pair_refs, refs = refs[: len(pairs)], refs[len(pairs) :]
        part_refs, refs = refs[:count], refs[count:]
        keep_ref, *_, out, made, held, other, sems, out_sems = refs
        i = pl.program_id(0)
        slot = i % 2

        def copy(step):
            start = pl.multiple_of(table_ref[at + step] * share, TILE)
            if by_rows:
                target = out.at[pl.ds(start, share)]
            else:
                target = out.at[:, pl.ds(start, share)]
            return pltpu.make_async_copy(made.at[step % 2], target, out_sems.at[step % 2])

        @pl.when(i == 0)
        def _():
            values = parts_of(part_refs, parts)
            if by_rows:
                stack(other, values)
            else:
                other[...] = jnp.concatenate(values).T

        fetch(i, pairs, pair_refs, held, sems)

        @pl.when(i >= 2)
        def _():
            copy(i - 2).wait()

        left = held[i].T if by_rows else other
        right = other[...] if by_rows else held[i]
        span = 2 * TILE
        for lo in range(0, block[0], span):
            term = contract(left[lo : lo + span, :], right, 1, 0)
            for k in range(0, span, TILE):
                tile = (lo + k) // TILE
                made[slot, lo + k : lo + k + TILE, :] = (
                    term[k : k + TILE].astype(BF16) * keep_ref[tile : tile + 1, :]
                )
        copy(i).start()

        @pl.when(i == steps - 1)
        def _():
            copy(i - 1).wait()
            copy(i).wait()

    call = pl.pallas_call(
        body,
        out_shape=jax.ShapeDtypeStruct(shape, BF16),
        grid_spec=pltpu.PrefetchScalarGridSpec(
            num_scalar_prefetch=1,
            grid=(steps,),
            in_specs=[pl.BlockSpec(memory_space=pl.ANY)] * len(pairs)
            + [whole(array) for array in flat(parts)]
            + [pl.BlockSpec((None,) + keep.shape[1:], lambda i, t: (t[at + i], 0, 0))]
            + [pl.BlockSpec(memory_space=pl.ANY)] * len(given),
            out_specs=pl.BlockSpec(memory_space=pl.ANY),
            scratch_shapes=[
                pltpu.VMEM((2,) + block, BF16),
                pltpu.VMEM((steps, tokens, share), BF16),
                pltpu.VMEM((tokens, wide) if by_rows else (wide, tokens), BF16),
                pltpu.SemaphoreType.DMA((len(pairs),)),
                pltpu.SemaphoreType.DMA((2,)),
            ],
        ),
        input_output_aliases={2 + len(pairs) + count: 0} if given else {},
        compiler_params=params(),
        cost_estimate=cost(
            2 * tokens * share * wide * steps, 2 * share * (wide + tokens) * steps
        ),
    )
    return call(table, *pairs, *flat(parts), keep, *given)


def per_device_tuned(n_row, n_col, inputs, w_up, w_down, mask_up, mask_down, cotangent):
    share = w_up.shape[1] // n_row
    table = share_table(lax.axis_index("row"))
    keep_up = jnp.repeat(mask_up.astype(BF16), TILE, axis=1)
    keep_up = keep_up.reshape(-1, n_row, share).transpose(1, 0, 2)
    keep_down = jnp.repeat(mask_down.astype(BF16), TILE, axis=1)
    keep_down = keep_down.reshape(n_row, share // TILE, -1)

    def between_cores(value):
        return lax.ppermute(value, "row", [(i, i ^ CORE) for i in range(n_row)])

    def along_first(value):
        return lax.ppermute(value, "row", [(i, i ^ first_of(i)) for i in range(n_row)])

    def along_second(value):
        second = [(X | Y) - first_of(i) for i in range(n_row)]
        return lax.ppermute(value, "row", [(i, i ^ second[i]) for i in range(n_row)])

    def along_col(value, shift):
        return lax.ppermute(value, "col", [(i, (i + shift) % n_col) for i in range(n_col)])

    def toward(value, step, froms):
        return lax.ppermute(value, "col", [(i, i + step) for i in froms])

    def relayed(lower, upper):
        return toward(upper, -1, (1, 2)), toward(lower, 1, (1, 2))

    def after(value, *done):
        return lax.optimization_barrier((value, *done))[0]

    def together(*values):
        return lax.optimization_barrier(values)

    def col_first(blocks):
        return toward(blocks[2], 1, (0, 1)), toward(blocks[2], -1, (2, 3))

    def col_second(blocks, from_lower, from_upper):
        to_upper, to_lower = added_pairs((blocks[3], from_lower), (blocks[1], from_upper))
        return along_col(to_upper, 1), along_col(to_lower, -1)

    features = range(0, w_up.shape[0], PIECE)
    keep_up, keep_down, table = together(keep_up, keep_down, table)
    lower, upper = along_col(inputs, 1), along_col(inputs, -1)
    up = kept_pieces(w_up, keep_up, n_row, False, features)
    lower, upper, *up = together(lower, upper, *up)
    far_lower, far_upper = relayed(lower, upper)
    down = kept_pieces(w_down, after(keep_down, lower), n_row, True, features[: len(features) // 2])
    far_lower, far_upper, *down = together(far_lower, far_upper, *down)
    inputs_all = [(inputs,), (lower,), (far_lower, far_upper), (upper,)]

    own = after(cotangent, far_lower)
    lower, upper = along_col(own, 1), along_col(own, -1)
    up_sent = project(after(table, *down), (AT_SENT,), inputs_all, up, False)[0]
    up_got = between_cores(up_sent)
    up_held = project(after(table, up_sent), (AT_HELD,), inputs_all, up, False)[0]
    pair, rest = add_cores(up_held, up_got)

    near = along_first(pair)
    down += kept_pieces(w_down, after(keep_down, pair), n_row, True, features[len(features) // 2 :])
    lower, upper, *down = together(lower, upper, *down)
    cot_all = [(cotangent,), (lower,), relayed(lower, upper), (upper,)]
    near, lower = together(near, lower)
    passed, own = add_first(rest, near)
    back_sent = project(after(table, passed), (AT_SENT,), cot_all, down, True)[0]
    last, back_sent = together(along_second(passed), back_sent)
    back_got = between_cores(back_sent)
    hidden, act = activated(own, last)

    back_held = project(after(table, act), (AT_HELD,), cot_all, down, True)[0]
    act_first, back_held = together(along_first(act), back_held)
    pair, rest = add_cores(back_held, back_got)
    near = along_first(pair)
    act_near = paired(act, after(act_first, pair))
    act_core = between_cores(act_near)

    def grad_down_of(start, at, pairs, into=None):
        return weight_gradient(
            after(table, start), at, pairs, cot_all, keep_down, w_down.shape, True, into
        )

    grad_down = grad_down_of(act_near, AT_NEAR, [act_near])
    act_far = along_second(after(act_near, grad_down))
    out_total = gathered(
        after(table, grad_down), AT_NEAR, [act_near, act_core], down, True
    )
    near, out_total = together(near, out_total)
    passed, own = add_first(rest, near)
    grad_down = grad_down_of(passed, AT_NEAR_CORE, [act_core], grad_down)
    last, grad_down = together(along_second(passed), grad_down)
    grad = pulled(hidden, own, last)

    grad_first = along_first(grad)
    act_far_core = between_cores(after(act_far, grad))
    out_blocks = gathered(
        after(table, grad), AT_FAR, [act_far, act_far_core], down, True, out_total, n_col
    )
    grad_first, out_far = together(grad_first, out_blocks[2])
    out_blocks = [out_blocks[0], out_blocks[1], out_far, out_blocks[3]]
    grad_near = paired(grad, grad_first)
    grad_far = along_second(grad_near)
    grad_core = between_cores(grad_near)
    out_got = col_first(out_blocks)
    in_total = gathered(table, AT_NEAR, [grad_near, grad_core], up, False)
    *out_got, in_total = together(*out_got, in_total)
    out_last = col_second(out_blocks, *out_got)
    grad_far, in_total = together(grad_far, in_total)
    grad_far_core = between_cores(grad_far)
    in_total = gathered(table, AT_FAR, [grad_far], up, False, in_total)
    in_blocks = gathered(table, AT_FAR_CORE, [grad_far_core], up, False, in_total, n_col)

    grad_down = grad_down_of(in_blocks[2], AT_FAR, [act_far, act_far_core], grad_down)
    *out_last, in_far = together(*out_last, in_blocks[2])
    in_blocks = [in_blocks[0], in_blocks[1], in_far, in_blocks[3]]
    *in_got, grad_down = together(*col_first(in_blocks), grad_down)
    in_last = col_second(in_blocks, *in_got)
    grad_up = weight_gradient(
        after(table, grad_down),
        AT_NEAR,
        [grad_near, grad_core, grad_far, grad_far_core],
        inputs_all,
        keep_up,
        w_up.shape,
        False,
    )
    *in_last, grad_up = together(*in_last, grad_up)
    outputs = added([out_blocks[0], *out_last])
    grad_inputs = added([in_blocks[0], *in_last])
    return (outputs, grad_inputs, grad_up, grad_down)


def solution(mesh):
    in_specs = (
        P("col", "row"),
        P("row", "col"),
        P("col", "row"),
        P("row", "col"),
        P("col", "row"),
        P("col", "row"),
    )
    out_specs = (P("col", "row"), P("col", "row"), P("row", "col"), P("col", "row"))
    n_row, n_col = mesh.shape["row"], mesh.shape["col"]

    def per_device(inputs, w_up, w_down, mask_up, mask_down, cotangent):
        fits = n_row == 8 and n_col == 4 and mask_up.shape[1] % n_row == 0 and w_up.shape[0] % PIECE == 0
        plan = functools.partial(per_device_tuned, n_row, n_col) if fits else per_device_plain
        return plan(inputs, w_up, w_down, mask_up, mask_down, cotangent)

    return jax.shard_map(
        per_device, mesh=mesh, in_specs=in_specs, out_specs=out_specs, check_vma=False
    )
```

```python
import functools

import jax
import jax.numpy as jnp
from jax import lax
from jax.experimental import pallas as pl
from jax.experimental.pallas import tpu as pltpu
from jax.sharding import PartitionSpec as P

TILE = 128
VMEM_LIMIT = 12 << 20
PIECE = 256
F32 = jnp.float32
BF16 = jnp.bfloat16


def smooth_gate(value):
    return jax.nn.gelu(value, approximate=True)


def contract(left, right, left_dim, right_dim):
    return lax.dot_general(
        left, right, (((left_dim,), (right_dim,)), ((), ())), preferred_element_type=F32
    )


def apply_mask(weight, mask):
    rows, cols = mask.shape
    tile = weight.shape[0] // rows
    shaped = weight.reshape(rows, tile, cols, tile)
    keep = mask[:, None, :, None].astype(weight.dtype)
    return (shaped * keep).reshape(weight.shape)


def activate(hidden, grad_act):
    act = smooth_gate(hidden).astype(BF16)
    _, pull = jax.vjp(smooth_gate, hidden)
    grad_hidden = pull(grad_act)[0].astype(BF16)
    return (act, grad_hidden)


def per_device_plain(inputs, w_up, w_down, mask_up, mask_down, cotangent):
    up_kept = apply_mask(w_up, mask_up)
    down_kept = apply_mask(w_down, mask_down)
    inputs_all, cot_all = (
        lax.all_gather(inputs, "col", axis=0, tiled=True),
        lax.all_gather(cotangent, "col", axis=0, tiled=True),
    )
    up_part = jnp.dot(inputs_all, up_kept, preferred_element_type=F32)
    back_part = contract(cot_all, down_kept, 1, 1)
    hidden, grad_act = (
        lax.psum_scatter(
            part.astype(BF16), "row", scatter_dimension=0, tiled=True
        ).astype(F32)
        for part in (up_part, back_part)
    )
    act, grad_hidden = activate(hidden, grad_act)
    act_all, grad_all = (
        lax.all_gather(act, "row", axis=0, tiled=True),
        lax.all_gather(grad_hidden, "row", axis=0, tiled=True),
    )
    out_part = jnp.dot(act_all, down_kept, preferred_element_type=F32)
    input_part = contract(grad_all, up_kept, 1, 1)
    outputs, grad_inputs = (
        lax.psum_scatter(
            part.astype(BF16), "col", scatter_dimension=0, tiled=True
        ).astype(F32)
        for part in (out_part, input_part)
    )
    grad_down = apply_mask(contract(act_all, cot_all, 0, 0).astype(BF16), mask_down)
    grad_up = apply_mask(contract(inputs_all, grad_all, 0, 0).astype(BF16), mask_up)
    return (outputs.astype(BF16), grad_inputs.astype(BF16), grad_up, grad_down)


CORE, X, Y = 1, 2, 4


def first_of(row):
    return X if row % 2 == 0 else Y


AT_SENT, AT_HELD, AT_NEAR, AT_FAR = 0, 4, 8, 12
AT_NEAR_CORE, AT_FAR_CORE = 10, 14


def share_table(row):
    first = jnp.where(row % 2 == 0, X, Y)
    second = (X | Y) - first
    other = row ^ CORE
    sent = [other ^ first ^ second, other ^ second, other ^ first, other]
    held = [row ^ first ^ second, row ^ first, row ^ second, row]
    near = [row, row ^ first, other, other ^ second]
    far = [row ^ second, row ^ second ^ first, other ^ first, other ^ first ^ second]
    return jnp.stack(sent + held + near + far)


def cost(flops, moved):
    return pl.CostEstimate(flops=int(flops) // 1000, bytes_accessed=int(moved) // 1000, transcendentals=0)


def params():
    return pltpu.CompilerParams(
        dimension_semantics=("arbitrary",), vmem_limit_bytes=VMEM_LIMIT
    )


def whole(array):
    return pl.BlockSpec(array.shape, lambda i, t: (0,) * len(array.shape))


def resident():
    return pl.BlockSpec(memory_space=pltpu.VMEM)


def in_vmem(array):
    return pltpu.with_memory_space_constraint(array, pltpu.VMEM)


def flat(parts):
    return [array for part in parts for array in part]


def parts_of(refs, parts):
    refs = iter(refs)
    return [functools.reduce(jnp.add, [next(refs)[...] for _ in part]) for part in parts]


def stack(dst, values):
    row = 0
    for value in values:
        dst[row : row + value.shape[0], :] = value
        row += value.shape[0]


def small(body, outs, *given):
    specs = tuple(resident() for _ in outs)
    return pl.pallas_call(
        body,
        out_shape=tuple(pltpu.VMEM(shape, dtype) for shape, dtype in outs),
        in_specs=[resident()] * len(given),
        out_specs=specs,
        compiler_params=pltpu.CompilerParams(vmem_limit_bytes=VMEM_LIMIT),
    )(*[in_vmem(array) for array in given])


def add_cores(held, got):
    _, tokens, share = held.shape

    def body(held_ref, got_ref, pair, rest):
        for k in range(4):
            total = held_ref[k].astype(F32) + got_ref[k].astype(F32)
            if k < 2:
                pair[k] = total.astype(BF16)
            else:
                rest[k - 2] = total

    shape = (2, tokens, share)
    return small(body, [(shape, BF16), (shape, F32)], held, got)


def add_first(rest, near):
    _, tokens, share = rest.shape

    def body(rest_ref, near_ref, passed, own):
        passed[...] = (rest_ref[0] + near_ref[0].astype(F32)).astype(BF16)
        own[...] = rest_ref[1] + near_ref[1].astype(F32)

    return small(body, [((tokens, share), BF16), ((tokens, share), F32)], rest, near)


def activated(own, last):
    def body(own_ref, last_ref, hidden, act):
        value = own_ref[...] + last_ref[...].astype(F32)
        hidden[...] = value
        act[...] = smooth_gate(value).astype(BF16)

    return small(body, [(own.shape, F32), (own.shape, BF16)], own, last)


def pulled(hidden, own, last):
    def body(hidden_ref, own_ref, last_ref, grad):
        _, pull = jax.vjp(smooth_gate, hidden_ref[...])
        grad[...] = pull(own_ref[...] + last_ref[...].astype(F32))[0].astype(BF16)

    return small(body, [(own.shape, BF16)], hidden, own, last)[0]


def paired(left, right):
    def body(left_ref, right_ref, pair):
        pair[0] = left_ref[...]
        pair[1] = right_ref[...]

    return small(body, [((2,) + left.shape, BF16)], left, right)[0]


def added(terms):
    def body(*refs):
        *given, out = refs
        out[...] = functools.reduce(jnp.add, [ref[...].astype(F32) for ref in given]).astype(BF16)

    return pl.pallas_call(
        body,
        out_shape=jax.ShapeDtypeStruct(terms[0].shape, BF16),
        compiler_params=pltpu.CompilerParams(vmem_limit_bytes=VMEM_LIMIT),
    )(*terms)


def kept_pieces(weight, keep, shares, by_rows, pieces):
    rows, columns = weight.shape
    share = (rows if by_rows else columns) // shares
    block = (share, PIECE) if by_rows else (PIECE, share)

    def body(weight_ref, keep_ref, *refs):
        *outs, sems = refs

        def copies(n):
            start = pl.multiple_of(n * share, TILE)
            for h, lo in enumerate(pieces):
                if by_rows:
                    source = weight_ref.at[pl.ds(start, share), pl.ds(lo, PIECE)]
                else:
                    source = weight_ref.at[pl.ds(lo, PIECE), pl.ds(start, share)]
                yield pltpu.make_async_copy(source, outs[h].at[n], sems.at[n, h])

        for n in range(shares):
            for copy in copies(n):
                copy.start()

        @pl.loop(0, shares)
        def _(n):
            for copy in copies(n):
                copy.wait()
            for lo, out in zip(pieces, outs):
                for k in range(0, block[0], TILE):
                    strip = slice(k, k + TILE)
                    if by_rows:
                        kept = keep_ref[n, k // TILE : k // TILE + 1, lo : lo + PIECE]
                    else:
                        tile = (lo + k) // TILE
                        kept = keep_ref[n, tile : tile + 1, :]
                    out[n, strip, :] = out[n, strip, :] * kept

    return pl.pallas_call(
        body,
        out_shape=(pltpu.VMEM((shares,) + block, BF16),) * len(pieces),
        in_specs=[pl.BlockSpec(memory_space=pltpu.HBM), resident()],
        out_specs=(resident(),) * len(pieces),
        scratch_shapes=[pltpu.SemaphoreType.DMA((shares, len(pieces)))],
        compiler_params=pltpu.CompilerParams(vmem_limit_bytes=VMEM_LIMIT),
        cost_estimate=cost(rows * columns, 4 * rows * columns),
    )(pltpu.with_memory_space_constraint(weight, pltpu.HBM), keep)


def share_block(kept_refs, share, by_rows):
    return jnp.concatenate([ref[share] for ref in kept_refs], axis=1 if by_rows else 0)


def project(table, ats, parts, kept, by_rows):
    tokens = sum(part[0].shape[0] for part in parts)
    wide = parts[0][0].shape[1]
    share = kept[0].shape[1 if by_rows else 2]
    count = len(flat(parts))

    def body(table_ref, *refs):
        part_refs, refs = refs[:count], refs[count:]
        kept_refs, (*outs, held) = refs[: len(kept)], refs[len(kept) :]
        i = pl.program_id(0)

        @pl.when(i == 0)
        def _():
            stack(held, parts_of(part_refs, parts))

        right = share_block(kept_refs, table_ref[ats[0] + i], by_rows)
        result = contract(held[...], right, 1, 1 if by_rows else 0).astype(BF16)
        for n, out in enumerate(outs):

            @pl.when(i // 4 == n)
            def _(out=out):
                out[...] = result

    def place(n):
        return lambda i, t: (jnp.clip(i - 4 * n, 0, 3), 0, 0)

    call = pl.pallas_call(
        body,
        out_shape=(jax.ShapeDtypeStruct((4, tokens, share), BF16),) * len(ats),
        grid_spec=pltpu.PrefetchScalarGridSpec(
            num_scalar_prefetch=1,
            grid=(4 * len(ats),),
            in_specs=[whole(array) for array in flat(parts)] + [resident()] * len(kept),
            out_specs=tuple(
                pl.BlockSpec((None, tokens, share), place(n)) for n in range(len(ats))
            ),
            scratch_shapes=[pltpu.VMEM((tokens, wide), BF16)],
        ),
        compiler_params=params(),
        cost_estimate=cost(
            8 * tokens * wide * share * len(ats),
            2 * (4 * len(ats) * share * (wide + tokens) + tokens * wide),
        ),
    )
    return call(table, *flat(parts), *map(in_vmem, kept))


def fetch(i, pairs, refs, held, sems):
    copies = [
        pltpu.make_async_copy(ref, held.at[pl.ds(2 * n, 2)], sems.at[n])
        for n, ref in enumerate(refs)
    ]

    @pl.when(i == 0)
    def _():
        for copy in copies:
            copy.start()

    for n, copy in enumerate(copies):

        @pl.when(i == 2 * n)
        def _(copy=copy):
            copy.wait()


def gathered(table, at, pairs, kept, by_rows, base=None, blocks=0):
    _, tokens, share = pairs[0].shape
    steps = 2 * len(pairs)
    wide = len(kept) * PIECE
    total_shape = (tokens, wide)
    given = [] if base is None else [base]

    def body(table_ref, *refs):
        pair_refs, refs = refs[: len(pairs)], refs[len(pairs) :]
        kept_refs, refs = refs[: len(kept)], refs[len(kept) :]
        base_refs, refs = refs[: len(given)], refs[len(given) :]
        if blocks:
            *outs, total, held, sems = refs
        else:
            total, held, sems = refs
        i = pl.program_id(0)
        fetch(i, pairs, pair_refs, held, sems)

        @pl.when(i == 0)
        def _():
            total[...] = base_refs[0][...] if given else jnp.zeros(total_shape, F32)

        right = share_block(kept_refs, table_ref[at + i], by_rows)
        total[...] += contract(held[i], right, 1, 0 if by_rows else 1)

        if blocks:

            @pl.when(i == steps - 1)
            def _():
                rows = tokens // blocks
                for k, out in enumerate(outs):
                    out[...] = total[k * rows : (k + 1) * rows, :].astype(BF16)

    scratch = [
        pltpu.VMEM((steps, tokens, share), BF16),
        pltpu.SemaphoreType.DMA((len(pairs),)),
    ]
    if blocks:
        out_shape = (jax.ShapeDtypeStruct((tokens // blocks, wide), BF16),) * blocks
        out_specs = (whole(out_shape[0]),) * blocks
        scratch.insert(0, pltpu.VMEM(total_shape, F32))
    else:
        out_shape = jax.ShapeDtypeStruct(total_shape, F32)
        out_specs = whole(out_shape)
    call = pl.pallas_call(
        body,
        out_shape=out_shape,
        grid_spec=pltpu.PrefetchScalarGridSpec(
            num_scalar_prefetch=1,
            grid=(steps,),
            in_specs=[pl.BlockSpec(memory_space=pl.ANY)] * len(pairs)
            + [resident()] * len(kept)
            + [whole(array) for array in given],
            out_specs=out_specs,
            scratch_shapes=scratch,
        ),
        compiler_params=params(),
        cost_estimate=cost(
            2 * tokens * share * wide * steps,
            2 * share * (wide + tokens) * steps + 4 * tokens * wide,
        ),
    )
    return call(table, *pairs, *map(in_vmem, kept), *given)


def weight_gradient(table, at, pairs, parts, keep, shape, by_rows, into=None):
    tokens = sum(part[0].shape[0] for part in parts)
    share = pairs[0].shape[2]
    wide = parts[0][0].shape[1]
    count = len(flat(parts))
    steps = 2 * len(pairs)
    block = (share, wide) if by_rows else (wide, share)
    given = [] if into is None else [into]

    def body(table_ref, *refs):
        pair_refs, refs = refs[: len(pairs)], refs[len(pairs) :]
        part_refs, refs = refs[:count], refs[count:]
        keep_ref, *_, out, made, held, other, sems, out_sems = refs
        i = pl.program_id(0)
        slot = i % 2

        def copy(step):
            start = pl.multiple_of(table_ref[at + step] * share, TILE)
            if by_rows:
                target = out.at[pl.ds(start, share)]
            else:
                target = out.at[:, pl.ds(start, share)]
            return pltpu.make_async_copy(made.at[step % 2], target, out_sems.at[step % 2])

        @pl.when(i == 0)
        def _():
            values = parts_of(part_refs, parts)
            if by_rows:
                stack(other, values)
            else:
                other[...] = jnp.concatenate(values).T

        fetch(i, pairs, pair_refs, held, sems)

        @pl.when(i >= 2)
        def _():
            copy(i - 2).wait()

        left = held[i].T if by_rows else other
        right = other[...] if by_rows else held[i]
        span = 2 * TILE
        for lo in range(0, block[0], span):
            term = contract(left[lo : lo + span, :], right, 1, 0)
            for k in range(0, span, TILE):
                tile = (lo + k) // TILE
                made[slot, lo + k : lo + k + TILE, :] = (
                    term[k : k + TILE].astype(BF16) * keep_ref[tile : tile + 1, :]
                )
        copy(i).start()

        @pl.when(i == steps - 1)
        def _():
            copy(i - 1).wait()
            copy(i).wait()

    call = pl.pallas_call(
        body,
        out_shape=jax.ShapeDtypeStruct(shape, BF16),
        grid_spec=pltpu.PrefetchScalarGridSpec(
            num_scalar_prefetch=1,
            grid=(steps,),
            in_specs=[pl.BlockSpec(memory_space=pl.ANY)] * len(pairs)
            + [whole(array) for array in flat(parts)]
            + [pl.BlockSpec((None,) + keep.shape[1:], lambda i, t: (t[at + i], 0, 0))]
            + [pl.BlockSpec(memory_space=pl.ANY)] * len(given),
            out_specs=pl.BlockSpec(memory_space=pl.ANY),
            scratch_shapes=[
                pltpu.VMEM((2,) + block, BF16),
                pltpu.VMEM((steps, tokens, share), BF16),
                pltpu.VMEM((tokens, wide) if by_rows else (wide, tokens), BF16),
                pltpu.SemaphoreType.DMA((len(pairs),)),
                pltpu.SemaphoreType.DMA((2,)),
            ],
        ),
        input_output_aliases={2 + len(pairs) + count: 0} if given else {},
        compiler_params=params(),
        cost_estimate=cost(
            2 * tokens * share * wide * steps, 2 * share * (wide + tokens) * steps
        ),
    )
    return call(table, *pairs, *flat(parts), keep, *given)


def per_device_tuned(n_row, n_col, inputs, w_up, w_down, mask_up, mask_down, cotangent):
    share = w_up.shape[1] // n_row
    table = share_table(lax.axis_index("row"))
    keep_up = jnp.repeat(mask_up.astype(BF16), TILE, axis=1)
    keep_up = keep_up.reshape(-1, n_row, share).transpose(1, 0, 2)
    keep_down = jnp.repeat(mask_down.astype(BF16), TILE, axis=1)
    keep_down = keep_down.reshape(n_row, share // TILE, -1)

    def between_cores(value):
        return lax.ppermute(value, "row", [(i, i ^ CORE) for i in range(n_row)])

    def along_first(value):
        return lax.ppermute(value, "row", [(i, i ^ first_of(i)) for i in range(n_row)])

    def along_second(value):
        second = [(X | Y) - first_of(i) for i in range(n_row)]
        return lax.ppermute(value, "row", [(i, i ^ second[i]) for i in range(n_row)])

    def along_col(value, shift):
        return lax.ppermute(value, "col", [(i, (i + shift) % n_col) for i in range(n_col)])

    def toward(value, step, froms):
        return lax.ppermute(value, "col", [(i, i + step) for i in froms])

    def relayed(lower, upper):
        return toward(upper, -1, (1, 2)), toward(lower, 1, (1, 2))

    def after(value, *done):
        return lax.optimization_barrier((value, *done))[0]

    def together(*values):
        return lax.optimization_barrier(values)

    def col_sum(blocks):
        return [blocks[0]] + [along_col(blocks[k], -k) for k in range(1, n_col)]

    features = range(0, w_up.shape[0], PIECE)
    keep_up, keep_down, table = together(keep_up, keep_down, table)
    lower, upper = along_col(inputs, 1), along_col(inputs, -1)
    up = kept_pieces(w_up, keep_up, n_row, False, features)
    lower, upper, *up = together(lower, upper, *up)
    far = relayed(lower, upper)
    inputs_all = [(inputs,), (lower,), far, (upper,)]
    cot = after(cotangent, lower, upper)
    lower, upper = along_col(cot, 1), along_col(cot, -1)
    down = kept_pieces(w_down, after(keep_down, cot), n_row, True, features)
    lower, upper, *down = together(lower, upper, *down)
    far = relayed(lower, upper)
    cot_all = [(cotangent,), (lower,), far, (upper,)]

    up_sent = project(after(table, lower, *down), (AT_SENT,), inputs_all, up, False)[0]
    up_got = between_cores(up_sent)
    up_held = project(after(table, up_sent), (AT_HELD,), inputs_all, up, False)[0]
    up_held = after(up_held, *far)
    pair, rest = add_cores(up_held, up_got)
    near = along_first(pair)

    back_sent, back_held = project(
        after(table, pair), (AT_SENT, AT_HELD), cot_all, down, True
    )
    near, back_sent, back_held = together(near, back_sent, back_held)
    passed, own = add_first(rest, near)
    last = along_second(passed)
    back_got = between_cores(after(back_sent, passed))
    back_pair, back_rest = add_cores(back_held, back_got)
    last, back_pair = together(last, back_pair)
    near = along_first(back_pair)
    hidden, act = activated(own, last)

    act_first = along_first(act)
    passed, own = add_first(back_rest, after(near, act))
    last = along_second(passed)
    act_near = paired(act, after(act_first, passed))
    act_far = along_second(act_near)
    act_core = between_cores(act_near)

    def grad_down_of(start, at, pairs, into=None):
        return weight_gradient(
            after(table, start), at, pairs, cot_all, keep_down, w_down.shape, True, into
        )

    grad_down = grad_down_of(act_near, AT_NEAR, [act_near])
    last, grad_down = together(last, grad_down)
    grad = pulled(hidden, own, last)

    grad_first = along_first(grad)
    out_total = gathered(
        after(table, grad), AT_NEAR, [act_near, act_core], down, True
    )
    grad_first, out_total = together(grad_first, out_total)
    grad_near = paired(grad, grad_first)
    grad_far = along_second(grad_near)
    grad_core = between_cores(grad_near)
    act_far_core = between_cores(after(act_far, grad_near))
    grad_down = grad_down_of(grad_near, AT_NEAR_CORE, [act_core], grad_down)
    out_blocks = gathered(
        after(table, grad_down), AT_FAR, [act_far, act_far_core], down, True, out_total, n_col
    )
    out_terms = col_sum(out_blocks)
    in_total = gathered(
        after(table, out_blocks[0]), AT_NEAR, [grad_near, grad_core], up, False
    )
    grad_far, in_total = together(grad_far, in_total)
    grad_far_core = between_cores(grad_far)
    in_total = gathered(table, AT_FAR, [grad_far], up, False, in_total)
    in_blocks = gathered(table, AT_FAR_CORE, [grad_far_core], up, False, in_total, n_col)

    in_terms = col_sum(in_blocks)
    grad_down = grad_down_of(in_blocks[0], AT_FAR, [act_far, act_far_core], grad_down)
    grad_up = weight_gradient(
        after(table, grad_down),
        AT_NEAR,
        [grad_near, grad_core, grad_far, grad_far_core],
        inputs_all,
        keep_up,
        w_up.shape,
        False,
    )
    out_terms[1:] = together(*out_terms[1:], grad_down)[:-1]
    outputs = added(out_terms)
    grad_inputs = added(in_terms)
    return (outputs, grad_inputs, grad_up, grad_down)


def solution(mesh):
    in_specs = (
        P("col", "row"),
        P("row", "col"),
        P("col", "row"),
        P("row", "col"),
        P("col", "row"),
        P("col", "row"),
    )
    out_specs = (P("col", "row"), P("col", "row"), P("row", "col"), P("col", "row"))
    n_row, n_col = mesh.shape["row"], mesh.shape["col"]

    def per_device(inputs, w_up, w_down, mask_up, mask_down, cotangent):
        fits = n_row == 8 and n_col == 4 and mask_up.shape[1] % n_row == 0 and w_up.shape[0] % PIECE == 0
        plan = functools.partial(per_device_tuned, n_row, n_col) if fits else per_device_plain
        return plan(inputs, w_up, w_down, mask_up, mask_down, cotangent)

    return jax.shard_map(
        per_device, mesh=mesh, in_specs=in_specs, out_specs=out_specs, check_vma=False
    )
```

```python
import functools

import jax
import jax.numpy as jnp
from jax import lax
from jax.experimental import pallas as pl
from jax.experimental.pallas import tpu as pltpu
from jax.sharding import PartitionSpec as P

TILE = 128
VMEM_LIMIT = 11 << 20
PIECE = 256
F32 = jnp.float32
BF16 = jnp.bfloat16


def smooth_gate(value):
    return jax.nn.gelu(value, approximate=True)


def contract(left, right, left_dim, right_dim):
    return lax.dot_general(
        left, right, (((left_dim,), (right_dim,)), ((), ())), preferred_element_type=F32
    )


def apply_mask(weight, mask):
    rows, cols = mask.shape
    tile = weight.shape[0] // rows
    shaped = weight.reshape(rows, tile, cols, tile)
    keep = mask[:, None, :, None].astype(weight.dtype)
    return (shaped * keep).reshape(weight.shape)


def activate(hidden, grad_act):
    act = smooth_gate(hidden).astype(BF16)
    _, pull = jax.vjp(smooth_gate, hidden)
    grad_hidden = pull(grad_act)[0].astype(BF16)
    return (act, grad_hidden)


def per_device_plain(inputs, w_up, w_down, mask_up, mask_down, cotangent):
    up_kept = apply_mask(w_up, mask_up)
    down_kept = apply_mask(w_down, mask_down)
    inputs_all, cot_all = (
        lax.all_gather(inputs, "col", axis=0, tiled=True),
        lax.all_gather(cotangent, "col", axis=0, tiled=True),
    )
    up_part = jnp.dot(inputs_all, up_kept, preferred_element_type=F32)
    back_part = contract(cot_all, down_kept, 1, 1)
    hidden, grad_act = (
        lax.psum_scatter(
            part.astype(BF16), "row", scatter_dimension=0, tiled=True
        ).astype(F32)
        for part in (up_part, back_part)
    )
    act, grad_hidden = activate(hidden, grad_act)
    act_all, grad_all = (
        lax.all_gather(act, "row", axis=0, tiled=True),
        lax.all_gather(grad_hidden, "row", axis=0, tiled=True),
    )
    out_part = jnp.dot(act_all, down_kept, preferred_element_type=F32)
    input_part = contract(grad_all, up_kept, 1, 1)
    outputs, grad_inputs = (
        lax.psum_scatter(
            part.astype(BF16), "col", scatter_dimension=0, tiled=True
        ).astype(F32)
        for part in (out_part, input_part)
    )
    grad_down = apply_mask(contract(act_all, cot_all, 0, 0).astype(BF16), mask_down)
    grad_up = apply_mask(contract(inputs_all, grad_all, 0, 0).astype(BF16), mask_up)
    return (outputs.astype(BF16), grad_inputs.astype(BF16), grad_up, grad_down)


CORE, X, Y = 1, 2, 4


def first_of(row):
    return X if row % 2 == 0 else Y


AT_SENT, AT_HELD, AT_NEAR, AT_FAR = 0, 4, 8, 12
AT_NEAR_CORE, AT_FAR_CORE = 10, 14


def share_table(row):
    first = jnp.where(row % 2 == 0, X, Y)
    second = (X | Y) - first
    other = row ^ CORE
    sent = [other ^ first ^ second, other ^ second, other ^ first, other]
    held = [row ^ first ^ second, row ^ first, row ^ second, row]
    near = [row, row ^ first, other, other ^ second]
    far = [row ^ second, row ^ second ^ first, other ^ first, other ^ first ^ second]
    return jnp.stack(sent + held + near + far)


def cost(flops, moved):
    return pl.CostEstimate(flops=int(flops) // 1000, bytes_accessed=int(moved) // 1000, transcendentals=0)


def params():
    return pltpu.CompilerParams(
        dimension_semantics=("arbitrary",), vmem_limit_bytes=VMEM_LIMIT
    )


def whole(array):
    return pl.BlockSpec(array.shape, lambda i, t: (0,) * len(array.shape))


def resident():
    return pl.BlockSpec(memory_space=pltpu.VMEM)


def in_vmem(array):
    return pltpu.with_memory_space_constraint(array, pltpu.VMEM)


def flat(parts):
    return [array for part in parts for array in part]


def parts_of(refs, parts):
    refs = iter(refs)
    return [functools.reduce(jnp.add, [next(refs)[...] for _ in part]) for part in parts]


def stack(dst, values):
    row = 0
    for value in values:
        dst[row : row + value.shape[0], :] = value
        row += value.shape[0]


def small(body, outs, *given):
    specs = tuple(resident() for _ in outs)
    return pl.pallas_call(
        body,
        out_shape=tuple(pltpu.VMEM(shape, dtype) for shape, dtype in outs),
        in_specs=[resident()] * len(given),
        out_specs=specs,
        compiler_params=pltpu.CompilerParams(vmem_limit_bytes=VMEM_LIMIT),
    )(*[in_vmem(array) for array in given])


def add_cores(held, got):
    _, tokens, share = held.shape

    def body(held_ref, got_ref, pair, rest):
        for k in range(4):
            total = held_ref[k].astype(F32) + got_ref[k].astype(F32)
            if k < 2:
                pair[k] = total.astype(BF16)
            else:
                rest[k - 2] = total

    shape = (2, tokens, share)
    return small(body, [(shape, BF16), (shape, F32)], held, got)


def add_first(rest, near):
    _, tokens, share = rest.shape

    def body(rest_ref, near_ref, passed, own):
        passed[...] = (rest_ref[0] + near_ref[0].astype(F32)).astype(BF16)
        own[...] = rest_ref[1] + near_ref[1].astype(F32)

    return small(body, [((tokens, share), BF16), ((tokens, share), F32)], rest, near)


def activated(own, last):
    def body(own_ref, last_ref, hidden, act):
        value = own_ref[...] + last_ref[...].astype(F32)
        hidden[...] = value
        act[...] = smooth_gate(value).astype(BF16)

    return small(body, [(own.shape, F32), (own.shape, BF16)], own, last)


def pulled(hidden, own, last):
    def body(hidden_ref, own_ref, last_ref, grad):
        _, pull = jax.vjp(smooth_gate, hidden_ref[...])
        grad[...] = pull(own_ref[...] + last_ref[...].astype(F32))[0].astype(BF16)

    return small(body, [(own.shape, BF16)], hidden, own, last)[0]


def paired(left, right):
    def body(left_ref, right_ref, pair):
        pair[0] = left_ref[...]
        pair[1] = right_ref[...]

    return small(body, [((2,) + left.shape, BF16)], left, right)[0]


def added(terms):
    def body(*refs):
        *given, out = refs
        out[...] = functools.reduce(jnp.add, [ref[...].astype(F32) for ref in given]).astype(BF16)

    return pl.pallas_call(
        body,
        out_shape=jax.ShapeDtypeStruct(terms[0].shape, BF16),
        compiler_params=pltpu.CompilerParams(vmem_limit_bytes=VMEM_LIMIT),
    )(*terms)


def kept_pieces(weight, keep, shares, by_rows, pieces):
    rows, columns = weight.shape
    share = (rows if by_rows else columns) // shares
    block = (share, PIECE) if by_rows else (PIECE, share)

    def body(weight_ref, keep_ref, *refs):
        *outs, sems = refs

        def copies(n):
            start = pl.multiple_of(n * share, TILE)
            for h, lo in enumerate(pieces):
                if by_rows:
                    source = weight_ref.at[pl.ds(start, share), pl.ds(lo, PIECE)]
                else:
                    source = weight_ref.at[pl.ds(lo, PIECE), pl.ds(start, share)]
                yield pltpu.make_async_copy(source, outs[h].at[n], sems.at[n, h])

        for n in range(shares):
            for copy in copies(n):
                copy.start()

        @pl.loop(0, shares)
        def _(n):
            for copy in copies(n):
                copy.wait()
            for lo, out in zip(pieces, outs):
                for k in range(0, block[0], TILE):
                    strip = slice(k, k + TILE)
                    if by_rows:
                        kept = keep_ref[n, k // TILE : k // TILE + 1, lo : lo + PIECE]
                    else:
                        tile = (lo + k) // TILE
                        kept = keep_ref[n, tile : tile + 1, :]
                    out[n, strip, :] = out[n, strip, :] * kept

    return pl.pallas_call(
        body,
        out_shape=(pltpu.VMEM((shares,) + block, BF16),) * len(pieces),
        in_specs=[pl.BlockSpec(memory_space=pltpu.HBM), resident()],
        out_specs=(resident(),) * len(pieces),
        scratch_shapes=[pltpu.SemaphoreType.DMA((shares, len(pieces)))],
        compiler_params=pltpu.CompilerParams(vmem_limit_bytes=VMEM_LIMIT),
        cost_estimate=cost(rows * columns, 4 * rows * columns),
    )(pltpu.with_memory_space_constraint(weight, pltpu.HBM), keep)


def share_block(kept_refs, share, by_rows):
    return jnp.concatenate([ref[share] for ref in kept_refs], axis=1 if by_rows else 0)


def project(table, ats, parts, kept, by_rows):
    tokens = sum(part[0].shape[0] for part in parts)
    wide = parts[0][0].shape[1]
    share = kept[0].shape[1 if by_rows else 2]
    count = len(flat(parts))

    def body(table_ref, *refs):
        part_refs, refs = refs[:count], refs[count:]
        kept_refs, (*outs, held) = refs[: len(kept)], refs[len(kept) :]
        i = pl.program_id(0)

        @pl.when(i == 0)
        def _():
            stack(held, parts_of(part_refs, parts))

        right = share_block(kept_refs, table_ref[ats[0] + i], by_rows)
        result = contract(held[...], right, 1, 1 if by_rows else 0).astype(BF16)
        for n, out in enumerate(outs):

            @pl.when(i // 4 == n)
            def _(out=out):
                out[...] = result

    def place(n):
        return lambda i, t: (jnp.clip(i - 4 * n, 0, 3), 0, 0)

    call = pl.pallas_call(
        body,
        out_shape=(jax.ShapeDtypeStruct((4, tokens, share), BF16),) * len(ats),
        grid_spec=pltpu.PrefetchScalarGridSpec(
            num_scalar_prefetch=1,
            grid=(4 * len(ats),),
            in_specs=[whole(array) for array in flat(parts)] + [resident()] * len(kept),
            out_specs=tuple(
                pl.BlockSpec((None, tokens, share), place(n)) for n in range(len(ats))
            ),
            scratch_shapes=[pltpu.VMEM((tokens, wide), BF16)],
        ),
        compiler_params=params(),
        cost_estimate=cost(
            8 * tokens * wide * share * len(ats),
            2 * (4 * len(ats) * share * (wide + tokens) + tokens * wide),
        ),
    )
    return call(table, *flat(parts), *map(in_vmem, kept))


def fetch(i, pairs, refs, held, sems):
    copies = [
        pltpu.make_async_copy(ref, held.at[pl.ds(2 * n, 2)], sems.at[n])
        for n, ref in enumerate(refs)
    ]

    @pl.when(i == 0)
    def _():
        for copy in copies:
            copy.start()

    for n, copy in enumerate(copies):

        @pl.when(i == 2 * n)
        def _(copy=copy):
            copy.wait()


def gathered(table, at, pairs, kept, by_rows, base=None, blocks=0):
    _, tokens, share = pairs[0].shape
    steps = 2 * len(pairs)
    wide = len(kept) * PIECE
    total_shape = (tokens, wide)
    given = [] if base is None else [base]

    def body(table_ref, *refs):
        pair_refs, refs = refs[: len(pairs)], refs[len(pairs) :]
        kept_refs, refs = refs[: len(kept)], refs[len(kept) :]
        base_refs, refs = refs[: len(given)], refs[len(given) :]
        if blocks:
            *outs, total, held, sems = refs
        else:
            total, held, sems = refs
        i = pl.program_id(0)
        fetch(i, pairs, pair_refs, held, sems)

        @pl.when(i == 0)
        def _():
            total[...] = base_refs[0][...] if given else jnp.zeros(total_shape, F32)

        right = share_block(kept_refs, table_ref[at + i], by_rows)
        total[...] += contract(held[i], right, 1, 0 if by_rows else 1)

        if blocks:

            @pl.when(i == steps - 1)
            def _():
                rows = tokens // blocks
                for k, out in enumerate(outs):
                    out[...] = total[k * rows : (k + 1) * rows, :].astype(BF16)

    scratch = [
        pltpu.VMEM((steps, tokens, share), BF16),
        pltpu.SemaphoreType.DMA((len(pairs),)),
    ]
    if blocks:
        out_shape = (jax.ShapeDtypeStruct((tokens // blocks, wide), BF16),) * blocks
        out_specs = (whole(out_shape[0]),) * blocks
        scratch.insert(0, pltpu.VMEM(total_shape, F32))
    else:
        out_shape = jax.ShapeDtypeStruct(total_shape, F32)
        out_specs = whole(out_shape)
    call = pl.pallas_call(
        body,
        out_shape=out_shape,
        grid_spec=pltpu.PrefetchScalarGridSpec(
            num_scalar_prefetch=1,
            grid=(steps,),
            in_specs=[pl.BlockSpec(memory_space=pl.ANY)] * len(pairs)
            + [resident()] * len(kept)
            + [whole(array) for array in given],
            out_specs=out_specs,
            scratch_shapes=scratch,
        ),
        compiler_params=params(),
        cost_estimate=cost(
            2 * tokens * share * wide * steps,
            2 * share * (wide + tokens) * steps + 4 * tokens * wide,
        ),
    )
    return call(table, *pairs, *map(in_vmem, kept), *given)


def weight_gradient(table, at, pairs, parts, keep, shape, by_rows, into=None):
    tokens = sum(part[0].shape[0] for part in parts)
    share = pairs[0].shape[2]
    wide = parts[0][0].shape[1]
    count = len(flat(parts))
    steps = 2 * len(pairs)
    block = (share, wide) if by_rows else (wide, share)
    given = [] if into is None else [into]

    def body(table_ref, *refs):
        pair_refs, refs = refs[: len(pairs)], refs[len(pairs) :]
        part_refs, refs = refs[:count], refs[count:]
        keep_ref, *_, out, made, held, other, sems, out_sems = refs
        i = pl.program_id(0)
        slot = i % 2

        def copy(step):
            start = pl.multiple_of(table_ref[at + step] * share, TILE)
            if by_rows:
                target = out.at[pl.ds(start, share)]
            else:
                target = out.at[:, pl.ds(start, share)]
            return pltpu.make_async_copy(made.at[step % 2], target, out_sems.at[step % 2])

        @pl.when(i == 0)
        def _():
            values = parts_of(part_refs, parts)
            if by_rows:
                stack(other, values)
            else:
                other[...] = jnp.concatenate(values).T

        fetch(i, pairs, pair_refs, held, sems)

        @pl.when(i >= 2)
        def _():
            copy(i - 2).wait()

        left = held[i].T if by_rows else other
        right = other[...] if by_rows else held[i]
        span = 2 * TILE
        for lo in range(0, block[0], span):
            term = contract(left[lo : lo + span, :], right, 1, 0)
            for k in range(0, span, TILE):
                tile = (lo + k) // TILE
                made[slot, lo + k : lo + k + TILE, :] = (
                    term[k : k + TILE].astype(BF16) * keep_ref[tile : tile + 1, :]
                )
        copy(i).start()

        @pl.when(i == steps - 1)
        def _():
            copy(i - 1).wait()
            copy(i).wait()

    call = pl.pallas_call(
        body,
        out_shape=jax.ShapeDtypeStruct(shape, BF16),
        grid_spec=pltpu.PrefetchScalarGridSpec(
            num_scalar_prefetch=1,
            grid=(steps,),
            in_specs=[pl.BlockSpec(memory_space=pl.ANY)] * len(pairs)
            + [whole(array) for array in flat(parts)]
            + [pl.BlockSpec((None,) + keep.shape[1:], lambda i, t: (t[at + i], 0, 0))]
            + [pl.BlockSpec(memory_space=pl.ANY)] * len(given),
            out_specs=pl.BlockSpec(memory_space=pl.ANY),
            scratch_shapes=[
                pltpu.VMEM((2,) + block, BF16),
                pltpu.VMEM((steps, tokens, share), BF16),
                pltpu.VMEM((tokens, wide) if by_rows else (wide, tokens), BF16),
                pltpu.SemaphoreType.DMA((len(pairs),)),
                pltpu.SemaphoreType.DMA((2,)),
            ],
        ),
        input_output_aliases={2 + len(pairs) + count: 0} if given else {},
        compiler_params=params(),
        cost_estimate=cost(
            2 * tokens * share * wide * steps, 2 * share * (wide + tokens) * steps
        ),
    )
    return call(table, *pairs, *flat(parts), keep, *given)


def per_device_tuned(n_row, n_col, inputs, w_up, w_down, mask_up, mask_down, cotangent):
    share = w_up.shape[1] // n_row
    table = share_table(lax.axis_index("row"))
    keep_up = jnp.repeat(mask_up.astype(BF16), TILE, axis=1)
    keep_up = keep_up.reshape(-1, n_row, share).transpose(1, 0, 2)
    keep_down = jnp.repeat(mask_down.astype(BF16), TILE, axis=1)
    keep_down = keep_down.reshape(n_row, share // TILE, -1)

    def between_cores(value):
        return lax.ppermute(value, "row", [(i, i ^ CORE) for i in range(n_row)])

    def along_first(value):
        return lax.ppermute(value, "row", [(i, i ^ first_of(i)) for i in range(n_row)])

    def along_second(value):
        second = [(X | Y) - first_of(i) for i in range(n_row)]
        return lax.ppermute(value, "row", [(i, i ^ second[i]) for i in range(n_row)])

    def along_col(value, shift):
        return lax.ppermute(value, "col", [(i, (i + shift) % n_col) for i in range(n_col)])

    def toward(value, step, froms):
        return lax.ppermute(value, "col", [(i, i + step) for i in froms])

    def relayed(lower, upper):
        return toward(upper, -1, (1, 2)), toward(lower, 1, (1, 2))

    def after(value, *done):
        return lax.optimization_barrier((value, *done))[0]

    def together(*values):
        return lax.optimization_barrier(values)

    def col_sum(blocks):
        return [blocks[0]] + [along_col(blocks[k], -k) for k in range(1, n_col)]

    features = range(0, w_up.shape[0], PIECE)
    middle = len(features) // 2
    keep_up, keep_down, table = together(keep_up, keep_down, table)
    lower, upper = along_col(inputs, 1), along_col(inputs, -1)
    up = kept_pieces(w_up, keep_up, n_row, False, features)
    lower, upper, *up = together(lower, upper, *up)
    far = relayed(lower, upper)
    down = kept_pieces(w_down, after(keep_down, lower), n_row, True, features[:middle])
    far_lower, far_upper, *down = together(*far, *down)
    inputs_all = [(inputs,), (lower,), (far_lower, far_upper), (upper,)]

    cot = after(cotangent, far_lower)
    lower, upper = along_col(cot, 1), along_col(cot, -1)
    up_sent, up_held = project(
        after(table, *down), (AT_SENT, AT_HELD), inputs_all, up, False
    )
    lower, upper, up_sent, up_held = together(lower, upper, up_sent, up_held)
    far = relayed(lower, upper)
    cot_all = [(cotangent,), (lower,), far, (upper,)]
    pair, rest = add_cores(up_held, between_cores(up_sent))

    near = along_first(pair)
    down += kept_pieces(w_down, after(keep_down, pair), n_row, True, features[middle:])
    back_sent, back_held = project(
        after(table, *down), (AT_SENT, AT_HELD), cot_all, down, True
    )
    near, back_sent, back_held = together(near, back_sent, back_held)
    passed, own = add_first(rest, near)
    last = along_second(passed)
    back_got = between_cores(after(back_sent, passed))
    back_pair, back_rest = add_cores(back_held, back_got)
    last, back_pair = together(last, back_pair)
    near = along_first(back_pair)
    hidden, act = activated(own, last)

    act_first = along_first(act)
    passed, own = add_first(back_rest, after(near, act))
    last = along_second(passed)
    act_near = paired(act, after(act_first, passed))
    act_far = along_second(act_near)
    act_core = between_cores(act_near)

    def grad_down_of(start, at, pairs, into=None):
        return weight_gradient(
            after(table, start), at, pairs, cot_all, keep_down, w_down.shape, True, into
        )

    grad_down = grad_down_of(act_near, AT_NEAR, [act_near])
    last, grad_down = together(last, grad_down)
    grad = pulled(hidden, own, last)

    grad_first = along_first(grad)
    out_total = gathered(
        after(table, grad), AT_NEAR, [act_near, act_core], down, True
    )
    grad_first, out_total = together(grad_first, out_total)
    grad_near = paired(grad, grad_first)
    grad_far = along_second(grad_near)
    grad_core = between_cores(grad_near)
    act_far_core = between_cores(after(act_far, grad_near))
    grad_down = grad_down_of(grad_near, AT_NEAR_CORE, [act_core], grad_down)
    out_blocks = gathered(
        after(table, grad_down), AT_FAR, [act_far, act_far_core], down, True, out_total, n_col
    )
    out_terms = col_sum(out_blocks)
    in_total = gathered(
        after(table, out_blocks[0]), AT_NEAR, [grad_near, grad_core], up, False
    )
    grad_far, in_total = together(grad_far, in_total)
    grad_far_core = between_cores(grad_far)
    in_total = gathered(table, AT_FAR, [grad_far], up, False, in_total)
    in_blocks = gathered(table, AT_FAR_CORE, [grad_far_core], up, False, in_total, n_col)

    in_terms = col_sum(in_blocks)
    grad_down = grad_down_of(in_blocks[0], AT_FAR, [act_far, act_far_core], grad_down)
    grad_up = weight_gradient(
        after(table, grad_down),
        AT_NEAR,
        [grad_near, grad_core, grad_far, grad_far_core],
        inputs_all,
        keep_up,
        w_up.shape,
        False,
    )
    out_terms[1:] = together(*out_terms[1:], grad_up)[:-1]
    outputs = added(out_terms)
    grad_inputs = added(in_terms)
    return (outputs, grad_inputs, grad_up, grad_down)


def solution(mesh):
    in_specs = (
        P("col", "row"),
        P("row", "col"),
        P("col", "row"),
        P("row", "col"),
        P("col", "row"),
        P("col", "row"),
    )
    out_specs = (P("col", "row"), P("col", "row"), P("row", "col"), P("col", "row"))
    n_row, n_col = mesh.shape["row"], mesh.shape["col"]

    def per_device(inputs, w_up, w_down, mask_up, mask_down, cotangent):
        fits = n_row == 8 and n_col == 4 and mask_up.shape[1] % n_row == 0 and w_up.shape[0] % PIECE == 0
        plan = functools.partial(per_device_tuned, n_row, n_col) if fits else per_device_plain
        return plan(inputs, w_up, w_down, mask_up, mask_down, cotangent)

    return jax.shard_map(
        per_device, mesh=mesh, in_specs=in_specs, out_specs=out_specs, check_vma=False
    )
```

```python
import functools

import jax
import jax.numpy as jnp
from jax import lax
from jax.experimental import pallas as pl
from jax.experimental.pallas import tpu as pltpu
from jax.sharding import PartitionSpec as P

TILE = 128
VMEM_LIMIT = 11 << 20
PIECE = 256
F32 = jnp.float32
BF16 = jnp.bfloat16


def smooth_gate(value):
    return jax.nn.gelu(value, approximate=True)


def contract(left, right, left_dim, right_dim):
    return lax.dot_general(
        left, right, (((left_dim,), (right_dim,)), ((), ())), preferred_element_type=F32
    )


def apply_mask(weight, mask):
    rows, cols = mask.shape
    tile = weight.shape[0] // rows
    shaped = weight.reshape(rows, tile, cols, tile)
    keep = mask[:, None, :, None].astype(weight.dtype)
    return (shaped * keep).reshape(weight.shape)


def activate(hidden, grad_act):
    act = smooth_gate(hidden).astype(BF16)
    _, pull = jax.vjp(smooth_gate, hidden)
    grad_hidden = pull(grad_act)[0].astype(BF16)
    return (act, grad_hidden)


def per_device_plain(inputs, w_up, w_down, mask_up, mask_down, cotangent):
    up_kept = apply_mask(w_up, mask_up)
    down_kept = apply_mask(w_down, mask_down)
    inputs_all, cot_all = (
        lax.all_gather(inputs, "col", axis=0, tiled=True),
        lax.all_gather(cotangent, "col", axis=0, tiled=True),
    )
    up_part = jnp.dot(inputs_all, up_kept, preferred_element_type=F32)
    back_part = contract(cot_all, down_kept, 1, 1)
    hidden, grad_act = (
        lax.psum_scatter(
            part.astype(BF16), "row", scatter_dimension=0, tiled=True
        ).astype(F32)
        for part in (up_part, back_part)
    )
    act, grad_hidden = activate(hidden, grad_act)
    act_all, grad_all = (
        lax.all_gather(act, "row", axis=0, tiled=True),
        lax.all_gather(grad_hidden, "row", axis=0, tiled=True),
    )
    out_part = jnp.dot(act_all, down_kept, preferred_element_type=F32)
    input_part = contract(grad_all, up_kept, 1, 1)
    outputs, grad_inputs = (
        lax.psum_scatter(
            part.astype(BF16), "col", scatter_dimension=0, tiled=True
        ).astype(F32)
        for part in (out_part, input_part)
    )
    grad_down = apply_mask(contract(act_all, cot_all, 0, 0).astype(BF16), mask_down)
    grad_up = apply_mask(contract(inputs_all, grad_all, 0, 0).astype(BF16), mask_up)
    return (outputs.astype(BF16), grad_inputs.astype(BF16), grad_up, grad_down)


CORE, X, Y = 1, 2, 4


def first_of(row):
    return X if row % 2 == 0 else Y


AT_SENT, AT_HELD, AT_NEAR, AT_FAR = 0, 4, 8, 12
AT_NEAR_CORE, AT_FAR_CORE = 10, 14


def share_table(row):
    first = jnp.where(row % 2 == 0, X, Y)
    second = (X | Y) - first
    other = row ^ CORE
    sent = [other ^ first ^ second, other ^ second, other ^ first, other]
    held = [row ^ first ^ second, row ^ first, row ^ second, row]
    near = [row, row ^ first, other, other ^ second]
    far = [row ^ second, row ^ second ^ first, other ^ first, other ^ first ^ second]
    return jnp.stack(sent + held + near + far)


def cost(flops, moved):
    return pl.CostEstimate(flops=int(flops) // 1000, bytes_accessed=int(moved) // 1000, transcendentals=0)


def params():
    return pltpu.CompilerParams(
        dimension_semantics=("arbitrary",), vmem_limit_bytes=VMEM_LIMIT
    )


def whole(array):
    return pl.BlockSpec(array.shape, lambda i, t: (0,) * len(array.shape))


def resident():
    return pl.BlockSpec(memory_space=pltpu.VMEM)


def in_vmem(array):
    return pltpu.with_memory_space_constraint(array, pltpu.VMEM)


def flat(parts):
    return [array for part in parts for array in part]


def parts_of(refs, parts):
    refs = iter(refs)
    return [functools.reduce(jnp.add, [next(refs)[...] for _ in part]) for part in parts]


def stack(dst, values):
    row = 0
    for value in values:
        dst[row : row + value.shape[0], :] = value
        row += value.shape[0]


def small(body, outs, *given):
    specs = tuple(resident() for _ in outs)
    return pl.pallas_call(
        body,
        out_shape=tuple(pltpu.VMEM(shape, dtype) for shape, dtype in outs),
        in_specs=[resident()] * len(given),
        out_specs=specs,
        compiler_params=pltpu.CompilerParams(vmem_limit_bytes=VMEM_LIMIT),
    )(*[in_vmem(array) for array in given])


def add_cores(held, got):
    _, tokens, share = held.shape

    def body(held_ref, got_ref, pair, rest):
        for k in range(4):
            total = held_ref[k].astype(F32) + got_ref[k].astype(F32)
            if k < 2:
                pair[k] = total.astype(BF16)
            else:
                rest[k - 2] = total

    shape = (2, tokens, share)
    return small(body, [(shape, BF16), (shape, F32)], held, got)


def add_first(rest, near):
    _, tokens, share = rest.shape

    def body(rest_ref, near_ref, passed, own):
        passed[...] = (rest_ref[0] + near_ref[0].astype(F32)).astype(BF16)
        own[...] = rest_ref[1] + near_ref[1].astype(F32)

    return small(body, [((tokens, share), BF16), ((tokens, share), F32)], rest, near)


def activated(own, last):
    def body(own_ref, last_ref, hidden, act):
        value = own_ref[...] + last_ref[...].astype(F32)
        hidden[...] = value
        act[...] = smooth_gate(value).astype(BF16)

    return small(body, [(own.shape, F32), (own.shape, BF16)], own, last)


def pulled(hidden, own, last):
    def body(hidden_ref, own_ref, last_ref, grad):
        _, pull = jax.vjp(smooth_gate, hidden_ref[...])
        grad[...] = pull(own_ref[...] + last_ref[...].astype(F32))[0].astype(BF16)

    return small(body, [(own.shape, BF16)], hidden, own, last)[0]


def paired(left, right):
    def body(left_ref, right_ref, pair):
        pair[0] = left_ref[...]
        pair[1] = right_ref[...]

    return small(body, [((2,) + left.shape, BF16)], left, right)[0]


def added(terms):
    def body(*refs):
        *given, out = refs
        out[...] = functools.reduce(jnp.add, [ref[...].astype(F32) for ref in given]).astype(BF16)

    return pl.pallas_call(
        body,
        out_shape=jax.ShapeDtypeStruct(terms[0].shape, BF16),
        compiler_params=pltpu.CompilerParams(vmem_limit_bytes=VMEM_LIMIT),
    )(*terms)


def kept_pieces(weight, keep, shares, by_rows, pieces):
    rows, columns = weight.shape
    share = (rows if by_rows else columns) // shares
    block = (share, PIECE) if by_rows else (PIECE, share)

    def body(weight_ref, keep_ref, *refs):
        *outs, sems = refs

        def copies(n):
            start = pl.multiple_of(n * share, TILE)
            for h, lo in enumerate(pieces):
                if by_rows:
                    source = weight_ref.at[pl.ds(start, share), pl.ds(lo, PIECE)]
                else:
                    source = weight_ref.at[pl.ds(lo, PIECE), pl.ds(start, share)]
                yield pltpu.make_async_copy(source, outs[h].at[n], sems.at[n, h])

        for n in range(shares):
            for copy in copies(n):
                copy.start()

        @pl.loop(0, shares)
        def _(n):
            for copy in copies(n):
                copy.wait()
            for lo, out in zip(pieces, outs):
                for k in range(0, block[0], TILE):
                    strip = slice(k, k + TILE)
                    if by_rows:
                        kept = keep_ref[n, k // TILE : k // TILE + 1, lo : lo + PIECE]
                    else:
                        tile = (lo + k) // TILE
                        kept = keep_ref[n, tile : tile + 1, :]
                    out[n, strip, :] = out[n, strip, :] * kept

    return pl.pallas_call(
        body,
        out_shape=(pltpu.VMEM((shares,) + block, BF16),) * len(pieces),
        in_specs=[pl.BlockSpec(memory_space=pltpu.HBM), resident()],
        out_specs=(resident(),) * len(pieces),
        scratch_shapes=[pltpu.SemaphoreType.DMA((shares, len(pieces)))],
        compiler_params=pltpu.CompilerParams(vmem_limit_bytes=VMEM_LIMIT),
        cost_estimate=cost(rows * columns, 4 * rows * columns),
    )(pltpu.with_memory_space_constraint(weight, pltpu.HBM), keep)


def share_block(kept_refs, share, by_rows):
    return jnp.concatenate([ref[share] for ref in kept_refs], axis=1 if by_rows else 0)


def project(table, ats, parts, kept, by_rows):
    tokens = sum(part[0].shape[0] for part in parts)
    wide = parts[0][0].shape[1]
    share = kept[0].shape[1 if by_rows else 2]
    count = len(flat(parts))

    def body(table_ref, *refs):
        part_refs, refs = refs[:count], refs[count:]
        kept_refs, (*outs, held) = refs[: len(kept)], refs[len(kept) :]
        i = pl.program_id(0)

        @pl.when(i == 0)
        def _():
            stack(held, parts_of(part_refs, parts))

        right = share_block(kept_refs, table_ref[ats[0] + i], by_rows)
        result = contract(held[...], right, 1, 1 if by_rows else 0).astype(BF16)
        for n, out in enumerate(outs):

            @pl.when(i // 4 == n)
            def _(out=out):
                out[...] = result

    def place(n):
        return lambda i, t: (jnp.clip(i - 4 * n, 0, 3), 0, 0)

    call = pl.pallas_call(
        body,
        out_shape=(jax.ShapeDtypeStruct((4, tokens, share), BF16),) * len(ats),
        grid_spec=pltpu.PrefetchScalarGridSpec(
            num_scalar_prefetch=1,
            grid=(4 * len(ats),),
            in_specs=[whole(array) for array in flat(parts)] + [resident()] * len(kept),
            out_specs=tuple(
                pl.BlockSpec((None, tokens, share), place(n)) for n in range(len(ats))
            ),
            scratch_shapes=[pltpu.VMEM((tokens, wide), BF16)],
        ),
        compiler_params=params(),
        cost_estimate=cost(
            8 * tokens * wide * share * len(ats),
            2 * (4 * len(ats) * share * (wide + tokens) + tokens * wide),
        ),
    )
    return call(table, *flat(parts), *map(in_vmem, kept))


def fetch(i, pairs, refs, held, sems):
    copies = [
        pltpu.make_async_copy(ref, held.at[pl.ds(2 * n, 2)], sems.at[n])
        for n, ref in enumerate(refs)
    ]

    @pl.when(i == 0)
    def _():
        for copy in copies:
            copy.start()

    for n, copy in enumerate(copies):

        @pl.when(i == 2 * n)
        def _(copy=copy):
            copy.wait()


def gathered(table, at, pairs, kept, by_rows, base=None, blocks=0):
    _, tokens, share = pairs[0].shape
    steps = 2 * len(pairs)
    wide = len(kept) * PIECE
    total_shape = (tokens, wide)
    given = [] if base is None else [base]

    def body(table_ref, *refs):
        pair_refs, refs = refs[: len(pairs)], refs[len(pairs) :]
        kept_refs, refs = refs[: len(kept)], refs[len(kept) :]
        base_refs, refs = refs[: len(given)], refs[len(given) :]
        if blocks:
            *outs, total, held, sems = refs
        else:
            total, held, sems = refs
        i = pl.program_id(0)
        fetch(i, pairs, pair_refs, held, sems)

        @pl.when(i == 0)
        def _():
            total[...] = base_refs[0][...] if given else jnp.zeros(total_shape, F32)

        right = share_block(kept_refs, table_ref[at + i], by_rows)
        total[...] += contract(held[i], right, 1, 0 if by_rows else 1)

        if blocks:

            @pl.when(i == steps - 1)
            def _():
                rows = tokens // blocks
                for k, out in enumerate(outs):
                    out[...] = total[k * rows : (k + 1) * rows, :].astype(BF16)

    scratch = [
        pltpu.VMEM((steps, tokens, share), BF16),
        pltpu.SemaphoreType.DMA((len(pairs),)),
    ]
    if blocks:
        out_shape = (jax.ShapeDtypeStruct((tokens // blocks, wide), BF16),) * blocks
        out_specs = (whole(out_shape[0]),) * blocks
        scratch.insert(0, pltpu.VMEM(total_shape, F32))
    else:
        out_shape = jax.ShapeDtypeStruct(total_shape, F32)
        out_specs = whole(out_shape)
    call = pl.pallas_call(
        body,
        out_shape=out_shape,
        grid_spec=pltpu.PrefetchScalarGridSpec(
            num_scalar_prefetch=1,
            grid=(steps,),
            in_specs=[pl.BlockSpec(memory_space=pl.ANY)] * len(pairs)
            + [resident()] * len(kept)
            + [whole(array) for array in given],
            out_specs=out_specs,
            scratch_shapes=scratch,
        ),
        compiler_params=params(),
        cost_estimate=cost(
            2 * tokens * share * wide * steps,
            2 * share * (wide + tokens) * steps + 4 * tokens * wide,
        ),
    )
    return call(table, *pairs, *map(in_vmem, kept), *given)


def weight_gradient(table, at, pairs, parts, keep, shape, by_rows, into=None):
    tokens = sum(part[0].shape[0] for part in parts)
    share = pairs[0].shape[2]
    wide = parts[0][0].shape[1]
    count = len(flat(parts))
    steps = 2 * len(pairs)
    block = (share, wide) if by_rows else (wide, share)
    given = [] if into is None else [into]

    def body(table_ref, *refs):
        pair_refs, refs = refs[: len(pairs)], refs[len(pairs) :]
        part_refs, refs = refs[:count], refs[count:]
        keep_ref, *_, out, made, held, other, sems, out_sems = refs
        i = pl.program_id(0)
        slot = i % 2

        def copy(step):
            start = pl.multiple_of(table_ref[at + step] * share, TILE)
            if by_rows:
                target = out.at[pl.ds(start, share)]
            else:
                target = out.at[:, pl.ds(start, share)]
            return pltpu.make_async_copy(made.at[step % 2], target, out_sems.at[step % 2])

        @pl.when(i == 0)
        def _():
            values = parts_of(part_refs, parts)
            if by_rows:
                stack(other, values)
            else:
                other[...] = jnp.concatenate(values).T

        fetch(i, pairs, pair_refs, held, sems)

        @pl.when(i >= 2)
        def _():
            copy(i - 2).wait()

        left = held[i].T if by_rows else other
        right = other[...] if by_rows else held[i]
        span = 2 * TILE
        for lo in range(0, block[0], span):
            term = contract(left[lo : lo + span, :], right, 1, 0)
            for k in range(0, span, TILE):
                tile = (lo + k) // TILE
                made[slot, lo + k : lo + k + TILE, :] = (
                    term[k : k + TILE].astype(BF16) * keep_ref[tile : tile + 1, :]
                )
        copy(i).start()

        @pl.when(i == steps - 1)
        def _():
            copy(i - 1).wait()
            copy(i).wait()

    call = pl.pallas_call(
        body,
        out_shape=jax.ShapeDtypeStruct(shape, BF16),
        grid_spec=pltpu.PrefetchScalarGridSpec(
            num_scalar_prefetch=1,
            grid=(steps,),
            in_specs=[pl.BlockSpec(memory_space=pl.ANY)] * len(pairs)
            + [whole(array) for array in flat(parts)]
            + [pl.BlockSpec((None,) + keep.shape[1:], lambda i, t: (t[at + i], 0, 0))]
            + [pl.BlockSpec(memory_space=pl.ANY)] * len(given),
            out_specs=pl.BlockSpec(memory_space=pl.ANY),
            scratch_shapes=[
                pltpu.VMEM((2,) + block, BF16),
                pltpu.VMEM((steps, tokens, share), BF16),
                pltpu.VMEM((tokens, wide) if by_rows else (wide, tokens), BF16),
                pltpu.SemaphoreType.DMA((len(pairs),)),
                pltpu.SemaphoreType.DMA((2,)),
            ],
        ),
        input_output_aliases={2 + len(pairs) + count: 0} if given else {},
        compiler_params=params(),
        cost_estimate=cost(
            2 * tokens * share * wide * steps, 2 * share * (wide + tokens) * steps
        ),
    )
    return call(table, *pairs, *flat(parts), keep, *given)


def per_device_tuned(n_row, n_col, inputs, w_up, w_down, mask_up, mask_down, cotangent):
    share = w_up.shape[1] // n_row
    table = share_table(lax.axis_index("row"))
    keep_up = jnp.repeat(mask_up.astype(BF16), TILE, axis=1)
    keep_up = keep_up.reshape(-1, n_row, share).transpose(1, 0, 2)
    keep_down = jnp.repeat(mask_down.astype(BF16), TILE, axis=1)
    keep_down = keep_down.reshape(n_row, share // TILE, -1)

    def between_cores(value):
        return lax.ppermute(value, "row", [(i, i ^ CORE) for i in range(n_row)])

    def along_first(value):
        return lax.ppermute(value, "row", [(i, i ^ first_of(i)) for i in range(n_row)])

    def along_second(value):
        second = [(X | Y) - first_of(i) for i in range(n_row)]
        return lax.ppermute(value, "row", [(i, i ^ second[i]) for i in range(n_row)])

    def along_col(value, shift):
        return lax.ppermute(value, "col", [(i, (i + shift) % n_col) for i in range(n_col)])

    def toward(value, step, froms):
        return lax.ppermute(value, "col", [(i, i + step) for i in froms])

    def relayed(lower, upper):
        return toward(upper, -1, (1, 2)), toward(lower, 1, (1, 2))

    def after(value, *done):
        return lax.optimization_barrier((value, *done))[0]

    def together(*values):
        return lax.optimization_barrier(values)

    def col_sum(blocks):
        return [blocks[0]] + [along_col(blocks[k], -k) for k in range(1, n_col)]

    features = range(0, w_up.shape[0], PIECE)
    middle = len(features) // 2
    keep_up, keep_down, table = together(keep_up, keep_down, table)
    lower, upper = along_col(inputs, 1), along_col(inputs, -1)
    up = kept_pieces(w_up, keep_up, n_row, False, features)
    lower, upper, *up = together(lower, upper, *up)
    far = relayed(lower, upper)
    down = kept_pieces(w_down, after(keep_down, lower), n_row, True, features[:middle])
    far_lower, far_upper, *down = together(*far, *down)
    inputs_all = [(inputs,), (lower,), (far_lower, far_upper), (upper,)]

    cot = after(cotangent, far_lower)
    lower, upper = along_col(cot, 1), along_col(cot, -1)
    up_sent, up_held = project(
        after(table, *down), (AT_SENT, AT_HELD), inputs_all, up, False
    )
    lower, upper, up_sent, up_held = together(lower, upper, up_sent, up_held)
    far = relayed(lower, upper)
    pair, rest = add_cores(up_held, between_cores(up_sent))

    near = along_first(pair)
    down += kept_pieces(w_down, after(keep_down, pair), n_row, True, features[middle:])
    near, far_lower, far_upper, *down = together(near, *far, *down)
    cot_all = [(cotangent,), (lower,), (far_lower, far_upper), (upper,)]
    passed, own = add_first(rest, near)
    last = along_second(passed)
    back_sent, back_held = project(
        after(table, passed), (AT_SENT, AT_HELD), cot_all, down, True
    )
    last, back_sent, back_held = together(last, back_sent, back_held)
    hidden, act = activated(own, last)

    act_first = along_first(act)
    back_pair, rest = add_cores(after(back_held, act), between_cores(back_sent))
    near = along_first(back_pair)
    act_near = paired(act, after(act_first, back_pair))
    act_far = along_second(act_near)
    act_core = between_cores(act_near)

    def grad_down_of(start, at, pairs, into=None):
        return weight_gradient(
            after(table, start), at, pairs, cot_all, keep_down, w_down.shape, True, into
        )

    grad_down = grad_down_of(act_near, AT_NEAR, [act_near])
    out_total = gathered(
        after(table, grad_down), AT_NEAR, [act_near, act_core], down, True
    )
    near, out_total = together(near, out_total)
    passed, own = add_first(rest, near)
    last = along_second(passed)
    act_far_core = between_cores(after(act_far, passed))
    grad_down = grad_down_of(passed, AT_NEAR_CORE, [act_core], grad_down)
    last, grad_down = together(last, grad_down)
    grad = pulled(hidden, own, last)

    grad_first = along_first(grad)
    out_blocks = gathered(
        after(table, grad), AT_FAR, [act_far, act_far_core], down, True, out_total, n_col
    )
    grad_first, *out_blocks = together(grad_first, *out_blocks)
    out_terms = col_sum(out_blocks)
    grad_near = paired(grad, grad_first)
    grad_far = along_second(grad_near)
    grad_core = between_cores(grad_near)
    in_total = gathered(table, AT_NEAR, [grad_near, grad_core], up, False)
    grad_far, in_total, out_terms[1], out_terms[3] = together(
        grad_far, in_total, out_terms[1], out_terms[3]
    )
    grad_far_core = between_cores(grad_far)
    in_total = gathered(table, AT_FAR, [grad_far], up, False, in_total)
    in_blocks = gathered(table, AT_FAR_CORE, [grad_far_core], up, False, in_total, n_col)

    in_terms = col_sum(in_blocks)
    grad_down = grad_down_of(in_blocks[0], AT_FAR, [act_far, act_far_core], grad_down)
    grad_up = weight_gradient(
        after(table, grad_down),
        AT_NEAR,
        [grad_near, grad_core, grad_far, grad_far_core],
        inputs_all,
        keep_up,
        w_up.shape,
        False,
    )
    out_terms[1:] = together(*out_terms[1:], grad_up)[:-1]
    outputs = added(out_terms)
    grad_inputs = added(in_terms)
    return (outputs, grad_inputs, grad_up, grad_down)


def solution(mesh):
    in_specs = (
        P("col", "row"),
        P("row", "col"),
        P("col", "row"),
        P("row", "col"),
        P("col", "row"),
        P("col", "row"),
    )
    out_specs = (P("col", "row"), P("col", "row"), P("row", "col"), P("col", "row"))
    n_row, n_col = mesh.shape["row"], mesh.shape["col"]

    def per_device(inputs, w_up, w_down, mask_up, mask_down, cotangent):
        fits = n_row == 8 and n_col == 4 and mask_up.shape[1] % n_row == 0 and w_up.shape[0] % PIECE == 0
        plan = functools.partial(per_device_tuned, n_row, n_col) if fits else per_device_plain
        return plan(inputs, w_up, w_down, mask_up, mask_down, cotangent)

    return jax.shard_map(
        per_device, mesh=mesh, in_specs=in_specs, out_specs=out_specs, check_vma=False
    )
```

```python
import functools

import jax
import jax.numpy as jnp
from jax import lax
from jax.experimental import pallas as pl
from jax.experimental.pallas import tpu as pltpu
from jax.sharding import PartitionSpec as P

TILE = 128
VMEM_LIMIT = 11 << 20
PIECE = 256
F32 = jnp.float32
BF16 = jnp.bfloat16


def smooth_gate(value):
    return jax.nn.gelu(value, approximate=True)


def contract(left, right, left_dim, right_dim):
    return lax.dot_general(
        left, right, (((left_dim,), (right_dim,)), ((), ())), preferred_element_type=F32
    )


def apply_mask(weight, mask):
    rows, cols = mask.shape
    tile = weight.shape[0] // rows
    shaped = weight.reshape(rows, tile, cols, tile)
    keep = mask[:, None, :, None].astype(weight.dtype)
    return (shaped * keep).reshape(weight.shape)


def activate(hidden, grad_act):
    act = smooth_gate(hidden).astype(BF16)
    _, pull = jax.vjp(smooth_gate, hidden)
    grad_hidden = pull(grad_act)[0].astype(BF16)
    return (act, grad_hidden)


def per_device_plain(inputs, w_up, w_down, mask_up, mask_down, cotangent):
    up_kept = apply_mask(w_up, mask_up)
    down_kept = apply_mask(w_down, mask_down)
    inputs_all, cot_all = (
        lax.all_gather(inputs, "col", axis=0, tiled=True),
        lax.all_gather(cotangent, "col", axis=0, tiled=True),
    )
    up_part = jnp.dot(inputs_all, up_kept, preferred_element_type=F32)
    back_part = contract(cot_all, down_kept, 1, 1)
    hidden, grad_act = (
        lax.psum_scatter(
            part.astype(BF16), "row", scatter_dimension=0, tiled=True
        ).astype(F32)
        for part in (up_part, back_part)
    )
    act, grad_hidden = activate(hidden, grad_act)
    act_all, grad_all = (
        lax.all_gather(act, "row", axis=0, tiled=True),
        lax.all_gather(grad_hidden, "row", axis=0, tiled=True),
    )
    out_part = jnp.dot(act_all, down_kept, preferred_element_type=F32)
    input_part = contract(grad_all, up_kept, 1, 1)
    outputs, grad_inputs = (
        lax.psum_scatter(
            part.astype(BF16), "col", scatter_dimension=0, tiled=True
        ).astype(F32)
        for part in (out_part, input_part)
    )
    grad_down = apply_mask(contract(act_all, cot_all, 0, 0).astype(BF16), mask_down)
    grad_up = apply_mask(contract(inputs_all, grad_all, 0, 0).astype(BF16), mask_up)
    return (outputs.astype(BF16), grad_inputs.astype(BF16), grad_up, grad_down)


CORE, X, Y = 1, 2, 4


def first_of(row):
    return X if row % 2 == 0 else Y


AT_SENT, AT_HELD, AT_NEAR, AT_FAR = 0, 4, 8, 12
AT_NEAR_CORE, AT_FAR_CORE = 10, 14


def share_table(row):
    first = jnp.where(row % 2 == 0, X, Y)
    second = (X | Y) - first
    other = row ^ CORE
    sent = [other ^ first ^ second, other ^ second, other ^ first, other]
    held = [row ^ first ^ second, row ^ first, row ^ second, row]
    near = [row, row ^ first, other, other ^ second]
    far = [row ^ second, row ^ second ^ first, other ^ first, other ^ first ^ second]
    return jnp.stack(sent + held + near + far)


def cost(flops, moved):
    return pl.CostEstimate(flops=int(flops) // 1000, bytes_accessed=int(moved) // 1000, transcendentals=0)


def params():
    return pltpu.CompilerParams(
        dimension_semantics=("arbitrary",), vmem_limit_bytes=VMEM_LIMIT
    )


def whole(array):
    return pl.BlockSpec(array.shape, lambda i, t: (0,) * len(array.shape))


def resident():
    return pl.BlockSpec(memory_space=pltpu.VMEM)


def in_vmem(array):
    return pltpu.with_memory_space_constraint(array, pltpu.VMEM)


def flat(parts):
    return [array for part in parts for array in part]


def parts_of(refs, parts):
    refs = iter(refs)
    return [functools.reduce(jnp.add, [next(refs)[...] for _ in part]) for part in parts]


def stack(dst, values):
    row = 0
    for value in values:
        dst[row : row + value.shape[0], :] = value
        row += value.shape[0]


def small(body, outs, *given):
    specs = tuple(resident() for _ in outs)
    return pl.pallas_call(
        body,
        out_shape=tuple(pltpu.VMEM(shape, dtype) for shape, dtype in outs),
        in_specs=[resident()] * len(given),
        out_specs=specs,
        compiler_params=pltpu.CompilerParams(vmem_limit_bytes=VMEM_LIMIT),
    )(*[in_vmem(array) for array in given])


def add_cores(held, got):
    _, tokens, share = held.shape

    def body(held_ref, got_ref, pair, rest):
        for k in range(4):
            total = held_ref[k].astype(F32) + got_ref[k].astype(F32)
            if k < 2:
                pair[k] = total.astype(BF16)
            else:
                rest[k - 2] = total

    shape = (2, tokens, share)
    return small(body, [(shape, BF16), (shape, F32)], held, got)


def add_first(rest, near):
    _, tokens, share = rest.shape

    def body(rest_ref, near_ref, passed, own):
        passed[...] = (rest_ref[0] + near_ref[0].astype(F32)).astype(BF16)
        own[...] = rest_ref[1] + near_ref[1].astype(F32)

    return small(body, [((tokens, share), BF16), ((tokens, share), F32)], rest, near)


def activated(own, last):
    def body(own_ref, last_ref, hidden, act):
        value = own_ref[...] + last_ref[...].astype(F32)
        hidden[...] = value
        act[...] = smooth_gate(value).astype(BF16)

    return small(body, [(own.shape, F32), (own.shape, BF16)], own, last)


def pulled(hidden, own, last):
    def body(hidden_ref, own_ref, last_ref, grad):
        _, pull = jax.vjp(smooth_gate, hidden_ref[...])
        grad[...] = pull(own_ref[...] + last_ref[...].astype(F32))[0].astype(BF16)

    return small(body, [(own.shape, BF16)], hidden, own, last)[0]


def paired(left, right):
    def body(left_ref, right_ref, pair):
        pair[0] = left_ref[...]
        pair[1] = right_ref[...]

    return small(body, [((2,) + left.shape, BF16)], left, right)[0]


def added(terms):
    def body(*refs):
        *given, out = refs
        out[...] = functools.reduce(jnp.add, [ref[...].astype(F32) for ref in given]).astype(BF16)

    return pl.pallas_call(
        body,
        out_shape=jax.ShapeDtypeStruct(terms[0].shape, BF16),
        compiler_params=pltpu.CompilerParams(vmem_limit_bytes=VMEM_LIMIT),
    )(*terms)


def kept_pieces(weight, keep, shares, by_rows, pieces):
    rows, columns = weight.shape
    share = (rows if by_rows else columns) // shares
    block = (share, PIECE) if by_rows else (PIECE, share)

    def body(weight_ref, keep_ref, *refs):
        *outs, sems = refs

        def copies(n):
            start = pl.multiple_of(n * share, TILE)
            for h, lo in enumerate(pieces):
                if by_rows:
                    source = weight_ref.at[pl.ds(start, share), pl.ds(lo, PIECE)]
                else:
                    source = weight_ref.at[pl.ds(lo, PIECE), pl.ds(start, share)]
                yield pltpu.make_async_copy(source, outs[h].at[n], sems.at[n, h])

        for n in range(shares):
            for copy in copies(n):
                copy.start()

        @pl.loop(0, shares)
        def _(n):
            for copy in copies(n):
                copy.wait()
            for lo, out in zip(pieces, outs):
                for k in range(0, block[0], TILE):
                    strip = slice(k, k + TILE)
                    if by_rows:
                        kept = keep_ref[n, k // TILE : k // TILE + 1, lo : lo + PIECE]
                    else:
                        tile = (lo + k) // TILE
                        kept = keep_ref[n, tile : tile + 1, :]
                    out[n, strip, :] = out[n, strip, :] * kept

    return pl.pallas_call(
        body,
        out_shape=(pltpu.VMEM((shares,) + block, BF16),) * len(pieces),
        in_specs=[pl.BlockSpec(memory_space=pltpu.HBM), resident()],
        out_specs=(resident(),) * len(pieces),
        scratch_shapes=[pltpu.SemaphoreType.DMA((shares, len(pieces)))],
        compiler_params=pltpu.CompilerParams(vmem_limit_bytes=VMEM_LIMIT),
        cost_estimate=cost(rows * columns, 4 * rows * columns),
    )(pltpu.with_memory_space_constraint(weight, pltpu.HBM), keep)


def share_block(kept_refs, share, by_rows):
    return jnp.concatenate([ref[share] for ref in kept_refs], axis=1 if by_rows else 0)


def project(table, ats, parts, kept, by_rows):
    tokens = sum(part[0].shape[0] for part in parts)
    wide = parts[0][0].shape[1]
    share = kept[0].shape[1 if by_rows else 2]
    count = len(flat(parts))

    def body(table_ref, *refs):
        part_refs, refs = refs[:count], refs[count:]
        kept_refs, (*outs, held) = refs[: len(kept)], refs[len(kept) :]
        i = pl.program_id(0)

        @pl.when(i == 0)
        def _():
            stack(held, parts_of(part_refs, parts))

        right = share_block(kept_refs, table_ref[ats[0] + i], by_rows)
        result = contract(held[...], right, 1, 1 if by_rows else 0).astype(BF16)
        for n, out in enumerate(outs):

            @pl.when(i // 4 == n)
            def _(out=out):
                out[...] = result

    def place(n):
        return lambda i, t: (jnp.clip(i - 4 * n, 0, 3), 0, 0)

    call = pl.pallas_call(
        body,
        out_shape=(jax.ShapeDtypeStruct((4, tokens, share), BF16),) * len(ats),
        grid_spec=pltpu.PrefetchScalarGridSpec(
            num_scalar_prefetch=1,
            grid=(4 * len(ats),),
            in_specs=[whole(array) for array in flat(parts)] + [resident()] * len(kept),
            out_specs=tuple(
                pl.BlockSpec((None, tokens, share), place(n)) for n in range(len(ats))
            ),
            scratch_shapes=[pltpu.VMEM((tokens, wide), BF16)],
        ),
        compiler_params=params(),
        cost_estimate=cost(
            8 * tokens * wide * share * len(ats),
            2 * (4 * len(ats) * share * (wide + tokens) + tokens * wide),
        ),
    )
    return call(table, *flat(parts), *map(in_vmem, kept))


def fetch(i, pairs, refs, held, sems):
    copies = [
        pltpu.make_async_copy(ref, held.at[pl.ds(2 * n, 2)], sems.at[n])
        for n, ref in enumerate(refs)
    ]

    @pl.when(i == 0)
    def _():
        for copy in copies:
            copy.start()

    for n, copy in enumerate(copies):

        @pl.when(i == 2 * n)
        def _(copy=copy):
            copy.wait()


def gathered(table, at, pairs, kept, by_rows, base=None, blocks=0):
    _, tokens, share = pairs[0].shape
    steps = 2 * len(pairs)
    wide = len(kept) * PIECE
    total_shape = (tokens, wide)
    given = [] if base is None else [base]

    def body(table_ref, *refs):
        pair_refs, refs = refs[: len(pairs)], refs[len(pairs) :]
        kept_refs, refs = refs[: len(kept)], refs[len(kept) :]
        base_refs, refs = refs[: len(given)], refs[len(given) :]
        if blocks:
            *outs, total, held, sems = refs
        else:
            total, held, sems = refs
        i = pl.program_id(0)
        fetch(i, pairs, pair_refs, held, sems)

        @pl.when(i == 0)
        def _():
            total[...] = base_refs[0][...] if given else jnp.zeros(total_shape, F32)

        right = share_block(kept_refs, table_ref[at + i], by_rows)
        total[...] += contract(held[i], right, 1, 0 if by_rows else 1)

        if blocks:

            @pl.when(i == steps - 1)
            def _():
                rows = tokens // blocks
                for k, out in enumerate(outs):
                    out[...] = total[k * rows : (k + 1) * rows, :].astype(BF16)

    scratch = [
        pltpu.VMEM((steps, tokens, share), BF16),
        pltpu.SemaphoreType.DMA((len(pairs),)),
    ]
    if blocks:
        out_shape = (jax.ShapeDtypeStruct((tokens // blocks, wide), BF16),) * blocks
        out_specs = (whole(out_shape[0]),) * blocks
        scratch.insert(0, pltpu.VMEM(total_shape, F32))
    else:
        out_shape = jax.ShapeDtypeStruct(total_shape, F32)
        out_specs = whole(out_shape)
    call = pl.pallas_call(
        body,
        out_shape=out_shape,
        grid_spec=pltpu.PrefetchScalarGridSpec(
            num_scalar_prefetch=1,
            grid=(steps,),
            in_specs=[pl.BlockSpec(memory_space=pl.ANY)] * len(pairs)
            + [resident()] * len(kept)
            + [whole(array) for array in given],
            out_specs=out_specs,
            scratch_shapes=scratch,
        ),
        compiler_params=params(),
        cost_estimate=cost(
            2 * tokens * share * wide * steps,
            2 * share * (wide + tokens) * steps + 4 * tokens * wide,
        ),
    )
    return call(table, *pairs, *map(in_vmem, kept), *given)


def weight_gradient(table, at, pairs, parts, keep, shape, by_rows, into=None):
    tokens = sum(part[0].shape[0] for part in parts)
    share = pairs[0].shape[2]
    wide = parts[0][0].shape[1]
    count = len(flat(parts))
    steps = 2 * len(pairs)
    block = (share, wide) if by_rows else (wide, share)
    given = [] if into is None else [into]

    def body(table_ref, *refs):
        pair_refs, refs = refs[: len(pairs)], refs[len(pairs) :]
        part_refs, refs = refs[:count], refs[count:]
        keep_ref, *_, out, made, held, other, sems, out_sems = refs
        i = pl.program_id(0)
        slot = i % 2

        def copy(step):
            start = pl.multiple_of(table_ref[at + step] * share, TILE)
            if by_rows:
                target = out.at[pl.ds(start, share)]
            else:
                target = out.at[:, pl.ds(start, share)]
            return pltpu.make_async_copy(made.at[step % 2], target, out_sems.at[step % 2])

        @pl.when(i == 0)
        def _():
            values = parts_of(part_refs, parts)
            if by_rows:
                stack(other, values)
            else:
                other[...] = jnp.concatenate(values).T

        fetch(i, pairs, pair_refs, held, sems)

        @pl.when(i >= 2)
        def _():
            copy(i - 2).wait()

        left = held[i].T if by_rows else other
        right = other[...] if by_rows else held[i]
        span = 2 * TILE
        for lo in range(0, block[0], span):
            term = contract(left[lo : lo + span, :], right, 1, 0)
            for k in range(0, span, TILE):
                tile = (lo + k) // TILE
                made[slot, lo + k : lo + k + TILE, :] = (
                    term[k : k + TILE].astype(BF16) * keep_ref[tile : tile + 1, :]
                )
        copy(i).start()

        @pl.when(i == steps - 1)
        def _():
            copy(i - 1).wait()
            copy(i).wait()

    call = pl.pallas_call(
        body,
        out_shape=jax.ShapeDtypeStruct(shape, BF16),
        grid_spec=pltpu.PrefetchScalarGridSpec(
            num_scalar_prefetch=1,
            grid=(steps,),
            in_specs=[pl.BlockSpec(memory_space=pl.ANY)] * len(pairs)
            + [whole(array) for array in flat(parts)]
            + [pl.BlockSpec((None,) + keep.shape[1:], lambda i, t: (t[at + i], 0, 0))]
            + [pl.BlockSpec(memory_space=pl.ANY)] * len(given),
            out_specs=pl.BlockSpec(memory_space=pl.ANY),
            scratch_shapes=[
                pltpu.VMEM((2,) + block, BF16),
                pltpu.VMEM((steps, tokens, share), BF16),
                pltpu.VMEM((tokens, wide) if by_rows else (wide, tokens), BF16),
                pltpu.SemaphoreType.DMA((len(pairs),)),
                pltpu.SemaphoreType.DMA((2,)),
            ],
        ),
        input_output_aliases={2 + len(pairs) + count: 0} if given else {},
        compiler_params=params(),
        cost_estimate=cost(
            2 * tokens * share * wide * steps, 2 * share * (wide + tokens) * steps
        ),
    )
    return call(table, *pairs, *flat(parts), keep, *given)


def per_device_tuned(n_row, n_col, inputs, w_up, w_down, mask_up, mask_down, cotangent):
    share = w_up.shape[1] // n_row
    table = share_table(lax.axis_index("row"))
    keep_up = jnp.repeat(mask_up.astype(BF16), TILE, axis=1)
    keep_up = keep_up.reshape(-1, n_row, share).transpose(1, 0, 2)
    keep_down = jnp.repeat(mask_down.astype(BF16), TILE, axis=1)
    keep_down = keep_down.reshape(n_row, share // TILE, -1)

    def between_cores(value):
        return lax.ppermute(value, "row", [(i, i ^ CORE) for i in range(n_row)])

    def along_first(value):
        return lax.ppermute(value, "row", [(i, i ^ first_of(i)) for i in range(n_row)])

    def along_second(value):
        second = [(X | Y) - first_of(i) for i in range(n_row)]
        return lax.ppermute(value, "row", [(i, i ^ second[i]) for i in range(n_row)])

    def along_col(value, shift):
        return lax.ppermute(value, "col", [(i, (i + shift) % n_col) for i in range(n_col)])

    def toward(value, step, froms):
        return lax.ppermute(value, "col", [(i, i + step) for i in froms])

    def relayed(lower, upper):
        return toward(upper, -1, (1, 2)), toward(lower, 1, (1, 2))

    def after(value, *done):
        return lax.optimization_barrier((value, *done))[0]

    def together(*values):
        return lax.optimization_barrier(values)

    def col_sum(blocks):
        return [blocks[0]] + [along_col(blocks[k], -k) for k in range(1, n_col)]

    features = range(0, w_up.shape[0], PIECE)
    middle = len(features) // 2
    keep_up, keep_down, table = together(keep_up, keep_down, table)
    lower, upper = along_col(inputs, 1), along_col(inputs, -1)
    up = kept_pieces(w_up, keep_up, n_row, False, features)
    lower, upper, *up = together(lower, upper, *up)
    far = relayed(lower, upper)
    down = kept_pieces(w_down, after(keep_down, lower), n_row, True, features[:middle])
    far_lower, far_upper, *down = together(*far, *down)
    inputs_all = [(inputs,), (lower,), (far_lower, far_upper), (upper,)]

    cot = after(cotangent, far_lower)
    lower, upper = along_col(cot, 1), along_col(cot, -1)
    up_sent, up_held = project(
        after(table, *down), (AT_SENT, AT_HELD), inputs_all, up, False
    )
    lower, upper, up_sent, up_held = together(lower, upper, up_sent, up_held)
    far = relayed(lower, upper)
    pair, rest = add_cores(up_held, between_cores(up_sent))

    near = along_first(pair)
    down += kept_pieces(w_down, after(keep_down, pair), n_row, True, features[middle:])
    near, far_lower, far_upper, *down = together(near, *far, *down)
    cot_all = [(cotangent,), (lower,), (far_lower, far_upper), (upper,)]
    passed, own = add_first(rest, near)
    last = along_second(passed)
    back_sent, back_held = project(
        after(table, passed), (AT_SENT, AT_HELD), cot_all, down, True
    )
    last, back_sent, back_held = together(last, back_sent, back_held)
    hidden, act = activated(own, last)

    act_first = along_first(act)
    back_pair, rest = add_cores(after(back_held, act), between_cores(back_sent))
    near = along_first(back_pair)
    act_near = paired(act, after(act_first, back_pair))
    act_far = along_second(act_near)
    act_core = between_cores(act_near)

    def grad_down_of(start, at, pairs, into=None):
        return weight_gradient(
            after(table, start), at, pairs, cot_all, keep_down, w_down.shape, True, into
        )

    grad_down = grad_down_of(act_near, AT_NEAR, [act_near])
    near, grad_down = together(near, grad_down)
    passed, own = add_first(rest, near)
    last = along_second(passed)
    act_core = after(act_core, passed)
    out_total = gathered(table, AT_NEAR, [act_near, act_core], down, True)
    last, out_total = together(last, out_total)
    act_far = after(act_far, out_total)
    act_far_core = between_cores(act_far)
    grad = pulled(hidden, own, last)

    grad_first = along_first(grad)
    grad_down = grad_down_of(grad, AT_NEAR_CORE, [act_core], grad_down)
    out_blocks = gathered(
        after(table, grad_down), AT_FAR, [act_far, act_far_core], down, True, out_total, n_col
    )
    grad_first, grad_down, *out_blocks = together(grad_first, grad_down, *out_blocks)
    out_terms = col_sum(out_blocks)
    grad_near = paired(grad, grad_first)
    grad_far = along_second(grad_near)
    grad_core = between_cores(grad_near)
    in_total = gathered(table, AT_NEAR, [grad_near, grad_core], up, False)
    grad_down = grad_down_of(in_total, AT_FAR, [act_far, act_far_core], grad_down)
    grad_far, in_total, grad_down, out_terms[1], out_terms[3] = together(
        grad_far, in_total, grad_down, out_terms[1], out_terms[3]
    )
    grad_far_core = between_cores(grad_far)
    in_total = gathered(table, AT_FAR, [grad_far], up, False, in_total)
    in_blocks = gathered(table, AT_FAR_CORE, [grad_far_core], up, False, in_total, n_col)

    in_terms = col_sum(in_blocks)
    grad_up = weight_gradient(
        after(table, in_blocks[0]),
        AT_NEAR,
        [grad_near, grad_core, grad_far, grad_far_core],
        inputs_all,
        keep_up,
        w_up.shape,
        False,
    )
    out_terms[1:] = together(*out_terms[1:], grad_up)[:-1]
    outputs = added(out_terms)
    grad_inputs = added(in_terms)
    return (outputs, grad_inputs, grad_up, grad_down)


def solution(mesh):
    in_specs = (
        P("col", "row"),
        P("row", "col"),
        P("col", "row"),
        P("row", "col"),
        P("col", "row"),
        P("col", "row"),
    )
    out_specs = (P("col", "row"), P("col", "row"), P("row", "col"), P("col", "row"))
    n_row, n_col = mesh.shape["row"], mesh.shape["col"]

    def per_device(inputs, w_up, w_down, mask_up, mask_down, cotangent):
        fits = n_row == 8 and n_col == 4 and mask_up.shape[1] % n_row == 0 and w_up.shape[0] % PIECE == 0
        plan = functools.partial(per_device_tuned, n_row, n_col) if fits else per_device_plain
        return plan(inputs, w_up, w_down, mask_up, mask_down, cotangent)

    return jax.shard_map(
        per_device, mesh=mesh, in_specs=in_specs, out_specs=out_specs, check_vma=False
    )
```

```python
import functools

import jax
import jax.numpy as jnp
from jax import lax
from jax.experimental import pallas as pl
from jax.experimental.pallas import tpu as pltpu
from jax.sharding import PartitionSpec as P

TILE = 128
VMEM_LIMIT = 11 << 20
PIECE = 256
F32 = jnp.float32
BF16 = jnp.bfloat16


def smooth_gate(value):
    return jax.nn.gelu(value, approximate=True)


def contract(left, right, left_dim, right_dim):
    return lax.dot_general(
        left, right, (((left_dim,), (right_dim,)), ((), ())), preferred_element_type=F32
    )


def apply_mask(weight, mask):
    rows, cols = mask.shape
    tile = weight.shape[0] // rows
    shaped = weight.reshape(rows, tile, cols, tile)
    keep = mask[:, None, :, None].astype(weight.dtype)
    return (shaped * keep).reshape(weight.shape)


def activate(hidden, grad_act):
    act = smooth_gate(hidden).astype(BF16)
    _, pull = jax.vjp(smooth_gate, hidden)
    grad_hidden = pull(grad_act)[0].astype(BF16)
    return (act, grad_hidden)


def per_device_plain(inputs, w_up, w_down, mask_up, mask_down, cotangent):
    up_kept = apply_mask(w_up, mask_up)
    down_kept = apply_mask(w_down, mask_down)
    inputs_all, cot_all = (
        lax.all_gather(inputs, "col", axis=0, tiled=True),
        lax.all_gather(cotangent, "col", axis=0, tiled=True),
    )
    up_part = jnp.dot(inputs_all, up_kept, preferred_element_type=F32)
    back_part = contract(cot_all, down_kept, 1, 1)
    hidden, grad_act = (
        lax.psum_scatter(
            part.astype(BF16), "row", scatter_dimension=0, tiled=True
        ).astype(F32)
        for part in (up_part, back_part)
    )
    act, grad_hidden = activate(hidden, grad_act)
    act_all, grad_all = (
        lax.all_gather(act, "row", axis=0, tiled=True),
        lax.all_gather(grad_hidden, "row", axis=0, tiled=True),
    )
    out_part = jnp.dot(act_all, down_kept, preferred_element_type=F32)
    input_part = contract(grad_all, up_kept, 1, 1)
    outputs, grad_inputs = (
        lax.psum_scatter(
            part.astype(BF16), "col", scatter_dimension=0, tiled=True
        ).astype(F32)
        for part in (out_part, input_part)
    )
    grad_down = apply_mask(contract(act_all, cot_all, 0, 0).astype(BF16), mask_down)
    grad_up = apply_mask(contract(inputs_all, grad_all, 0, 0).astype(BF16), mask_up)
    return (outputs.astype(BF16), grad_inputs.astype(BF16), grad_up, grad_down)


CORE, X, Y = 1, 2, 4


def first_of(row):
    return X if row % 2 == 0 else Y


AT_SENT, AT_HELD, AT_NEAR, AT_FAR = 0, 4, 8, 12
AT_NEAR_CORE, AT_FAR_CORE = 10, 14


def share_table(row):
    first = jnp.where(row % 2 == 0, X, Y)
    second = (X | Y) - first
    other = row ^ CORE
    sent = [other ^ first ^ second, other ^ second, other ^ first, other]
    held = [row ^ first ^ second, row ^ first, row ^ second, row]
    near = [row, row ^ first, other, other ^ second]
    far = [row ^ second, row ^ second ^ first, other ^ first, other ^ first ^ second]
    return jnp.stack(sent + held + near + far)


def cost(flops, moved):
    return pl.CostEstimate(flops=int(flops) // 1000, bytes_accessed=int(moved) // 1000, transcendentals=0)


def params():
    return pltpu.CompilerParams(
        dimension_semantics=("arbitrary",), vmem_limit_bytes=VMEM_LIMIT
    )


def whole(array):
    return pl.BlockSpec(array.shape, lambda i, t: (0,) * len(array.shape))


def resident():
    return pl.BlockSpec(memory_space=pltpu.VMEM)


def in_vmem(array):
    return pltpu.with_memory_space_constraint(array, pltpu.VMEM)


def flat(parts):
    return [array for part in parts for array in part]


def parts_of(refs, parts):
    refs = iter(refs)
    return [functools.reduce(jnp.add, [next(refs)[...] for _ in part]) for part in parts]


def stack(dst, values):
    row = 0
    for value in values:
        dst[row : row + value.shape[0], :] = value
        row += value.shape[0]


def small(body, outs, *given):
    specs = tuple(resident() for _ in outs)
    return pl.pallas_call(
        body,
        out_shape=tuple(pltpu.VMEM(shape, dtype) for shape, dtype in outs),
        in_specs=[resident()] * len(given),
        out_specs=specs,
        compiler_params=pltpu.CompilerParams(vmem_limit_bytes=VMEM_LIMIT),
    )(*[in_vmem(array) for array in given])


def add_cores(held, got):
    _, tokens, share = held.shape

    def body(held_ref, got_ref, pair, rest):
        for k in range(4):
            total = held_ref[k].astype(F32) + got_ref[k].astype(F32)
            if k < 2:
                pair[k] = total.astype(BF16)
            else:
                rest[k - 2] = total

    shape = (2, tokens, share)
    return small(body, [(shape, BF16), (shape, F32)], held, got)


def add_first(rest, near):
    _, tokens, share = rest.shape

    def body(rest_ref, near_ref, passed, own):
        passed[...] = (rest_ref[0] + near_ref[0].astype(F32)).astype(BF16)
        own[...] = rest_ref[1] + near_ref[1].astype(F32)

    return small(body, [((tokens, share), BF16), ((tokens, share), F32)], rest, near)


def activated(own, last):
    def body(own_ref, last_ref, hidden, act):
        value = own_ref[...] + last_ref[...].astype(F32)
        hidden[...] = value
        act[...] = smooth_gate(value).astype(BF16)

    return small(body, [(own.shape, F32), (own.shape, BF16)], own, last)


def pulled(hidden, own, last):
    def body(hidden_ref, own_ref, last_ref, grad):
        _, pull = jax.vjp(smooth_gate, hidden_ref[...])
        grad[...] = pull(own_ref[...] + last_ref[...].astype(F32))[0].astype(BF16)

    return small(body, [(own.shape, BF16)], hidden, own, last)[0]


def paired(left, right):
    def body(left_ref, right_ref, pair):
        pair[0] = left_ref[...]
        pair[1] = right_ref[...]

    return small(body, [((2,) + left.shape, BF16)], left, right)[0]


def added(terms):
    def body(*refs):
        *given, out = refs
        out[...] = functools.reduce(jnp.add, [ref[...].astype(F32) for ref in given]).astype(BF16)

    return pl.pallas_call(
        body,
        out_shape=jax.ShapeDtypeStruct(terms[0].shape, BF16),
        compiler_params=pltpu.CompilerParams(vmem_limit_bytes=VMEM_LIMIT),
    )(*terms)


def kept_pieces(weight, keep, shares, by_rows, pieces):
    rows, columns = weight.shape
    share = (rows if by_rows else columns) // shares
    block = (share, PIECE) if by_rows else (PIECE, share)

    def body(weight_ref, keep_ref, *refs):
        *outs, sems = refs

        def copies(n):
            start = pl.multiple_of(n * share, TILE)
            for h, lo in enumerate(pieces):
                if by_rows:
                    source = weight_ref.at[pl.ds(start, share), pl.ds(lo, PIECE)]
                else:
                    source = weight_ref.at[pl.ds(lo, PIECE), pl.ds(start, share)]
                yield pltpu.make_async_copy(source, outs[h].at[n], sems.at[n, h])

        for n in range(shares):
            for copy in copies(n):
                copy.start()

        @pl.loop(0, shares)
        def _(n):
            for copy in copies(n):
                copy.wait()
            for lo, out in zip(pieces, outs):
                for k in range(0, block[0], TILE):
                    strip = slice(k, k + TILE)
                    if by_rows:
                        kept = keep_ref[n, k // TILE : k // TILE + 1, lo : lo + PIECE]
                    else:
                        tile = (lo + k) // TILE
                        kept = keep_ref[n, tile : tile + 1, :]
                    out[n, strip, :] = out[n, strip, :] * kept

    return pl.pallas_call(
        body,
        out_shape=(pltpu.VMEM((shares,) + block, BF16),) * len(pieces),
        in_specs=[pl.BlockSpec(memory_space=pltpu.HBM), resident()],
        out_specs=(resident(),) * len(pieces),
        scratch_shapes=[pltpu.SemaphoreType.DMA((shares, len(pieces)))],
        compiler_params=pltpu.CompilerParams(vmem_limit_bytes=VMEM_LIMIT),
        cost_estimate=cost(rows * columns, 4 * rows * columns),
    )(pltpu.with_memory_space_constraint(weight, pltpu.HBM), keep)


def share_block(kept_refs, share, by_rows):
    return jnp.concatenate([ref[share] for ref in kept_refs], axis=1 if by_rows else 0)


def project(table, ats, parts, kept, by_rows):
    tokens = sum(part[0].shape[0] for part in parts)
    wide = parts[0][0].shape[1]
    share = kept[0].shape[1 if by_rows else 2]
    count = len(flat(parts))

    def body(table_ref, *refs):
        part_refs, refs = refs[:count], refs[count:]
        kept_refs, (*outs, held) = refs[: len(kept)], refs[len(kept) :]
        i = pl.program_id(0)

        @pl.when(i == 0)
        def _():
            stack(held, parts_of(part_refs, parts))

        right = share_block(kept_refs, table_ref[ats[0] + i], by_rows)
        result = contract(held[...], right, 1, 1 if by_rows else 0).astype(BF16)
        for n, out in enumerate(outs):

            @pl.when(i // 4 == n)
            def _(out=out):
                out[...] = result

    def place(n):
        return lambda i, t: (jnp.clip(i - 4 * n, 0, 3), 0, 0)

    call = pl.pallas_call(
        body,
        out_shape=(jax.ShapeDtypeStruct((4, tokens, share), BF16),) * len(ats),
        grid_spec=pltpu.PrefetchScalarGridSpec(
            num_scalar_prefetch=1,
            grid=(4 * len(ats),),
            in_specs=[whole(array) for array in flat(parts)] + [resident()] * len(kept),
            out_specs=tuple(
                pl.BlockSpec((None, tokens, share), place(n)) for n in range(len(ats))
            ),
            scratch_shapes=[pltpu.VMEM((tokens, wide), BF16)],
        ),
        compiler_params=params(),
        cost_estimate=cost(
            8 * tokens * wide * share * len(ats),
            2 * (4 * len(ats) * share * (wide + tokens) + tokens * wide),
        ),
    )
    return call(table, *flat(parts), *map(in_vmem, kept))


def fetch(i, pairs, refs, held, sems):
    copies = [
        pltpu.make_async_copy(ref, held.at[pl.ds(2 * n, 2)], sems.at[n])
        for n, ref in enumerate(refs)
    ]

    @pl.when(i == 0)
    def _():
        for copy in copies:
            copy.start()

    for n, copy in enumerate(copies):

        @pl.when(i == 2 * n)
        def _(copy=copy):
            copy.wait()


def gathered(table, at, pairs, kept, by_rows, base=None, blocks=0):
    _, tokens, share = pairs[0].shape
    steps = 2 * len(pairs)
    wide = len(kept) * PIECE
    total_shape = (tokens, wide)
    given = [] if base is None else [base]

    def body(table_ref, *refs):
        pair_refs, refs = refs[: len(pairs)], refs[len(pairs) :]
        kept_refs, refs = refs[: len(kept)], refs[len(kept) :]
        base_refs, refs = refs[: len(given)], refs[len(given) :]
        if blocks:
            *outs, total, held, sems = refs
        else:
            total, held, sems = refs
        i = pl.program_id(0)
        fetch(i, pairs, pair_refs, held, sems)

        @pl.when(i == 0)
        def _():
            total[...] = base_refs[0][...] if given else jnp.zeros(total_shape, F32)

        right = share_block(kept_refs, table_ref[at + i], by_rows)
        total[...] += contract(held[i], right, 1, 0 if by_rows else 1)

        if blocks:

            @pl.when(i == steps - 1)
            def _():
                rows = tokens // blocks
                for k, out in enumerate(outs):
                    out[...] = total[k * rows : (k + 1) * rows, :].astype(BF16)

    scratch = [
        pltpu.VMEM((steps, tokens, share), BF16),
        pltpu.SemaphoreType.DMA((len(pairs),)),
    ]
    if blocks:
        out_shape = (jax.ShapeDtypeStruct((tokens // blocks, wide), BF16),) * blocks
        out_specs = (whole(out_shape[0]),) * blocks
        scratch.insert(0, pltpu.VMEM(total_shape, F32))
    else:
        out_shape = jax.ShapeDtypeStruct(total_shape, F32)
        out_specs = whole(out_shape)
    call = pl.pallas_call(
        body,
        out_shape=out_shape,
        grid_spec=pltpu.PrefetchScalarGridSpec(
            num_scalar_prefetch=1,
            grid=(steps,),
            in_specs=[pl.BlockSpec(memory_space=pl.ANY)] * len(pairs)
            + [resident()] * len(kept)
            + [whole(array) for array in given],
            out_specs=out_specs,
            scratch_shapes=scratch,
        ),
        compiler_params=params(),
        cost_estimate=cost(
            2 * tokens * share * wide * steps,
            2 * share * (wide + tokens) * steps + 4 * tokens * wide,
        ),
    )
    return call(table, *pairs, *map(in_vmem, kept), *given)


def weight_gradient(table, at, pairs, parts, keep, shape, by_rows, into=None):
    tokens = sum(part[0].shape[0] for part in parts)
    share = pairs[0].shape[2]
    wide = parts[0][0].shape[1]
    count = len(flat(parts))
    steps = 2 * len(pairs)
    block = (share, wide) if by_rows else (wide, share)
    given = [] if into is None else [into]

    def body(table_ref, *refs):
        pair_refs, refs = refs[: len(pairs)], refs[len(pairs) :]
        part_refs, refs = refs[:count], refs[count:]
        keep_ref, *_, out, made, held, other, sems, out_sems = refs
        i = pl.program_id(0)
        slot = i % 2

        def copy(step):
            start = pl.multiple_of(table_ref[at + step] * share, TILE)
            if by_rows:
                target = out.at[pl.ds(start, share)]
            else:
                target = out.at[:, pl.ds(start, share)]
            return pltpu.make_async_copy(made.at[step % 2], target, out_sems.at[step % 2])

        @pl.when(i == 0)
        def _():
            values = parts_of(part_refs, parts)
            if by_rows:
                stack(other, values)
            else:
                other[...] = jnp.concatenate(values).T

        fetch(i, pairs, pair_refs, held, sems)

        @pl.when(i >= 2)
        def _():
            copy(i - 2).wait()

        left = held[i].T if by_rows else other
        right = other[...] if by_rows else held[i]
        span = 2 * TILE
        for lo in range(0, block[0], span):
            term = contract(left[lo : lo + span, :], right, 1, 0)
            for k in range(0, span, TILE):
                tile = (lo + k) // TILE
                made[slot, lo + k : lo + k + TILE, :] = (
                    term[k : k + TILE].astype(BF16) * keep_ref[tile : tile + 1, :]
                )
        copy(i).start()

        @pl.when(i == steps - 1)
        def _():
            copy(i - 1).wait()
            copy(i).wait()

    call = pl.pallas_call(
        body,
        out_shape=jax.ShapeDtypeStruct(shape, BF16),
        grid_spec=pltpu.PrefetchScalarGridSpec(
            num_scalar_prefetch=1,
            grid=(steps,),
            in_specs=[pl.BlockSpec(memory_space=pl.ANY)] * len(pairs)
            + [whole(array) for array in flat(parts)]
            + [pl.BlockSpec((None,) + keep.shape[1:], lambda i, t: (t[at + i], 0, 0))]
            + [pl.BlockSpec(memory_space=pl.ANY)] * len(given),
            out_specs=pl.BlockSpec(memory_space=pl.ANY),
            scratch_shapes=[
                pltpu.VMEM((2,) + block, BF16),
                pltpu.VMEM((steps, tokens, share), BF16),
                pltpu.VMEM((tokens, wide) if by_rows else (wide, tokens), BF16),
                pltpu.SemaphoreType.DMA((len(pairs),)),
                pltpu.SemaphoreType.DMA((2,)),
            ],
        ),
        input_output_aliases={2 + len(pairs) + count: 0} if given else {},
        compiler_params=params(),
        cost_estimate=cost(
            2 * tokens * share * wide * steps, 2 * share * (wide + tokens) * steps
        ),
    )
    return call(table, *pairs, *flat(parts), keep, *given)


def per_device_tuned(n_row, n_col, inputs, w_up, w_down, mask_up, mask_down, cotangent):
    share = w_up.shape[1] // n_row
    table = share_table(lax.axis_index("row"))
    keep_up = jnp.repeat(mask_up.astype(BF16), TILE, axis=1)
    keep_up = keep_up.reshape(-1, n_row, share).transpose(1, 0, 2)
    keep_down = jnp.repeat(mask_down.astype(BF16), TILE, axis=1)
    keep_down = keep_down.reshape(n_row, share // TILE, -1)

    def between_cores(value):
        return lax.ppermute(value, "row", [(i, i ^ CORE) for i in range(n_row)])

    def along_first(value):
        return lax.ppermute(value, "row", [(i, i ^ first_of(i)) for i in range(n_row)])

    def along_second(value):
        second = [(X | Y) - first_of(i) for i in range(n_row)]
        return lax.ppermute(value, "row", [(i, i ^ second[i]) for i in range(n_row)])

    def along_col(value, shift):
        return lax.ppermute(value, "col", [(i, (i + shift) % n_col) for i in range(n_col)])

    def toward(value, step, froms):
        return lax.ppermute(value, "col", [(i, i + step) for i in froms])

    def relayed(lower, upper):
        return toward(upper, -1, (1, 2)), toward(lower, 1, (1, 2))

    def after(value, *done):
        return lax.optimization_barrier((value, *done))[0]

    def together(*values):
        return lax.optimization_barrier(values)

    def col_sum(blocks):
        return [blocks[0]] + [along_col(blocks[k], -k) for k in range(1, n_col)]

    features = range(0, w_up.shape[0], PIECE)
    keep_up, keep_down, table = together(keep_up, keep_down, table)
    shifts = [along_col(inputs, k) for k in range(1, n_col)]
    up = kept_pieces(w_up, keep_up, n_row, False, features)
    down = kept_pieces(w_down, after(keep_down, up[0]), n_row, True, features)
    shifts, up, down = together(shifts, up, down)
    inputs_all = [(inputs,)] + [(shift,) for shift in shifts]

    cot = after(cotangent, *shifts)
    lower, upper = along_col(cot, 1), along_col(cot, -1)
    up_sent, up_held = project(
        after(table, down[0]), (AT_SENT, AT_HELD), inputs_all, up, False
    )
    lower, upper, up_sent, up_held = together(lower, upper, up_sent, up_held)
    far = relayed(lower, upper)
    pair, rest = add_cores(up_held, between_cores(up_sent))

    near = along_first(pair)
    near, far_lower, far_upper = together(near, *far)
    cot_all = [(cotangent,), (lower,), (far_lower, far_upper), (upper,)]
    passed, own = add_first(rest, near)
    last = along_second(passed)
    back_sent, back_held = project(
        after(table, passed), (AT_SENT, AT_HELD), cot_all, down, True
    )
    last, back_sent, back_held = together(last, back_sent, back_held)
    hidden, act = activated(own, last)

    act_first = along_first(act)
    back_pair, rest = add_cores(after(back_held, act), between_cores(back_sent))
    near = along_first(back_pair)
    act_near = paired(act, after(act_first, back_pair))
    act_far = along_second(act_near)
    act_core = between_cores(act_near)

    def grad_down_of(start, at, pairs, into=None):
        return weight_gradient(
            after(table, start), at, pairs, cot_all, keep_down, w_down.shape, True, into
        )

    grad_down = grad_down_of(act_near, AT_NEAR, [act_near])
    near, grad_down = together(near, grad_down)
    passed, own = add_first(rest, near)
    last = along_second(passed)
    act_core = after(act_core, passed)
    out_total = gathered(table, AT_NEAR, [act_near, act_core], down, True)
    grad_down = grad_down_of(out_total, AT_NEAR_CORE, [act_core], grad_down)
    last, out_total, grad_down = together(last, out_total, grad_down)
    act_far = after(act_far, out_total)
    act_far_core = between_cores(act_far)
    grad = pulled(hidden, own, last)

    grad_first = along_first(grad)
    out_blocks = gathered(
        after(table, grad), AT_FAR, [act_far, act_far_core], down, True, out_total, n_col
    )
    grad_first, *out_blocks = together(grad_first, *out_blocks)
    out_terms = col_sum(out_blocks)
    grad_near = paired(grad, grad_first)
    grad_far = along_second(grad_near)
    grad_core = between_cores(grad_near)
    in_total = gathered(table, AT_NEAR, [grad_near, grad_core], up, False)
    grad_far, in_total, out_terms[1], out_terms[3] = together(
        grad_far, in_total, out_terms[1], out_terms[3]
    )
    grad_far_core = between_cores(grad_far)
    in_total = gathered(table, AT_FAR, [grad_far], up, False, in_total)
    in_blocks = gathered(table, AT_FAR_CORE, [grad_far_core], up, False, in_total, n_col)

    in_terms = col_sum(in_blocks)
    grad_down = grad_down_of(in_blocks[0], AT_FAR, [act_far, act_far_core], grad_down)
    grad_up = weight_gradient(
        after(table, grad_down),
        AT_NEAR,
        [grad_near, grad_core, grad_far, grad_far_core],
        inputs_all,
        keep_up,
        w_up.shape,
        False,
    )
    out_terms[1:] = together(*out_terms[1:], grad_up)[:-1]
    outputs = added(out_terms)
    grad_inputs = added(in_terms)
    return (outputs, grad_inputs, grad_up, grad_down)


def solution(mesh):
    in_specs = (
        P("col", "row"),
        P("row", "col"),
        P("col", "row"),
        P("row", "col"),
        P("col", "row"),
        P("col", "row"),
    )
    out_specs = (P("col", "row"), P("col", "row"), P("row", "col"), P("col", "row"))
    n_row, n_col = mesh.shape["row"], mesh.shape["col"]

    def per_device(inputs, w_up, w_down, mask_up, mask_down, cotangent):
        fits = n_row == 8 and n_col == 4 and mask_up.shape[1] % n_row == 0 and w_up.shape[0] % PIECE == 0
        plan = functools.partial(per_device_tuned, n_row, n_col) if fits else per_device_plain
        return plan(inputs, w_up, w_down, mask_up, mask_down, cotangent)

    return jax.shard_map(
        per_device, mesh=mesh, in_specs=in_specs, out_specs=out_specs, check_vma=False
    )
```

```python
import functools

import jax
import jax.numpy as jnp
from jax import lax
from jax.experimental import pallas as pl
from jax.experimental.pallas import tpu as pltpu
from jax.sharding import PartitionSpec as P

TILE = 128
VMEM_LIMIT = 11 << 20
PIECE = 256
F32 = jnp.float32
BF16 = jnp.bfloat16


def smooth_gate(value):
    return jax.nn.gelu(value, approximate=True)


def contract(left, right, left_dim, right_dim):
    return lax.dot_general(
        left, right, (((left_dim,), (right_dim,)), ((), ())), preferred_element_type=F32
    )


def apply_mask(weight, mask):
    rows, cols = mask.shape
    tile = weight.shape[0] // rows
    shaped = weight.reshape(rows, tile, cols, tile)
    keep = mask[:, None, :, None].astype(weight.dtype)
    return (shaped * keep).reshape(weight.shape)


def activate(hidden, grad_act):
    act = smooth_gate(hidden).astype(BF16)
    _, pull = jax.vjp(smooth_gate, hidden)
    grad_hidden = pull(grad_act)[0].astype(BF16)
    return (act, grad_hidden)


def per_device_plain(inputs, w_up, w_down, mask_up, mask_down, cotangent):
    up_kept = apply_mask(w_up, mask_up)
    down_kept = apply_mask(w_down, mask_down)
    inputs_all, cot_all = (
        lax.all_gather(inputs, "col", axis=0, tiled=True),
        lax.all_gather(cotangent, "col", axis=0, tiled=True),
    )
    up_part = jnp.dot(inputs_all, up_kept, preferred_element_type=F32)
    back_part = contract(cot_all, down_kept, 1, 1)
    hidden, grad_act = (
        lax.psum_scatter(
            part.astype(BF16), "row", scatter_dimension=0, tiled=True
        ).astype(F32)
        for part in (up_part, back_part)
    )
    act, grad_hidden = activate(hidden, grad_act)
    act_all, grad_all = (
        lax.all_gather(act, "row", axis=0, tiled=True),
        lax.all_gather(grad_hidden, "row", axis=0, tiled=True),
    )
    out_part = jnp.dot(act_all, down_kept, preferred_element_type=F32)
    input_part = contract(grad_all, up_kept, 1, 1)
    outputs, grad_inputs = (
        lax.psum_scatter(
            part.astype(BF16), "col", scatter_dimension=0, tiled=True
        ).astype(F32)
        for part in (out_part, input_part)
    )
    grad_down = apply_mask(contract(act_all, cot_all, 0, 0).astype(BF16), mask_down)
    grad_up = apply_mask(contract(inputs_all, grad_all, 0, 0).astype(BF16), mask_up)
    return (outputs.astype(BF16), grad_inputs.astype(BF16), grad_up, grad_down)


CORE, X, Y = 1, 2, 4


def first_of(row):
    return X if row % 2 == 0 else Y


AT_SENT, AT_HELD, AT_NEAR, AT_FAR = 0, 4, 8, 12
AT_NEAR_CORE, AT_FAR_CORE = 10, 14


def spans(length):
    span = 2 * TILE if length % (2 * TILE) == 0 else TILE
    return [slice(lo, lo + span) for lo in range(0, length, span)]


def share_table(row):
    first = jnp.where(row % 2 == 0, X, Y)
    second = (X | Y) - first
    other = row ^ CORE
    sent = [other ^ first ^ second, other ^ second, other ^ first, other]
    held = [row ^ first ^ second, row ^ first, row ^ second, row]
    near = [row, row ^ first, other, other ^ second]
    far = [row ^ second, row ^ second ^ first, other ^ first, other ^ first ^ second]
    return jnp.stack(sent + held + near + far)


def cost(flops, moved):
    return pl.CostEstimate(flops=int(flops) // 1000, bytes_accessed=int(moved) // 1000, transcendentals=0)


def params():
    return pltpu.CompilerParams(
        dimension_semantics=("arbitrary",), vmem_limit_bytes=VMEM_LIMIT
    )


def whole(array):
    return pl.BlockSpec(array.shape, lambda i, t: (0,) * len(array.shape))


def resident():
    return pl.BlockSpec(memory_space=pltpu.VMEM)


def in_vmem(array):
    return pltpu.with_memory_space_constraint(array, pltpu.VMEM)


def flat(parts):
    return [array for part in parts for array in part]


def parts_of(refs, parts):
    refs = iter(refs)
    return [functools.reduce(jnp.add, [next(refs)[...] for _ in part]) for part in parts]


def stack(dst, values):
    row = 0
    for value in values:
        dst[row : row + value.shape[0], :] = value
        row += value.shape[0]


def small(body, outs, *given):
    specs = tuple(resident() for _ in outs)
    return pl.pallas_call(
        body,
        out_shape=tuple(pltpu.VMEM(shape, dtype) for shape, dtype in outs),
        in_specs=[resident()] * len(given),
        out_specs=specs,
        compiler_params=pltpu.CompilerParams(vmem_limit_bytes=VMEM_LIMIT),
    )(*[in_vmem(array) for array in given])


def add_cores(held, got):
    _, tokens, share = held.shape

    def body(held_ref, got_ref, pair, rest):
        for k in range(4):
            total = held_ref[k].astype(F32) + got_ref[k].astype(F32)
            if k < 2:
                pair[k] = total.astype(BF16)
            else:
                rest[k - 2] = total

    shape = (2, tokens, share)
    return small(body, [(shape, BF16), (shape, F32)], held, got)


def add_first(rest, near):
    _, tokens, share = rest.shape

    def body(rest_ref, near_ref, passed, own):
        passed[...] = (rest_ref[0] + near_ref[0].astype(F32)).astype(BF16)
        own[...] = rest_ref[1] + near_ref[1].astype(F32)

    return small(body, [((tokens, share), BF16), ((tokens, share), F32)], rest, near)


def activated(own, last):
    def body(own_ref, last_ref, hidden, act):
        value = own_ref[...] + last_ref[...].astype(F32)
        hidden[...] = value
        act[...] = smooth_gate(value).astype(BF16)

    return small(body, [(own.shape, F32), (own.shape, BF16)], own, last)


def pulled(hidden, own, last):
    def body(hidden_ref, own_ref, last_ref, grad):
        _, pull = jax.vjp(smooth_gate, hidden_ref[...])
        grad[...] = pull(own_ref[...] + last_ref[...].astype(F32))[0].astype(BF16)

    return small(body, [(own.shape, BF16)], hidden, own, last)[0]


def paired(left, right):
    def body(left_ref, right_ref, pair):
        pair[0] = left_ref[...]
        pair[1] = right_ref[...]

    return small(body, [((2,) + left.shape, BF16)], left, right)[0]


def added_pairs(*pairs):
    def body(*refs):
        given, outs = refs[: 2 * len(pairs)], refs[2 * len(pairs) :]
        for n, out in enumerate(outs):
            left, right = given[2 * n : 2 * n + 2]
            out[...] = (left[...].astype(F32) + right[...].astype(F32)).astype(BF16)

    return small(body, [(left.shape, BF16) for left, _ in pairs], *flat(pairs))


def added(terms):
    def body(*refs):
        *given, out = refs
        out[...] = functools.reduce(jnp.add, [ref[...].astype(F32) for ref in given]).astype(BF16)

    return pl.pallas_call(
        body,
        out_shape=jax.ShapeDtypeStruct(terms[0].shape, BF16),
        compiler_params=pltpu.CompilerParams(vmem_limit_bytes=VMEM_LIMIT),
    )(*terms)


def kept_pieces(weight, keep, shares, by_rows, pieces):
    rows, columns = weight.shape
    share = (rows if by_rows else columns) // shares
    block = (share, PIECE) if by_rows else (PIECE, share)

    def body(weight_ref, keep_ref, *refs):
        *outs, sems = refs

        def copies(n):
            start = pl.multiple_of(n * share, TILE)
            for h, lo in enumerate(pieces):
                if by_rows:
                    source = weight_ref.at[pl.ds(start, share), pl.ds(lo, PIECE)]
                else:
                    source = weight_ref.at[pl.ds(lo, PIECE), pl.ds(start, share)]
                yield pltpu.make_async_copy(source, outs[h].at[n], sems.at[n, h])

        for n in range(shares):
            for copy in copies(n):
                copy.start()

        @pl.loop(0, shares)
        def _(n):
            for copy in copies(n):
                copy.wait()
            for lo, out in zip(pieces, outs):
                for k in range(0, block[0], TILE):
                    strip = slice(k, k + TILE)
                    if by_rows:
                        kept = keep_ref[n, k // TILE : k // TILE + 1, lo : lo + PIECE]
                    else:
                        tile = (lo + k) // TILE
                        kept = keep_ref[n, tile : tile + 1, :]
                    out[n, strip, :] = out[n, strip, :] * kept

    return pl.pallas_call(
        body,
        out_shape=(pltpu.VMEM((shares,) + block, BF16),) * len(pieces),
        in_specs=[pl.BlockSpec(memory_space=pltpu.HBM), resident()],
        out_specs=(resident(),) * len(pieces),
        scratch_shapes=[pltpu.SemaphoreType.DMA((shares, len(pieces)))],
        compiler_params=pltpu.CompilerParams(vmem_limit_bytes=VMEM_LIMIT),
        cost_estimate=cost(rows * columns, 4 * rows * columns),
    )(pltpu.with_memory_space_constraint(weight, pltpu.HBM), keep)


def share_block(kept_refs, share, by_rows):
    return jnp.concatenate([ref[share] for ref in kept_refs], axis=1 if by_rows else 0)


def project(table, ats, parts, kept, by_rows):
    tokens = sum(part[0].shape[0] for part in parts)
    wide = parts[0][0].shape[1]
    share = kept[0].shape[1 if by_rows else 2]
    count = len(flat(parts))

    def body(table_ref, *refs):
        part_refs, refs = refs[:count], refs[count:]
        kept_refs, (*outs, held) = refs[: len(kept)], refs[len(kept) :]
        i = pl.program_id(0)

        @pl.when(i == 0)
        def _():
            stack(held, parts_of(part_refs, parts))

        right = share_block(kept_refs, table_ref[ats[0] + i], by_rows)
        result = contract(held[...], right, 1, 1 if by_rows else 0).astype(BF16)
        for n, out in enumerate(outs):

            @pl.when(i // 4 == n)
            def _(out=out):
                out[...] = result

    def place(n):
        return lambda i, t: (jnp.clip(i - 4 * n, 0, 3), 0, 0)

    call = pl.pallas_call(
        body,
        out_shape=(jax.ShapeDtypeStruct((4, tokens, share), BF16),) * len(ats),
        grid_spec=pltpu.PrefetchScalarGridSpec(
            num_scalar_prefetch=1,
            grid=(4 * len(ats),),
            in_specs=[whole(array) for array in flat(parts)] + [resident()] * len(kept),
            out_specs=tuple(
                pl.BlockSpec((None, tokens, share), place(n)) for n in range(len(ats))
            ),
            scratch_shapes=[pltpu.VMEM((tokens, wide), BF16)],
        ),
        compiler_params=params(),
        cost_estimate=cost(
            8 * tokens * wide * share * len(ats),
            2 * (4 * len(ats) * share * (wide + tokens) + tokens * wide),
        ),
    )
    return call(table, *flat(parts), *map(in_vmem, kept))


def fetch(i, pairs, refs, held, sems):
    copies = [
        pltpu.make_async_copy(ref, held.at[pl.ds(2 * n, 2)], sems.at[n])
        for n, ref in enumerate(refs)
    ]

    @pl.when(i == 0)
    def _():
        for copy in copies:
            copy.start()

    for n, copy in enumerate(copies):

        @pl.when(i == 2 * n)
        def _(copy=copy):
            copy.wait()


def gathered(table, at, pairs, kept, by_rows, base=None, blocks=0):
    _, tokens, share = pairs[0].shape
    steps = 2 * len(pairs)
    wide = len(kept) * PIECE
    total_shape = (tokens, wide)
    given = [] if base is None else [base]

    def body(table_ref, *refs):
        pair_refs, refs = refs[: len(pairs)], refs[len(pairs) :]
        kept_refs, refs = refs[: len(kept)], refs[len(kept) :]
        base_refs, refs = refs[: len(given)], refs[len(given) :]
        if blocks:
            *outs, total, held, sems = refs
        else:
            total, held, sems = refs
        i = pl.program_id(0)
        fetch(i, pairs, pair_refs, held, sems)

        @pl.when(i == 0)
        def _():
            total[...] = base_refs[0][...] if given else jnp.zeros(total_shape, F32)

        right = share_block(kept_refs, table_ref[at + i], by_rows)
        total[...] += contract(held[i], right, 1, 0 if by_rows else 1)

        if blocks:

            @pl.when(i == steps - 1)
            def _():
                rows = tokens // blocks
                for k, out in enumerate(outs):
                    out[...] = total[k * rows : (k + 1) * rows, :].astype(BF16)

    scratch = [
        pltpu.VMEM((steps, tokens, share), BF16),
        pltpu.SemaphoreType.DMA((len(pairs),)),
    ]
    if blocks:
        out_shape = (jax.ShapeDtypeStruct((tokens // blocks, wide), BF16),) * blocks
        out_specs = (whole(out_shape[0]),) * blocks
        scratch.insert(0, pltpu.VMEM(total_shape, F32))
    else:
        out_shape = jax.ShapeDtypeStruct(total_shape, F32)
        out_specs = whole(out_shape)
    call = pl.pallas_call(
        body,
        out_shape=out_shape,
        grid_spec=pltpu.PrefetchScalarGridSpec(
            num_scalar_prefetch=1,
            grid=(steps,),
            in_specs=[pl.BlockSpec(memory_space=pl.ANY)] * len(pairs)
            + [resident()] * len(kept)
            + [whole(array) for array in given],
            out_specs=out_specs,
            scratch_shapes=scratch,
        ),
        compiler_params=params(),
        cost_estimate=cost(
            2 * tokens * share * wide * steps,
            2 * share * (wide + tokens) * steps + 4 * tokens * wide,
        ),
    )
    return call(table, *pairs, *map(in_vmem, kept), *given)


def weight_gradient(table, at, pairs, parts, keep, shape, by_rows, into=None):
    tokens = sum(part[0].shape[0] for part in parts)
    share = pairs[0].shape[2]
    wide = parts[0][0].shape[1]
    count = len(flat(parts))
    steps = 2 * len(pairs)
    block = (share, wide) if by_rows else (wide, share)
    given = [] if into is None else [into]

    def body(table_ref, *refs):
        pair_refs, refs = refs[: len(pairs)], refs[len(pairs) :]
        part_refs, refs = refs[:count], refs[count:]
        keep_ref, *_, out, made, held, other, sems, out_sems = refs
        i = pl.program_id(0)
        slot = i % 2

        def copy(step):
            start = pl.multiple_of(table_ref[at + step] * share, TILE)
            if by_rows:
                target = out.at[pl.ds(start, share)]
            else:
                target = out.at[:, pl.ds(start, share)]
            return pltpu.make_async_copy(made.at[step % 2], target, out_sems.at[step % 2])

        @pl.when(i == 0)
        def _():
            values = parts_of(part_refs, parts)
            if by_rows:
                stack(other, values)
            else:
                other[...] = jnp.concatenate(values).T

        fetch(i, pairs, pair_refs, held, sems)

        @pl.when(i >= 2)
        def _():
            copy(i - 2).wait()

        left = held[i].T if by_rows else other
        right = other if by_rows else held.at[i]
        span = share if block[0] % share == 0 else TILE
        for lo in range(0, block[0], span):
            for columns in spans(block[1]):
                term = contract(left[lo : lo + span, :], right[:, columns], 1, 0)
                for k in range(0, span, TILE):
                    tile = (lo + k) // TILE
                    made[slot, lo + k : lo + k + TILE, columns] = (
                        term[k : k + TILE].astype(BF16) * keep_ref[tile : tile + 1, columns]
                    )
        copy(i).start()

        @pl.when(i == steps - 1)
        def _():
            copy(i - 1).wait()
            copy(i).wait()

    call = pl.pallas_call(
        body,
        out_shape=jax.ShapeDtypeStruct(shape, BF16),
        grid_spec=pltpu.PrefetchScalarGridSpec(
            num_scalar_prefetch=1,
            grid=(steps,),
            in_specs=[pl.BlockSpec(memory_space=pl.ANY)] * len(pairs)
            + [whole(array) for array in flat(parts)]
            + [pl.BlockSpec((None,) + keep.shape[1:], lambda i, t: (t[at + i], 0, 0))]
            + [pl.BlockSpec(memory_space=pl.ANY)] * len(given),
            out_specs=pl.BlockSpec(memory_space=pl.ANY),
            scratch_shapes=[
                pltpu.VMEM((2,) + block, BF16),
                pltpu.VMEM((steps, tokens, share), BF16),
                pltpu.VMEM((tokens, wide) if by_rows else (wide, tokens), BF16),
                pltpu.SemaphoreType.DMA((len(pairs),)),
                pltpu.SemaphoreType.DMA((2,)),
            ],
        ),
        input_output_aliases={2 + len(pairs) + count: 0} if given else {},
        compiler_params=params(),
        cost_estimate=cost(
            2 * tokens * share * wide * steps, 2 * share * (wide + tokens) * steps
        ),
    )
    return call(table, *pairs, *flat(parts), keep, *given)


def per_device_tuned(n_row, n_col, inputs, w_up, w_down, mask_up, mask_down, cotangent):
    share = w_up.shape[1] // n_row
    table = share_table(lax.axis_index("row"))
    keep_up = jnp.repeat(mask_up.astype(BF16), TILE, axis=1)
    keep_up = keep_up.reshape(-1, n_row, share).transpose(1, 0, 2)
    keep_down = jnp.repeat(mask_down.astype(BF16), TILE, axis=1)
    keep_down = keep_down.reshape(n_row, share // TILE, -1)

    def between_cores(value):
        return lax.ppermute(value, "row", [(i, i ^ CORE) for i in range(n_row)])

    def along_first(value):
        return lax.ppermute(value, "row", [(i, i ^ first_of(i)) for i in range(n_row)])

    def along_second(value):
        second = [(X | Y) - first_of(i) for i in range(n_row)]
        return lax.ppermute(value, "row", [(i, i ^ second[i]) for i in range(n_row)])

    def along_col(value, shift):
        return lax.ppermute(value, "col", [(i, (i + shift) % n_col) for i in range(n_col)])

    def toward(value, step, froms):
        return lax.ppermute(value, "col", [(i, i + step) for i in froms])

    def relayed(lower, upper):
        return toward(upper, -1, (1, 2)), toward(lower, 1, (1, 2))

    def after(value, *done):
        return lax.optimization_barrier((value, *done))[0]

    def together(*values):
        return lax.optimization_barrier(values)

    def col_sum(blocks):
        return [blocks[0]] + [along_col(blocks[k], -k) for k in range(1, n_col)]

    features = range(0, w_up.shape[0], PIECE)
    keep_up, keep_down, table = together(keep_up, keep_down, table)
    shifts = [along_col(inputs, k) for k in range(1, n_col)]
    up = kept_pieces(w_up, keep_up, n_row, False, features)
    down = kept_pieces(w_down, after(keep_down, up[0]), n_row, True, features)
    shifts, up, down = together(shifts, up, down)
    inputs_all = [(inputs,)] + [(shift,) for shift in shifts]

    cot = after(cotangent, *shifts)
    lower, upper = along_col(cot, 1), along_col(cot, -1)
    up_sent, up_held = project(
        after(table, down[0]), (AT_SENT, AT_HELD), inputs_all, up, False
    )
    lower, upper, up_sent, up_held = together(lower, upper, up_sent, up_held)
    up_got = between_cores(up_sent)
    far = relayed(lower, upper)
    pair, rest = add_cores(up_held, up_got)

    near = along_first(pair)
    near, far_lower, far_upper = together(near, *far)
    cot_all = [(cotangent,), (lower,), (far_lower, far_upper), (upper,)]
    passed, own = add_first(rest, near)
    last = along_second(passed)
    back_sent, back_held = project(
        after(table, passed), (AT_SENT, AT_HELD), cot_all, down, True
    )
    last, back_sent, back_held = together(last, back_sent, back_held)
    hidden, act = activated(own, last)

    act_first = along_first(act)
    back_pair, rest = add_cores(after(back_held, act), between_cores(back_sent))
    near = along_first(back_pair)
    act_near = paired(act, after(act_first, back_pair))
    act_far = along_second(act_near)
    act_core = between_cores(act_near)

    def grad_down_of(start, at, pairs, into=None):
        return weight_gradient(
            after(table, start), at, pairs, cot_all, keep_down, w_down.shape, True, into
        )

    grad_down = grad_down_of(act_near, AT_NEAR, [act_near])
    near, grad_down = together(near, grad_down)
    passed, own = add_first(rest, near)
    last = along_second(passed)
    act_core = after(act_core, passed)
    out_total = gathered(table, AT_NEAR, [act_near, act_core], down, True)
    grad_down = grad_down_of(out_total, AT_NEAR_CORE, [act_core], grad_down)
    last, out_total, grad_down = together(last, out_total, grad_down)
    act_far = after(act_far, out_total)
    act_far_core = between_cores(act_far)
    grad = pulled(hidden, own, last)

    grad_first = along_first(grad)
    out_blocks = gathered(
        after(table, grad), AT_FAR, [act_far, act_far_core], down, True, out_total, n_col
    )
    grad_first, *out_blocks = together(grad_first, *out_blocks)
    hops = toward(out_blocks[2], 1, (0, 1)), toward(out_blocks[2], -1, (2, 3))
    grad_near = paired(grad, grad_first)
    grad_far = along_second(grad_near)
    grad_core = between_cores(grad_near)
    in_total = gathered(table, AT_NEAR, [grad_near, grad_core], up, False)
    *hops, in_total = together(*hops, in_total)
    to_upper, to_lower = added_pairs((out_blocks[3], hops[0]), (out_blocks[1], hops[1]))
    grad_far, in_total, to_upper, to_lower = together(
        grad_far, in_total, to_upper, to_lower
    )
    out_terms = [out_blocks[0], along_col(to_upper, 1), along_col(to_lower, -1)]
    grad_far_core = between_cores(grad_far)
    in_total = gathered(table, AT_FAR, [grad_far], up, False, in_total)
    in_blocks = gathered(table, AT_FAR_CORE, [grad_far_core], up, False, in_total, n_col)

    in_terms = col_sum(in_blocks)
    grad_down = grad_down_of(in_blocks[0], AT_FAR, [act_far, act_far_core], grad_down)
    grad_up = weight_gradient(
        after(table, grad_down),
        AT_NEAR,
        [grad_near, grad_core, grad_far, grad_far_core],
        inputs_all,
        keep_up,
        w_up.shape,
        False,
    )
    out_terms[1:] = together(*out_terms[1:], grad_up)[:-1]
    outputs = added(out_terms)
    grad_inputs = added(in_terms)
    return (outputs, grad_inputs, grad_up, grad_down)


def solution(mesh):
    in_specs = (
        P("col", "row"),
        P("row", "col"),
        P("col", "row"),
        P("row", "col"),
        P("col", "row"),
        P("col", "row"),
    )
    out_specs = (P("col", "row"), P("col", "row"), P("row", "col"), P("col", "row"))
    n_row, n_col = mesh.shape["row"], mesh.shape["col"]

    def per_device(inputs, w_up, w_down, mask_up, mask_down, cotangent):
        fits = n_row == 8 and n_col == 4 and mask_up.shape[1] % n_row == 0 and w_up.shape[0] % PIECE == 0
        plan = functools.partial(per_device_tuned, n_row, n_col) if fits else per_device_plain
        return plan(inputs, w_up, w_down, mask_up, mask_down, cotangent)

    return jax.shard_map(
        per_device, mesh=mesh, in_specs=in_specs, out_specs=out_specs, check_vma=False
    )
```

```python
import functools

import jax
import jax.numpy as jnp
from jax import lax
from jax.experimental import pallas as pl
from jax.experimental.pallas import tpu as pltpu
from jax.sharding import PartitionSpec as P

TILE = 128
VMEM_LIMIT = 11 << 20
TAIL_LIMIT = 24 << 20
PIECE = 256
F32 = jnp.float32
BF16 = jnp.bfloat16


def smooth_gate(value):
    return jax.nn.gelu(value, approximate=True)


def contract(left, right, left_dim, right_dim):
    return lax.dot_general(
        left, right, (((left_dim,), (right_dim,)), ((), ())), preferred_element_type=F32
    )


def apply_mask(weight, mask):
    rows, cols = mask.shape
    tile = weight.shape[0] // rows
    shaped = weight.reshape(rows, tile, cols, tile)
    keep = mask[:, None, :, None].astype(weight.dtype)
    return (shaped * keep).reshape(weight.shape)


def activate(hidden, grad_act):
    act = smooth_gate(hidden).astype(BF16)
    _, pull = jax.vjp(smooth_gate, hidden)
    grad_hidden = pull(grad_act)[0].astype(BF16)
    return (act, grad_hidden)


def per_device_plain(inputs, w_up, w_down, mask_up, mask_down, cotangent):
    up_kept = apply_mask(w_up, mask_up)
    down_kept = apply_mask(w_down, mask_down)
    inputs_all, cot_all = (
        lax.all_gather(inputs, "col", axis=0, tiled=True),
        lax.all_gather(cotangent, "col", axis=0, tiled=True),
    )
    up_part = jnp.dot(inputs_all, up_kept, preferred_element_type=F32)
    back_part = contract(cot_all, down_kept, 1, 1)
    hidden, grad_act = (
        lax.psum_scatter(
            part.astype(BF16), "row", scatter_dimension=0, tiled=True
        ).astype(F32)
        for part in (up_part, back_part)
    )
    act, grad_hidden = activate(hidden, grad_act)
    act_all, grad_all = (
        lax.all_gather(act, "row", axis=0, tiled=True),
        lax.all_gather(grad_hidden, "row", axis=0, tiled=True),
    )
    out_part = jnp.dot(act_all, down_kept, preferred_element_type=F32)
    input_part = contract(grad_all, up_kept, 1, 1)
    outputs, grad_inputs = (
        lax.psum_scatter(
            part.astype(BF16), "col", scatter_dimension=0, tiled=True
        ).astype(F32)
        for part in (out_part, input_part)
    )
    grad_down = apply_mask(contract(act_all, cot_all, 0, 0).astype(BF16), mask_down)
    grad_up = apply_mask(contract(inputs_all, grad_all, 0, 0).astype(BF16), mask_up)
    return (outputs.astype(BF16), grad_inputs.astype(BF16), grad_up, grad_down)


CORE, X, Y = 1, 2, 4


def first_of(row):
    return X if row % 2 == 0 else Y


AT_SENT, AT_HELD, AT_NEAR, AT_FAR = 0, 4, 8, 12
AT_NEAR_CORE = 10


def spans(length):
    span = 2 * TILE if length % (2 * TILE) == 0 else TILE
    return [slice(lo, lo + span) for lo in range(0, length, span)]


def share_table(row):
    first = jnp.where(row % 2 == 0, X, Y)
    second = (X | Y) - first
    other = row ^ CORE
    sent = [other ^ first ^ second, other ^ second, other ^ first, other]
    held = [row ^ first ^ second, row ^ first, row ^ second, row]
    near = [row, row ^ first, other, other ^ second]
    far = [row ^ second, row ^ second ^ first, other ^ first, other ^ first ^ second]
    return jnp.stack(sent + held + near + far)


def cost(flops, moved):
    return pl.CostEstimate(flops=int(flops) // 1000, bytes_accessed=int(moved) // 1000, transcendentals=0)


def params():
    return pltpu.CompilerParams(
        dimension_semantics=("arbitrary",), vmem_limit_bytes=VMEM_LIMIT
    )


def whole(array):
    return pl.BlockSpec(array.shape, lambda i, t: (0,) * len(array.shape))


def resident():
    return pl.BlockSpec(memory_space=pltpu.VMEM)


def in_vmem(array):
    return pltpu.with_memory_space_constraint(array, pltpu.VMEM)


def flat(parts):
    return [array for part in parts for array in part]


def parts_of(refs, parts):
    refs = iter(refs)
    return [functools.reduce(jnp.add, [next(refs)[...] for _ in part]) for part in parts]


def stack(dst, values):
    row = 0
    for value in values:
        dst[row : row + value.shape[0], :] = value
        row += value.shape[0]


def small(body, outs, *given):
    specs = tuple(resident() for _ in outs)
    return pl.pallas_call(
        body,
        out_shape=tuple(pltpu.VMEM(shape, dtype) for shape, dtype in outs),
        in_specs=[resident()] * len(given),
        out_specs=specs,
        compiler_params=pltpu.CompilerParams(vmem_limit_bytes=VMEM_LIMIT),
    )(*[in_vmem(array) for array in given])


def add_cores(held, got):
    _, tokens, share = held.shape

    def body(held_ref, got_ref, pair, rest):
        for k in range(4):
            total = held_ref[k].astype(F32) + got_ref[k].astype(F32)
            if k < 2:
                pair[k] = total.astype(BF16)
            else:
                rest[k - 2] = total

    shape = (2, tokens, share)
    return small(body, [(shape, BF16), (shape, F32)], held, got)


def add_first(rest, near):
    _, tokens, share = rest.shape

    def body(rest_ref, near_ref, passed, own):
        passed[...] = (rest_ref[0] + near_ref[0].astype(F32)).astype(BF16)
        own[...] = rest_ref[1] + near_ref[1].astype(F32)

    return small(body, [((tokens, share), BF16), ((tokens, share), F32)], rest, near)


def activated(own, last):
    def body(own_ref, last_ref, hidden, act):
        value = own_ref[...] + last_ref[...].astype(F32)
        hidden[...] = value
        act[...] = smooth_gate(value).astype(BF16)

    return small(body, [(own.shape, F32), (own.shape, BF16)], own, last)


def pulled(hidden, own, last):
    def body(hidden_ref, own_ref, last_ref, grad):
        _, pull = jax.vjp(smooth_gate, hidden_ref[...])
        grad[...] = pull(own_ref[...] + last_ref[...].astype(F32))[0].astype(BF16)

    return small(body, [(own.shape, BF16)], hidden, own, last)[0]


def paired(left, right):
    def body(left_ref, right_ref, pair):
        pair[0] = left_ref[...]
        pair[1] = right_ref[...]

    return small(body, [((2,) + left.shape, BF16)], left, right)[0]


def added_pairs(*pairs):
    def body(*refs):
        given, outs = refs[: 2 * len(pairs)], refs[2 * len(pairs) :]
        for n, out in enumerate(outs):
            left, right = given[2 * n : 2 * n + 2]
            out[...] = (left[...].astype(F32) + right[...].astype(F32)).astype(BF16)

    return small(body, [(left.shape, BF16) for left, _ in pairs], *flat(pairs))


def added(*sums):
    def body(*refs):
        refs, outs = iter(refs[: -len(sums)]), refs[-len(sums) :]
        for terms, out in zip(sums, outs):
            values = [next(refs)[...].astype(F32) for _ in terms]
            out[...] = functools.reduce(jnp.add, values).astype(BF16)

    return pl.pallas_call(
        body,
        out_shape=tuple(jax.ShapeDtypeStruct(terms[0].shape, BF16) for terms in sums),
        compiler_params=pltpu.CompilerParams(vmem_limit_bytes=VMEM_LIMIT),
    )(*flat(sums))


def kept_pieces(weight, keep, shares, by_rows, pieces):
    rows, columns = weight.shape
    share = (rows if by_rows else columns) // shares
    block = (share, PIECE) if by_rows else (PIECE, share)

    def body(weight_ref, keep_ref, *refs):
        *outs, sems = refs

        def copies(n):
            start = pl.multiple_of(n * share, TILE)
            for h, lo in enumerate(pieces):
                if by_rows:
                    source = weight_ref.at[pl.ds(start, share), pl.ds(lo, PIECE)]
                else:
                    source = weight_ref.at[pl.ds(lo, PIECE), pl.ds(start, share)]
                yield pltpu.make_async_copy(source, outs[h].at[n], sems.at[n, h])

        for n in range(shares):
            for copy in copies(n):
                copy.start()

        @pl.loop(0, shares)
        def _(n):
            for copy in copies(n):
                copy.wait()
            for lo, out in zip(pieces, outs):
                for k in range(0, block[0], TILE):
                    strip = slice(k, k + TILE)
                    if by_rows:
                        kept = keep_ref[n, k // TILE : k // TILE + 1, lo : lo + PIECE]
                    else:
                        tile = (lo + k) // TILE
                        kept = keep_ref[n, tile : tile + 1, :]
                    out[n, strip, :] = out[n, strip, :] * kept

    return pl.pallas_call(
        body,
        out_shape=(pltpu.VMEM((shares,) + block, BF16),) * len(pieces),
        in_specs=[pl.BlockSpec(memory_space=pltpu.HBM), resident()],
        out_specs=(resident(),) * len(pieces),
        scratch_shapes=[pltpu.SemaphoreType.DMA((shares, len(pieces)))],
        compiler_params=pltpu.CompilerParams(vmem_limit_bytes=VMEM_LIMIT),
        cost_estimate=cost(rows * columns, 4 * rows * columns),
    )(pltpu.with_memory_space_constraint(weight, pltpu.HBM), keep)


def share_block(kept_refs, share, by_rows):
    return jnp.concatenate([ref[share] for ref in kept_refs], axis=1 if by_rows else 0)


def project(table, ats, parts, kept, by_rows):
    tokens = sum(part[0].shape[0] for part in parts)
    wide = parts[0][0].shape[1]
    share = kept[0].shape[1 if by_rows else 2]
    count = len(flat(parts))

    def body(table_ref, *refs):
        part_refs, refs = refs[:count], refs[count:]
        kept_refs, (*outs, held) = refs[: len(kept)], refs[len(kept) :]
        i = pl.program_id(0)

        @pl.when(i == 0)
        def _():
            stack(held, parts_of(part_refs, parts))

        right = share_block(kept_refs, table_ref[ats[0] + i], by_rows)
        result = contract(held[...], right, 1, 1 if by_rows else 0).astype(BF16)
        for n, out in enumerate(outs):

            @pl.when(i // 4 == n)
            def _(out=out):
                out[...] = result

    def place(n):
        return lambda i, t: (jnp.clip(i - 4 * n, 0, 3), 0, 0)

    call = pl.pallas_call(
        body,
        out_shape=(jax.ShapeDtypeStruct((4, tokens, share), BF16),) * len(ats),
        grid_spec=pltpu.PrefetchScalarGridSpec(
            num_scalar_prefetch=1,
            grid=(4 * len(ats),),
            in_specs=[whole(array) for array in flat(parts)] + [resident()] * len(kept),
            out_specs=tuple(
                pl.BlockSpec((None, tokens, share), place(n)) for n in range(len(ats))
            ),
            scratch_shapes=[pltpu.VMEM((tokens, wide), BF16)],
        ),
        compiler_params=params(),
        cost_estimate=cost(
            8 * tokens * wide * share * len(ats),
            2 * (4 * len(ats) * share * (wide + tokens) + tokens * wide),
        ),
    )
    return call(table, *flat(parts), *map(in_vmem, kept))


def fetch(i, pairs, refs, held, sems, begin):
    copies = [
        pltpu.make_async_copy(ref, held.at[pl.ds(2 * n, 2)], sems.at[n])
        for n, ref in enumerate(refs)
    ]

    @pl.when(begin)
    def _():
        for copy in copies:
            copy.start()

    for n, copy in enumerate(copies):

        @pl.when(i == 2 * n)
        def _(copy=copy):
            copy.wait()


def gathered(table, at, pairs, kept, by_rows, base=None, blocks=0):
    _, tokens, share = pairs[0].shape
    steps = 2 * len(pairs)
    wide = len(kept) * PIECE
    total_shape = (tokens, wide)
    given = [] if base is None else [base]

    def body(table_ref, *refs):
        pair_refs, refs = refs[: len(pairs)], refs[len(pairs) :]
        kept_refs, refs = refs[: len(kept)], refs[len(kept) :]
        base_refs, refs = refs[: len(given)], refs[len(given) :]
        if blocks:
            *outs, total, held, sems = refs
        else:
            total, held, sems = refs
        i = pl.program_id(0)
        fetch(i, pairs, pair_refs, held, sems, i == 0)

        @pl.when(i == 0)
        def _():
            total[...] = base_refs[0][...] if given else jnp.zeros(total_shape, F32)

        right = share_block(kept_refs, table_ref[at + i], by_rows)
        total[...] += contract(held[i], right, 1, 0 if by_rows else 1)

        if blocks:

            @pl.when(i == steps - 1)
            def _():
                rows = tokens // blocks
                for k, out in enumerate(outs):
                    out[...] = total[k * rows : (k + 1) * rows, :].astype(BF16)

    scratch = [
        pltpu.VMEM((steps, tokens, share), BF16),
        pltpu.SemaphoreType.DMA((len(pairs),)),
    ]
    if blocks:
        out_shape = (jax.ShapeDtypeStruct((tokens // blocks, wide), BF16),) * blocks
        out_specs = (whole(out_shape[0]),) * blocks
        scratch.insert(0, pltpu.VMEM(total_shape, F32))
    else:
        out_shape = jax.ShapeDtypeStruct(total_shape, F32)
        out_specs = whole(out_shape)
    call = pl.pallas_call(
        body,
        out_shape=out_shape,
        grid_spec=pltpu.PrefetchScalarGridSpec(
            num_scalar_prefetch=1,
            grid=(steps,),
            in_specs=[pl.BlockSpec(memory_space=pl.ANY)] * len(pairs)
            + [resident()] * len(kept)
            + [whole(array) for array in given],
            out_specs=out_specs,
            scratch_shapes=scratch,
        ),
        compiler_params=params(),
        cost_estimate=cost(
            2 * tokens * share * wide * steps,
            2 * share * (wide + tokens) * steps + 4 * tokens * wide,
        ),
    )
    return call(table, *pairs, *map(in_vmem, kept), *given)


class Gradient:

    def __init__(self, at, pairs, parts, keep, shape, by_rows, into=None):
        self.at, self.pairs, self.parts, self.keep = at, pairs, parts, keep
        self.shape, self.by_rows = shape, by_rows
        self.given = [] if into is None else [into]
        self.arrays = [*pairs, *flat(parts), keep, *self.given]
        self.steps = 2 * len(pairs)
        self.tokens, self.share = pairs[0].shape[1:]
        self.wide = parts[0][0].shape[1]
        sides = (self.share, self.wide)
        self.block = sides if by_rows else sides[::-1]

    def specs(self, first):
        anywhere = pl.BlockSpec(memory_space=pl.ANY)

        def place(i, t):
            return t[self.at + jnp.clip(i - first, 0, self.steps - 1)], 0, 0

        return (
            [anywhere] * len(self.pairs)
            + [whole(array) for array in flat(self.parts)]
            + [pl.BlockSpec((None,) + self.keep.shape[1:], place)]
            + [anywhere] * len(self.given)
        )

    def scratch(self):
        other = (self.tokens, self.wide) if self.by_rows else (self.wide, self.tokens)
        return [
            pltpu.VMEM((2,) + self.block, BF16),
            pltpu.VMEM((self.steps, self.tokens, self.share), BF16),
            pltpu.VMEM(other, BF16),
            pltpu.SemaphoreType.DMA((len(self.pairs),)),
            pltpu.SemaphoreType.DMA((2,)),
        ]

    def copy(self, table_ref, out, made, out_sems, step):
        start = pl.multiple_of(table_ref[self.at + step] * self.share, TILE)
        target = out.at[pl.ds(start, self.share)] if self.by_rows else out.at[:, pl.ds(start, self.share)]
        return pltpu.make_async_copy(made.at[step % 2], target, out_sems.at[step % 2])

    def run(self, table_ref, refs, out, scratch, i, begin):
        count = len(self.pairs)
        pair_refs, refs = refs[:count], refs[count:]
        count = len(flat(self.parts))
        part_refs, keep_ref = refs[:count], refs[count]
        made, held, other, sems, out_sems = scratch
        fetch(i, self.pairs, pair_refs, held, sems, begin)

        @pl.when(i == 0)
        def _():
            values = parts_of(part_refs, self.parts)
            if self.by_rows:
                stack(other, values)
            else:
                other[...] = jnp.concatenate(values).T

        @pl.when((i >= 2) & (i < self.steps))
        def _():
            self.copy(table_ref, out, made, out_sems, i - 2).wait()

        @pl.when((i >= 0) & (i < self.steps))
        def _():
            left = held[i].T if self.by_rows else other
            right = other if self.by_rows else held.at[i]
            for lo in range(0, self.block[0], self.share):
                for columns in spans(self.block[1]):
                    term = contract(left[lo : lo + self.share, :], right[:, columns], 1, 0)
                    for k in range(0, self.share, TILE):
                        row = lo + k
                        tile = row // TILE
                        made[i % 2, row : row + TILE, columns] = (
                            term[k : k + TILE].astype(BF16) * keep_ref[tile : tile + 1, columns]
                        )
            self.copy(table_ref, out, made, out_sems, i).start()


def weight_gradients(table, jobs, limit=VMEM_LIMIT):
    firsts = [sum(job.steps for job in jobs[:n]) for n in range(len(jobs))]
    steps = sum(job.steps for job in jobs)

    def body(table_ref, *refs):
        refs = list(refs)
        operands = [[refs.pop(0) for _ in job.arrays] for job in jobs]
        outs = [refs.pop(0) for _ in jobs]
        scratch = [[refs.pop(0) for _ in job.scratch()] for job in jobs]
        i = pl.program_id(0)
        for job, first, given, out, own in zip(jobs, firsts, operands, outs, scratch):
            job.run(table_ref, given, out, own, i - first, i == 0)

        @pl.when(i == steps - 1)
        def _():
            for job, out, (made, *_, out_sems) in zip(jobs, outs, scratch):
                for step in (job.steps - 2, job.steps - 1):
                    job.copy(table_ref, out, made, out_sems, step).wait()

    aliases, at = {}, 1
    for n, job in enumerate(jobs):
        at += len(job.arrays)
        if job.given:
            aliases[at - 1] = n
    outs = pl.pallas_call(
        body,
        out_shape=tuple(jax.ShapeDtypeStruct(job.shape, BF16) for job in jobs),
        grid_spec=pltpu.PrefetchScalarGridSpec(
            num_scalar_prefetch=1,
            grid=(steps,),
            in_specs=flat([job.specs(first) for job, first in zip(jobs, firsts)]),
            out_specs=(pl.BlockSpec(memory_space=pl.ANY),) * len(jobs),
            scratch_shapes=flat([job.scratch() for job in jobs]),
        ),
        input_output_aliases=aliases,
        compiler_params=pltpu.CompilerParams(
            dimension_semantics=("arbitrary",), vmem_limit_bytes=limit
        ),
        cost_estimate=cost(
            sum(2 * job.tokens * job.share * job.wide * job.steps for job in jobs),
            sum(2 * job.share * (job.wide + job.tokens) * job.steps for job in jobs),
        ),
    )
    return outs(table, *flat([job.arrays for job in jobs]))


def per_device_tuned(n_row, n_col, inputs, w_up, w_down, mask_up, mask_down, cotangent):
    share = w_up.shape[1] // n_row
    table = share_table(lax.axis_index("row"))
    keep_up = jnp.repeat(mask_up.astype(BF16), TILE, axis=1)
    keep_up = keep_up.reshape(-1, n_row, share).transpose(1, 0, 2)
    keep_down = jnp.repeat(mask_down.astype(BF16), TILE, axis=1)
    keep_down = keep_down.reshape(n_row, share // TILE, -1)

    def between_cores(value):
        return lax.ppermute(value, "row", [(i, i ^ CORE) for i in range(n_row)])

    def along_first(value):
        return lax.ppermute(value, "row", [(i, i ^ first_of(i)) for i in range(n_row)])

    def along_second(value):
        second = [(X | Y) - first_of(i) for i in range(n_row)]
        return lax.ppermute(value, "row", [(i, i ^ second[i]) for i in range(n_row)])

    def along_col(value, shift):
        return lax.ppermute(value, "col", [(i, (i + shift) % n_col) for i in range(n_col)])

    def toward(value, step, froms):
        return lax.ppermute(value, "col", [(i, i + step) for i in froms])

    def relayed(lower, upper):
        return toward(upper, -1, (1, 2)), toward(lower, 1, (1, 2))

    def after(value, *done):
        return lax.optimization_barrier((value, *done))[0]

    def together(*values):
        return lax.optimization_barrier(values)

    def col_sum(blocks):
        return [blocks[0]] + [along_col(blocks[k], -k) for k in range(1, n_col)]

    features = range(0, w_up.shape[0], PIECE)
    keep_up, keep_down, table = together(keep_up, keep_down, table)
    shifts = [along_col(inputs, k) for k in range(1, n_col)]
    up = kept_pieces(w_up, keep_up, n_row, False, features)
    down = kept_pieces(w_down, after(keep_down, up[0]), n_row, True, features)
    shifts, up, down = together(shifts, up, down)
    inputs_all = [(inputs,)] + [(shift,) for shift in shifts]

    cot = after(cotangent, *shifts)
    lower, upper = along_col(cot, 1), along_col(cot, -1)
    up_sent, up_held = project(
        after(table, down[0]), (AT_SENT, AT_HELD), inputs_all, up, False
    )
    lower, upper, up_sent, up_held = together(lower, upper, up_sent, up_held)
    up_got = between_cores(up_sent)
    far = relayed(lower, upper)
    pair, rest = add_cores(up_held, up_got)

    near = along_first(pair)
    near, far_lower, far_upper = together(near, *far)
    cot_all = [(cotangent,), (lower,), (far_lower, far_upper), (upper,)]
    passed, own = add_first(rest, near)
    last = along_second(passed)
    back_sent, back_held = project(
        after(table, passed), (AT_SENT, AT_HELD), cot_all, down, True
    )
    last, back_sent, back_held = together(last, back_sent, back_held)
    hidden, act = activated(own, last)

    act_first = along_first(act)
    back_pair, rest = add_cores(after(back_held, act), between_cores(back_sent))
    near = along_first(back_pair)
    act_near = paired(act, after(act_first, back_pair))
    act_far = along_second(act_near)
    act_core = between_cores(act_near)

    def grad_down_job(at, pairs, into=None):
        return Gradient(at, pairs, cot_all, keep_down, w_down.shape, True, into)

    def grad_down_of(start, *job):
        return weight_gradients(after(table, start), [grad_down_job(*job)])[0]

    grad_down = grad_down_of(act_near, AT_NEAR, [act_near])
    near, grad_down = together(near, grad_down)
    passed, own = add_first(rest, near)
    last = along_second(passed)
    act_core = after(act_core, passed)
    out_total = gathered(table, AT_NEAR, [act_near, act_core], down, True)
    grad_down = grad_down_of(out_total, AT_NEAR_CORE, [act_core], grad_down)
    last, out_total, grad_down = together(last, out_total, grad_down)
    act_far = after(act_far, out_total)
    act_far_core = between_cores(act_far)
    grad = pulled(hidden, own, last)

    grad_first = along_first(grad)
    out_blocks = gathered(
        after(table, grad), AT_FAR, [act_far, act_far_core], down, True, out_total, n_col
    )
    grad_first, *out_blocks = together(grad_first, *out_blocks)
    hops = toward(out_blocks[2], 1, (0, 1)), toward(out_blocks[2], -1, (2, 3))
    grad_near = paired(grad, grad_first)
    grad_far = along_second(grad_near)
    grad_core = between_cores(grad_near)
    in_total = gathered(table, AT_NEAR, [grad_near, grad_core], up, False)
    *hops, in_total = together(*hops, in_total)
    to_upper, to_lower = added_pairs((out_blocks[3], hops[0]), (out_blocks[1], hops[1]))
    grad_far, in_total, to_upper, to_lower = together(
        grad_far, in_total, to_upper, to_lower
    )
    out_terms = [out_blocks[0], along_col(to_upper, 1), along_col(to_lower, -1)]
    grad_far_core = between_cores(grad_far)
    in_blocks = gathered(
        table, AT_FAR, [grad_far, grad_far_core], up, False, in_total, n_col
    )

    in_terms = col_sum(in_blocks)
    grad_down, grad_up = weight_gradients(
        after(table, in_blocks[0]),
        [
            grad_down_job(AT_FAR, [act_far, act_far_core], grad_down),
            Gradient(
                AT_NEAR,
                [grad_near, grad_core, grad_far, grad_far_core],
                inputs_all,
                keep_up,
                w_up.shape,
                False,
            ),
        ],
        TAIL_LIMIT,
    )
    out_terms[1:] = together(*out_terms[1:], grad_up)[:-1]
    outputs, grad_inputs = added(out_terms, in_terms)
    return (outputs, grad_inputs, grad_up, grad_down)


def solution(mesh):
    in_specs = (
        P("col", "row"),
        P("row", "col"),
        P("col", "row"),
        P("row", "col"),
        P("col", "row"),
        P("col", "row"),
    )
    out_specs = (P("col", "row"), P("col", "row"), P("row", "col"), P("col", "row"))
    n_row, n_col = mesh.shape["row"], mesh.shape["col"]

    def per_device(inputs, w_up, w_down, mask_up, mask_down, cotangent):
        fits = n_row == 8 and n_col == 4 and mask_up.shape[1] % n_row == 0 and w_up.shape[0] % PIECE == 0
        plan = functools.partial(per_device_tuned, n_row, n_col) if fits else per_device_plain
        return plan(inputs, w_up, w_down, mask_up, mask_down, cotangent)

    return jax.shard_map(
        per_device, mesh=mesh, in_specs=in_specs, out_specs=out_specs, check_vma=False
    )
```

```python
import functools

import jax
import jax.numpy as jnp
from jax import lax
from jax.experimental import pallas as pl
from jax.experimental.pallas import tpu as pltpu
from jax.sharding import PartitionSpec as P

TILE = 128
VMEM_LIMIT = 11 << 20
TAIL_LIMIT = 24 << 20
PIECE = 256
F32 = jnp.float32
BF16 = jnp.bfloat16


def smooth_gate(value):
    return jax.nn.gelu(value, approximate=True)


def contract(left, right, left_dim, right_dim):
    return lax.dot_general(
        left, right, (((left_dim,), (right_dim,)), ((), ())), preferred_element_type=F32
    )


def apply_mask(weight, mask):
    rows, cols = mask.shape
    tile = weight.shape[0] // rows
    shaped = weight.reshape(rows, tile, cols, tile)
    keep = mask[:, None, :, None].astype(weight.dtype)
    return (shaped * keep).reshape(weight.shape)


def activate(hidden, grad_act):
    act = smooth_gate(hidden).astype(BF16)
    _, pull = jax.vjp(smooth_gate, hidden)
    grad_hidden = pull(grad_act)[0].astype(BF16)
    return (act, grad_hidden)


def per_device_plain(inputs, w_up, w_down, mask_up, mask_down, cotangent):
    up_kept = apply_mask(w_up, mask_up)
    down_kept = apply_mask(w_down, mask_down)
    inputs_all, cot_all = (
        lax.all_gather(inputs, "col", axis=0, tiled=True),
        lax.all_gather(cotangent, "col", axis=0, tiled=True),
    )
    up_part = jnp.dot(inputs_all, up_kept, preferred_element_type=F32)
    back_part = contract(cot_all, down_kept, 1, 1)
    hidden, grad_act = (
        lax.psum_scatter(
            part.astype(BF16), "row", scatter_dimension=0, tiled=True
        ).astype(F32)
        for part in (up_part, back_part)
    )
    act, grad_hidden = activate(hidden, grad_act)
    act_all, grad_all = (
        lax.all_gather(act, "row", axis=0, tiled=True),
        lax.all_gather(grad_hidden, "row", axis=0, tiled=True),
    )
    out_part = jnp.dot(act_all, down_kept, preferred_element_type=F32)
    input_part = contract(grad_all, up_kept, 1, 1)
    outputs, grad_inputs = (
        lax.psum_scatter(
            part.astype(BF16), "col", scatter_dimension=0, tiled=True
        ).astype(F32)
        for part in (out_part, input_part)
    )
    grad_down = apply_mask(contract(act_all, cot_all, 0, 0).astype(BF16), mask_down)
    grad_up = apply_mask(contract(inputs_all, grad_all, 0, 0).astype(BF16), mask_up)
    return (outputs.astype(BF16), grad_inputs.astype(BF16), grad_up, grad_down)


CORE, X, Y = 1, 2, 4


def first_of(row):
    return X if row % 2 == 0 else Y


AT_SENT, AT_HELD, AT_NEAR, AT_FAR = 0, 4, 8, 12
AT_NEAR_CORE = 10
AT_ODD = 16


def spans(length):
    span = 2 * TILE if length % (2 * TILE) == 0 else TILE
    return [slice(lo, lo + span) for lo in range(0, length, span)]


def share_table(row, col):
    first = jnp.where(row % 2 == 0, X, Y)
    second = (X | Y) - first
    other = row ^ CORE
    sent = [other ^ first ^ second, other ^ second, other ^ first, other]
    held = [row ^ first ^ second, row ^ first, row ^ second, row]
    near = [row, row ^ first, other, other ^ second]
    far = [row ^ second, row ^ second ^ first, other ^ first, other ^ first ^ second]
    return jnp.stack(sent + held + near + far + [col % 2])


def cost(flops, moved):
    return pl.CostEstimate(flops=int(flops) // 1000, bytes_accessed=int(moved) // 1000, transcendentals=0)


def params():
    return pltpu.CompilerParams(
        dimension_semantics=("arbitrary",), vmem_limit_bytes=VMEM_LIMIT
    )


def whole(array):
    return pl.BlockSpec(array.shape, lambda i, t: (0,) * len(array.shape))


def resident():
    return pl.BlockSpec(memory_space=pltpu.VMEM)


def in_vmem(array):
    return pltpu.with_memory_space_constraint(array, pltpu.VMEM)


def flat(parts):
    return [array for part in parts for array in part]


def parts_of(refs, parts):
    refs = iter(refs)
    return [functools.reduce(jnp.add, [next(refs)[...] for _ in part]) for part in parts]


def stack(dst, values):
    row = 0
    for value in values:
        dst[row : row + value.shape[0], :] = value
        row += value.shape[0]


def small(body, outs, *given):
    specs = tuple(resident() for _ in outs)
    return pl.pallas_call(
        body,
        out_shape=tuple(pltpu.VMEM(shape, dtype) for shape, dtype in outs),
        in_specs=[resident()] * len(given),
        out_specs=specs,
        compiler_params=pltpu.CompilerParams(vmem_limit_bytes=VMEM_LIMIT),
    )(*[in_vmem(array) for array in given])


def add_cores(held, got):
    _, tokens, share = held.shape

    def body(held_ref, got_ref, pair, rest):
        for k in range(4):
            total = held_ref[k].astype(F32) + got_ref[k].astype(F32)
            if k < 2:
                pair[k] = total.astype(BF16)
            else:
                rest[k - 2] = total

    shape = (2, tokens, share)
    return small(body, [(shape, BF16), (shape, F32)], held, got)


def add_first(rest, near):
    _, tokens, share = rest.shape

    def body(rest_ref, near_ref, passed, own):
        passed[...] = (rest_ref[0] + near_ref[0].astype(F32)).astype(BF16)
        own[...] = rest_ref[1] + near_ref[1].astype(F32)

    return small(body, [((tokens, share), BF16), ((tokens, share), F32)], rest, near)


def activated(own, last):
    def body(own_ref, last_ref, hidden, act):
        value = own_ref[...] + last_ref[...].astype(F32)
        hidden[...] = value
        act[...] = smooth_gate(value).astype(BF16)

    return small(body, [(own.shape, F32), (own.shape, BF16)], own, last)


def pulled(hidden, own, last):
    def body(hidden_ref, own_ref, last_ref, grad):
        _, pull = jax.vjp(smooth_gate, hidden_ref[...])
        grad[...] = pull(own_ref[...] + last_ref[...].astype(F32))[0].astype(BF16)

    return small(body, [(own.shape, BF16)], hidden, own, last)[0]


def paired(left, right):
    def body(left_ref, right_ref, pair):
        pair[0] = left_ref[...]
        pair[1] = right_ref[...]

    return small(body, [((2,) + left.shape, BF16)], left, right)[0]


def by_place(body, table, outs, *given):
    return pl.pallas_call(
        body,
        out_shape=tuple(pltpu.VMEM(shape, BF16) for shape in outs),
        in_specs=[pl.BlockSpec(memory_space=pltpu.SMEM)] + [resident()] * len(given),
        out_specs=tuple(resident() for _ in outs),
        compiler_params=pltpu.CompilerParams(vmem_limit_bytes=VMEM_LIMIT),
    )(table, *[in_vmem(array) for array in given])


def chosen(table, odd, even):
    def body(table_ref, odd_ref, even_ref, out):
        @pl.when(table_ref[AT_ODD] == 1)
        def _():
            out[...] = odd_ref[...]

        @pl.when(table_ref[AT_ODD] == 0)
        def _():
            out[...] = even_ref[...]

    return by_place(body, table, [odd.shape], odd, even)[0]


def joined(table, upper, lower, hop):
    def body(table_ref, upper_ref, lower_ref, hop_ref, to_upper, to_lower):
        def join(out, ref):
            out[...] = (ref[...].astype(F32) + hop_ref[...].astype(F32)).astype(BF16)

        @pl.when(table_ref[AT_ODD] == 1)
        def _():
            join(to_upper, upper_ref)
            to_lower[...] = lower_ref[...]

        @pl.when(table_ref[AT_ODD] == 0)
        def _():
            join(to_lower, lower_ref)
            to_upper[...] = upper_ref[...]

    return by_place(body, table, [upper.shape] * 2, upper, lower, hop)


def added(*sums):
    def body(*refs):
        refs, outs = iter(refs[: -len(sums)]), refs[-len(sums) :]
        for terms, out in zip(sums, outs):
            values = [next(refs)[...].astype(F32) for _ in terms]
            out[...] = functools.reduce(jnp.add, values).astype(BF16)

    return pl.pallas_call(
        body,
        out_shape=tuple(jax.ShapeDtypeStruct(terms[0].shape, BF16) for terms in sums),
        compiler_params=pltpu.CompilerParams(vmem_limit_bytes=VMEM_LIMIT),
    )(*flat(sums))


def kept_pieces(weight, keep, shares, by_rows, pieces):
    rows, columns = weight.shape
    share = (rows if by_rows else columns) // shares
    block = (share, PIECE) if by_rows else (PIECE, share)

    def body(weight_ref, keep_ref, *refs):
        *outs, sems = refs

        def copies(n):
            start = pl.multiple_of(n * share, TILE)
            for h, lo in enumerate(pieces):
                if by_rows:
                    source = weight_ref.at[pl.ds(start, share), pl.ds(lo, PIECE)]
                else:
                    source = weight_ref.at[pl.ds(lo, PIECE), pl.ds(start, share)]
                yield pltpu.make_async_copy(source, outs[h].at[n], sems.at[n, h])

        for n in range(shares):
            for copy in copies(n):
                copy.start()

        @pl.loop(0, shares)
        def _(n):
            for copy in copies(n):
                copy.wait()
            for lo, out in zip(pieces, outs):
                for k in range(0, block[0], TILE):
                    strip = slice(k, k + TILE)
                    if by_rows:
                        kept = keep_ref[n, k // TILE : k // TILE + 1, lo : lo + PIECE]
                    else:
                        tile = (lo + k) // TILE
                        kept = keep_ref[n, tile : tile + 1, :]
                    out[n, strip, :] = out[n, strip, :] * kept

    return pl.pallas_call(
        body,
        out_shape=(pltpu.VMEM((shares,) + block, BF16),) * len(pieces),
        in_specs=[pl.BlockSpec(memory_space=pltpu.HBM), resident()],
        out_specs=(resident(),) * len(pieces),
        scratch_shapes=[pltpu.SemaphoreType.DMA((shares, len(pieces)))],
        compiler_params=pltpu.CompilerParams(vmem_limit_bytes=VMEM_LIMIT),
        cost_estimate=cost(rows * columns, 4 * rows * columns),
    )(pltpu.with_memory_space_constraint(weight, pltpu.HBM), keep)


def share_block(kept_refs, share, by_rows):
    return jnp.concatenate([ref[share] for ref in kept_refs], axis=1 if by_rows else 0)


def project(table, ats, parts, kept, by_rows):
    tokens = sum(part[0].shape[0] for part in parts)
    wide = parts[0][0].shape[1]
    share = kept[0].shape[1 if by_rows else 2]
    count = len(flat(parts))

    def body(table_ref, *refs):
        part_refs, refs = refs[:count], refs[count:]
        kept_refs, (*outs, held) = refs[: len(kept)], refs[len(kept) :]
        i = pl.program_id(0)

        @pl.when(i == 0)
        def _():
            stack(held, parts_of(part_refs, parts))

        right = share_block(kept_refs, table_ref[ats[0] + i], by_rows)
        result = contract(held[...], right, 1, 1 if by_rows else 0).astype(BF16)
        for n, out in enumerate(outs):

            @pl.when(i // 4 == n)
            def _(out=out):
                out[...] = result

    def place(n):
        return lambda i, t: (jnp.clip(i - 4 * n, 0, 3), 0, 0)

    call = pl.pallas_call(
        body,
        out_shape=(jax.ShapeDtypeStruct((4, tokens, share), BF16),) * len(ats),
        grid_spec=pltpu.PrefetchScalarGridSpec(
            num_scalar_prefetch=1,
            grid=(4 * len(ats),),
            in_specs=[whole(array) for array in flat(parts)] + [resident()] * len(kept),
            out_specs=tuple(
                pl.BlockSpec((None, tokens, share), place(n)) for n in range(len(ats))
            ),
            scratch_shapes=[pltpu.VMEM((tokens, wide), BF16)],
        ),
        compiler_params=params(),
        cost_estimate=cost(
            8 * tokens * wide * share * len(ats),
            2 * (4 * len(ats) * share * (wide + tokens) + tokens * wide),
        ),
    )
    return call(table, *flat(parts), *map(in_vmem, kept))


def fetch(i, pairs, refs, held, sems, begin):
    copies = [
        pltpu.make_async_copy(ref, held.at[pl.ds(2 * n, 2)], sems.at[n])
        for n, ref in enumerate(refs)
    ]

    @pl.when(begin)
    def _():
        for copy in copies:
            copy.start()

    for n, copy in enumerate(copies):

        @pl.when(i == 2 * n)
        def _(copy=copy):
            copy.wait()


def gathered(table, at, pairs, kept, by_rows, base=None, blocks=0):
    _, tokens, share = pairs[0].shape
    steps = 2 * len(pairs)
    wide = len(kept) * PIECE
    total_shape = (tokens, wide)
    given = [] if base is None else [base]

    def body(table_ref, *refs):
        pair_refs, refs = refs[: len(pairs)], refs[len(pairs) :]
        kept_refs, refs = refs[: len(kept)], refs[len(kept) :]
        base_refs, refs = refs[: len(given)], refs[len(given) :]
        if blocks:
            *outs, total, held, sems = refs
        else:
            total, held, sems = refs
        i = pl.program_id(0)
        fetch(i, pairs, pair_refs, held, sems, i == 0)

        @pl.when(i == 0)
        def _():
            total[...] = base_refs[0][...] if given else jnp.zeros(total_shape, F32)

        right = share_block(kept_refs, table_ref[at + i], by_rows)
        total[...] += contract(held[i], right, 1, 0 if by_rows else 1)

        if blocks:

            @pl.when(i == steps - 1)
            def _():
                rows = tokens // blocks
                for k, out in enumerate(outs):
                    out[...] = total[k * rows : (k + 1) * rows, :].astype(BF16)

    scratch = [
        pltpu.VMEM((steps, tokens, share), BF16),
        pltpu.SemaphoreType.DMA((len(pairs),)),
    ]
    if blocks:
        out_shape = (jax.ShapeDtypeStruct((tokens // blocks, wide), BF16),) * blocks
        out_specs = (whole(out_shape[0]),) * blocks
        scratch.insert(0, pltpu.VMEM(total_shape, F32))
    else:
        out_shape = jax.ShapeDtypeStruct(total_shape, F32)
        out_specs = whole(out_shape)
    call = pl.pallas_call(
        body,
        out_shape=out_shape,
        grid_spec=pltpu.PrefetchScalarGridSpec(
            num_scalar_prefetch=1,
            grid=(steps,),
            in_specs=[pl.BlockSpec(memory_space=pl.ANY)] * len(pairs)
            + [resident()] * len(kept)
            + [whole(array) for array in given],
            out_specs=out_specs,
            scratch_shapes=scratch,
        ),
        compiler_params=params(),
        cost_estimate=cost(
            2 * tokens * share * wide * steps,
            2 * share * (wide + tokens) * steps + 4 * tokens * wide,
        ),
    )
    return call(table, *pairs, *map(in_vmem, kept), *given)


class Gradient:

    def __init__(self, at, pairs, parts, keep, shape, by_rows, into=None):
        self.at, self.pairs, self.parts, self.keep = at, pairs, parts, keep
        self.shape, self.by_rows = shape, by_rows
        self.given = [] if into is None else [into]
        self.arrays = [*pairs, *flat(parts), keep, *self.given]
        self.steps = 2 * len(pairs)
        self.tokens, self.share = pairs[0].shape[1:]
        self.wide = parts[0][0].shape[1]
        sides = (self.share, self.wide)
        self.block = sides if by_rows else sides[::-1]

    def specs(self, first):
        anywhere = pl.BlockSpec(memory_space=pl.ANY)

        def place(i, t):
            return t[self.at + jnp.clip(i - first, 0, self.steps - 1)], 0, 0

        return (
            [anywhere] * len(self.pairs)
            + [whole(array) for array in flat(self.parts)]
            + [pl.BlockSpec((None,) + self.keep.shape[1:], place)]
            + [anywhere] * len(self.given)
        )

    def scratch(self):
        other = (self.tokens, self.wide) if self.by_rows else (self.wide, self.tokens)
        return [
            pltpu.VMEM((2,) + self.block, BF16),
            pltpu.VMEM((self.steps, self.tokens, self.share), BF16),
            pltpu.VMEM(other, BF16),
            pltpu.SemaphoreType.DMA((len(self.pairs),)),
            pltpu.SemaphoreType.DMA((2,)),
        ]

    def copy(self, table_ref, out, made, out_sems, step):
        start = pl.multiple_of(table_ref[self.at + step] * self.share, TILE)
        target = out.at[pl.ds(start, self.share)] if self.by_rows else out.at[:, pl.ds(start, self.share)]
        return pltpu.make_async_copy(made.at[step % 2], target, out_sems.at[step % 2])

    def run(self, table_ref, refs, out, scratch, i, begin):
        count = len(self.pairs)
        pair_refs, refs = refs[:count], refs[count:]
        count = len(flat(self.parts))
        part_refs, keep_ref = refs[:count], refs[count]
        made, held, other, sems, out_sems = scratch
        fetch(i, self.pairs, pair_refs, held, sems, begin)

        @pl.when(i == 0)
        def _():
            values = parts_of(part_refs, self.parts)
            if self.by_rows:
                stack(other, values)
            else:
                other[...] = jnp.concatenate(values).T

        @pl.when((i >= 2) & (i < self.steps))
        def _():
            self.copy(table_ref, out, made, out_sems, i - 2).wait()

        @pl.when((i >= 0) & (i < self.steps))
        def _():
            left = held[i].T if self.by_rows else other
            right = other if self.by_rows else held.at[i]
            for lo in range(0, self.block[0], self.share):
                for columns in spans(self.block[1]):
                    term = contract(left[lo : lo + self.share, :], right[:, columns], 1, 0)
                    for k in range(0, self.share, TILE):
                        row = lo + k
                        tile = row // TILE
                        made[i % 2, row : row + TILE, columns] = (
                            term[k : k + TILE].astype(BF16) * keep_ref[tile : tile + 1, columns]
                        )
            self.copy(table_ref, out, made, out_sems, i).start()


def weight_gradients(table, jobs, limit=VMEM_LIMIT):
    firsts = [sum(job.steps for job in jobs[:n]) for n in range(len(jobs))]
    steps = sum(job.steps for job in jobs)

    def body(table_ref, *refs):
        refs = list(refs)
        operands = [[refs.pop(0) for _ in job.arrays] for job in jobs]
        outs = [refs.pop(0) for _ in jobs]
        scratch = [[refs.pop(0) for _ in job.scratch()] for job in jobs]
        i = pl.program_id(0)
        for job, first, given, out, own in zip(jobs, firsts, operands, outs, scratch):
            job.run(table_ref, given, out, own, i - first, i == 0)

        @pl.when(i == steps - 1)
        def _():
            for job, out, (made, *_, out_sems) in zip(jobs, outs, scratch):
                for step in (job.steps - 2, job.steps - 1):
                    job.copy(table_ref, out, made, out_sems, step).wait()

    aliases, at = {}, 1
    for n, job in enumerate(jobs):
        at += len(job.arrays)
        if job.given:
            aliases[at - 1] = n
    outs = pl.pallas_call(
        body,
        out_shape=tuple(jax.ShapeDtypeStruct(job.shape, BF16) for job in jobs),
        grid_spec=pltpu.PrefetchScalarGridSpec(
            num_scalar_prefetch=1,
            grid=(steps,),
            in_specs=flat([job.specs(first) for job, first in zip(jobs, firsts)]),
            out_specs=(pl.BlockSpec(memory_space=pl.ANY),) * len(jobs),
            scratch_shapes=flat([job.scratch() for job in jobs]),
        ),
        input_output_aliases=aliases,
        compiler_params=pltpu.CompilerParams(
            dimension_semantics=("arbitrary",), vmem_limit_bytes=limit
        ),
        cost_estimate=cost(
            sum(2 * job.tokens * job.share * job.wide * job.steps for job in jobs),
            sum(2 * job.share * (job.wide + job.tokens) * job.steps for job in jobs),
        ),
    )
    return outs(table, *flat([job.arrays for job in jobs]))


def per_device_tuned(n_row, n_col, inputs, w_up, w_down, mask_up, mask_down, cotangent):
    share = w_up.shape[1] // n_row
    table = share_table(lax.axis_index("row"), lax.axis_index("col"))
    keep_up = jnp.repeat(mask_up.astype(BF16), TILE, axis=1)
    keep_up = keep_up.reshape(-1, n_row, share).transpose(1, 0, 2)
    keep_down = jnp.repeat(mask_down.astype(BF16), TILE, axis=1)
    keep_down = keep_down.reshape(n_row, share // TILE, -1)

    def between_cores(value):
        return lax.ppermute(value, "row", [(i, i ^ CORE) for i in range(n_row)])

    def along_first(value):
        return lax.ppermute(value, "row", [(i, i ^ first_of(i)) for i in range(n_row)])

    def along_second(value):
        second = [(X | Y) - first_of(i) for i in range(n_row)]
        return lax.ppermute(value, "row", [(i, i ^ second[i]) for i in range(n_row)])

    def along_col(value, shift):
        return lax.ppermute(value, "col", [(i, (i + shift) % n_col) for i in range(n_col)])

    def between_places(value):
        return lax.ppermute(value, "col", [(i, i ^ 1) for i in range(n_col)])

    def relayed(lower, upper):
        return between_places(chosen(table, upper, lower))

    def after(value, *done):
        return lax.optimization_barrier((value, *done))[0]

    def together(*values):
        return lax.optimization_barrier(values)

    def col_sum(blocks):
        return [blocks[0]] + [along_col(blocks[k], -k) for k in range(1, n_col)]

    features = range(0, w_up.shape[0], PIECE)
    keep_up, keep_down, table = together(keep_up, keep_down, table)
    shifts = [along_col(inputs, k) for k in range(1, n_col)]
    up = kept_pieces(w_up, keep_up, n_row, False, features)
    down = kept_pieces(w_down, after(keep_down, up[0]), n_row, True, features)
    shifts, up, down = together(shifts, up, down)
    inputs_all = [(inputs,)] + [(shift,) for shift in shifts]

    cot = after(cotangent, *shifts)
    lower, upper = along_col(cot, 1), along_col(cot, -1)
    up_sent, up_held = project(
        after(table, down[0]), (AT_SENT, AT_HELD), inputs_all, up, False
    )
    lower, upper, up_sent, up_held = together(lower, upper, up_sent, up_held)
    up_got = between_cores(up_sent)
    far = relayed(lower, upper)
    pair, rest = add_cores(up_held, up_got)

    near = along_first(pair)
    near, far = together(near, far)
    cot_all = [(cotangent,), (lower,), (far,), (upper,)]
    passed, own = add_first(rest, near)
    last = along_second(passed)
    back_sent, back_held = project(
        after(table, passed), (AT_SENT, AT_HELD), cot_all, down, True
    )
    last, back_sent, back_held = together(last, back_sent, back_held)
    hidden, act = activated(own, last)

    act_first = along_first(act)
    back_pair, rest = add_cores(after(back_held, act), between_cores(back_sent))
    near = along_first(back_pair)
    act_near = paired(act, after(act_first, back_pair))
    act_far = along_second(act_near)
    act_core = between_cores(act_near)

    def grad_down_job(at, pairs, into=None):
        return Gradient(at, pairs, cot_all, keep_down, w_down.shape, True, into)

    def grad_down_of(start, *job):
        return weight_gradients(after(table, start), [grad_down_job(*job)])[0]

    grad_down = grad_down_of(act_near, AT_NEAR, [act_near])
    near, grad_down = together(near, grad_down)
    passed, own = add_first(rest, near)
    last = along_second(passed)
    act_core = after(act_core, passed)
    out_total = gathered(table, AT_NEAR, [act_near, act_core], down, True)
    grad_down = grad_down_of(out_total, AT_NEAR_CORE, [act_core], grad_down)
    last, out_total, grad_down = together(last, out_total, grad_down)
    act_far = after(act_far, out_total)
    act_far_core = between_cores(act_far)
    grad = pulled(hidden, own, last)

    grad_first = along_first(grad)
    out_blocks = gathered(
        after(table, grad), AT_FAR, [act_far, act_far_core], down, True, out_total, n_col
    )
    grad_first, *out_blocks = together(grad_first, *out_blocks)
    hop = between_places(out_blocks[2])
    grad_near = paired(grad, grad_first)
    grad_far = along_second(grad_near)
    grad_core = between_cores(grad_near)
    in_total = gathered(table, AT_NEAR, [grad_near, grad_core], up, False)
    hop, in_total = together(hop, in_total)
    to_upper, to_lower = joined(table, out_blocks[3], out_blocks[1], hop)
    grad_far, in_total, to_upper, to_lower = together(
        grad_far, in_total, to_upper, to_lower
    )
    out_terms = [out_blocks[0], along_col(to_upper, 1), along_col(to_lower, -1)]
    grad_far_core = between_cores(grad_far)
    in_blocks = gathered(
        table, AT_FAR, [grad_far, grad_far_core], up, False, in_total, n_col
    )

    in_terms = col_sum(in_blocks)
    grad_down, grad_up = weight_gradients(
        after(table, in_blocks[0]),
        [
            grad_down_job(AT_FAR, [act_far, act_far_core], grad_down),
            Gradient(
                AT_NEAR,
                [grad_near, grad_core, grad_far, grad_far_core],
                inputs_all,
                keep_up,
                w_up.shape,
                False,
            ),
        ],
        TAIL_LIMIT,
    )
    out_terms[1:] = together(*out_terms[1:], grad_up)[:-1]
    outputs, grad_inputs = added(out_terms, in_terms)
    return (outputs, grad_inputs, grad_up, grad_down)


def solution(mesh):
    in_specs = (
        P("col", "row"),
        P("row", "col"),
        P("col", "row"),
        P("row", "col"),
        P("col", "row"),
        P("col", "row"),
    )
    out_specs = (P("col", "row"), P("col", "row"), P("row", "col"), P("col", "row"))
    n_row, n_col = mesh.shape["row"], mesh.shape["col"]

    def per_device(inputs, w_up, w_down, mask_up, mask_down, cotangent):
        fits = n_row == 8 and n_col == 4 and mask_up.shape[1] % n_row == 0 and w_up.shape[0] % PIECE == 0
        plan = functools.partial(per_device_tuned, n_row, n_col) if fits else per_device_plain
        return plan(inputs, w_up, w_down, mask_up, mask_down, cotangent)

    return jax.shard_map(
        per_device, mesh=mesh, in_specs=in_specs, out_specs=out_specs, check_vma=False
    )
```
